256 devices in a mesh: dp: 256 (over y, x, z, core).
Axes of the slice: x: 4, y: 4, z: 8, core: 2. Of those that a mesh axis runs over, the one named last changes fastest.
Arguments:
- activations: bfloat16 [262144, 512], P('dp'), may hold values from -24 to 24
- grad_key: bfloat16 [262144, 512], P('dp'), may hold values from -8 to 8
- grad_value: bfloat16 [262144, 512], P('dp'), may hold values from -6 to 6
- time_start: int32 [2048, 2], P('dp'), may hold values from 0 to 112
- time_width: int32 [2048, 2], P('dp'), may hold values from 0 to 16
- bases: bfloat16 [3, 512, 512], replicated, may hold values from -2 to 2
- old_factors: float32 [512, 3, 512], P('dp'), may hold values from -0.0004 to 0.6, as said below
Outputs:
- new_factors: float32 [512, 3, 512], P('dp')
- gradients: float32 [512, 2, 512], P('dp')
- updates: bfloat16 [2, 512, 512], P(None, 'dp')
The draws below stay inside these ranges and needn't reach their ends.
Inputs may be any that keep to these rules, and one draw needn't show every extreme that they name: `old_factors`: symmetric within each factor, with a positive diagonal that dominates each row.
All inputs are finite; a program needn't handle non-finite values.
Results may differ from the reference program's by a relative error of at most 0.014.
Values may be sent and summed in bfloat16 or wider, within the bound.
No kernel may reach another device: no remote copies, remote signals or barrier semaphores. Data moves between devices by JAX's collectives and lax.ppermute only.
A program may use at most 64 MiB of HBM per device.

```python
import jax
import jax.numpy as jnp
from jax import lax

D = 512
LEN = 128
MASKS = 2
MAXW = 16
NFACT = 3
NPROJ = 2
UTTS = 2048
TOKENS = 262144


def draw_bases(key, part):
    key = jax.random.fold_in(key, 11)
    entry_key, scale_key = jax.random.split(key)
    entries = jax.random.uniform(entry_key, (NFACT, D, D), jnp.float32, -1.0, 1.0)
    lower = 0.5
    logs = jax.random.uniform(scale_key, (NFACT, 1, D), jnp.float32, jnp.log(lower), jnp.log(2.0))
    return (entries * jnp.exp(logs)).astype(jnp.bfloat16)


def draw_old_factors(key, part):
    key = jax.random.fold_in(key, 23)
    diag_key, off_key = jax.random.split(key)
    diag_base = jnp.exp(jax.random.uniform(diag_key, (NFACT, D), jnp.float32, jnp.log(0.02), jnp.log(0.2)))
    rise = 1.0 + 2.0 * jnp.arange(D, dtype=jnp.float32) / (D - 1)
    diag = diag_base * rise[None, :]
    off = jax.random.uniform(off_key, (NFACT, D, D), jnp.float32, -1.0, 1.0)
    sym = (off + jnp.swapaxes(off, 1, 2)) * (0.4 * 0.02 / D)
    eye = jnp.eye(D, dtype=jnp.float32)
    whole = sym * (1.0 - eye)[None] + diag[:, :, None] * eye[None]
    return jnp.transpose(whole, (1, 0, 2))


def draw_grad_key(key, part):
    key = jax.random.fold_in(key, 37)
    common_key, sign_key, noise_key = jax.random.split(key, 3)
    common = jax.random.normal(common_key, (TOKENS, 1), jnp.float32)
    direction = jax.random.uniform(sign_key, (1, D), jnp.float32, -1.0, 1.0)
    noise = jax.random.normal(noise_key, (TOKENS, D), jnp.float32)
    return jnp.clip(common * direction + noise, -8.0, 8.0).astype(jnp.bfloat16)


def place_ends(array, stream_key, least, top_value):
    longest = array.shape.index(max(array.shape))
    spots = []
    for shift in (0, 1):
        where = [jax.random.randint(jax.random.fold_in(stream_key, axis), (), 0, length) for axis, length in enumerate(array.shape)]
        where[longest] = (where[longest] + shift) % array.shape[longest]
        spots.append(tuple(where))
    return array.at[spots[0]].set(least).at[spots[1]].set(top_value)


def with_spikes(drawn, stream_key, source, target, parts, factor):
    owner, partner = [(jnp.arange(drawn.shape[dim]) // (drawn.shape[dim] // parts)).reshape([-1 if axis == dim else 1 for axis in range(drawn.ndim)]) for dim in (source, target)]
    chosen = jax.random.permutation(stream_key, parts)[partner]
    strong = (owner == chosen) | (owner == (partner + parts // 2) % parts)
    return jnp.where(strong, factor * drawn, drawn)


def levels(stream_key, extent, pieces, low, high):
    def one(dim, shards_of):
        steps = jax.random.uniform(jax.random.fold_in(jax.random.fold_in(stream_key, 6), dim), (shards_of,), jnp.float32, low / len(pieces), high / len(pieces))
        return jnp.repeat(jnp.exp(steps), extent[dim] // shards_of).reshape((-1,) + (1,) * (len(extent) - dim - 1))

    level = one(*pieces[0])
    for cut in pieces[1:]:
        level = level * one(*cut)
    return level


def normal_values(rng, shape, spread, reach, shards=(), kind=jnp.bfloat16):
    drawn = jax.random.normal(rng, shape, jnp.float32) * spread
    if len(shards) > 0:
        drawn = levels(rng, shape, shards, -0.22, 0.18) * drawn
    return jnp.clip(drawn, min=-reach, max=reach).astype(kind)


def noise_with(own_key, shape, spread, most, pieces, heavy, kind=jnp.bfloat16):
    array = spread * jax.random.normal(own_key, shape, jnp.float32)
    if pieces:
        array = array * levels(own_key, shape, pieces, -0.22, 0.18)
    return jnp.clip(with_spikes(array, jax.random.fold_in(own_key, 3), *heavy), -most, most).astype(kind)


def setup_inputs(seed: int = 0) -> dict:
    key_list = jax.random.split(jax.random.key(seed), 8)
    return {
        "activations": noise_with(key_list[0], (TOKENS, D), 1.0, 24.0, ((0, 256),), (0, 1, 256, 6.0)),
        "grad_key": draw_grad_key(jax.random.fold_in(key_list[7], 71), 0),
        "grad_value": normal_values(key_list[2], (TOKENS, D), 1.0, 6.0, ((0, 256),)),
        "time_start": place_ends(jax.random.randint(key_list[3], (UTTS, MASKS), 0, LEN - MAXW + 1), jax.random.fold_in(key_list[3], 1), 0, LEN - MAXW).astype(jnp.int32),
        "time_width": place_ends(jax.random.randint(key_list[4], (UTTS, MASKS), 0, MAXW + 1), jax.random.fold_in(key_list[4], 1), 0, MAXW).astype(jnp.int32),
        "bases": draw_bases(jax.random.fold_in(key_list[7], 71), 0),
        "old_factors": draw_old_factors(jax.random.fold_in(key_list[7], 71), 0),
    }


decay = 0.8
damping = 0.001
kl_clip = 0.001
learn_rate = 7e-05

def frame_keep(time_start, time_width):
    position = jnp.arange(LEN, dtype=jnp.int32)
    inside = (position[None, None, :] >= time_start[:, :, None]) & (position[None, None, :] < (time_start + time_width)[:, :, None])
    masked = jnp.any(inside, axis=1).reshape(-1)
    return jnp.where(masked, 0.0, 1.0).astype(jnp.bfloat16)

def precondition(grad_low, basis_in, basis_out, lam_in, lam_out):
    rot_out = jnp.dot(grad_low, basis_out, preferred_element_type=jnp.float32).astype(jnp.bfloat16)
    rotated = jnp.dot(basis_in.T, rot_out, preferred_element_type=jnp.float32)
    scaled = (rotated / (lam_in[:, None] * lam_out[None, :] + damping)).astype(jnp.bfloat16)
    back_out = jnp.dot(scaled, basis_out.T, preferred_element_type=jnp.float32).astype(jnp.bfloat16)
    return jnp.dot(basis_in, back_out, preferred_element_type=jnp.float32).astype(jnp.bfloat16)

def reference(activations, grad_key, grad_value, time_start, time_width, bases, old_factors):
    keep = frame_keep(time_start, time_width)[:, None]
    inputs = [activations * keep, grad_key * keep, grad_value * keep]
    batch = jnp.stack([jnp.dot(x.T, x, preferred_element_type=jnp.float32) for x in inputs], axis=1) / TOKENS
    new_factors = decay * old_factors + (1.0 - decay) * batch
    gradients = jnp.stack([jnp.dot(inputs[0].T, inputs[1 + p], preferred_element_type=jnp.float32) for p in range(NPROJ)], axis=1)
    lam = []
    for f in range(NFACT):
        basis = bases[f].astype(jnp.float32)
        image = jnp.dot(new_factors[:, f, :], basis, precision=lax.Precision.HIGHEST)
        lam.append(lax.optimization_barrier(jnp.sum(basis * image, axis=0)))
    precs = []
    curvature = jnp.float32(0.0)
    for p in range(NPROJ):
        grad_low = gradients[:, p, :].astype(jnp.bfloat16)
        prec = precondition(grad_low, bases[0], bases[1 + p], lam[0], lam[1 + p])
        curvature = curvature + jnp.sum(prec.astype(jnp.float32) * grad_low.astype(jnp.float32))
        precs.append(prec)
    factor = jnp.sqrt(kl_clip / (learn_rate * learn_rate * curvature))
    updates = jnp.stack([(factor * q.astype(jnp.float32)).astype(jnp.bfloat16) for q in precs], axis=0)
    return (new_factors, gradients, updates)
```

```python
import jax
import jax.numpy as jnp
from jax import lax
from jax.sharding import PartitionSpec as P

LEN = 128
NX, NY, NZ, NC = 4, 4, 8, 2
NXY = NX * NY
D = 512
ROWS_XY = D // NXY
ROWS_Z = ROWS_XY // NZ

decay = 0.8
damping = 0.001
kl_clip = 0.001
learn_rate = 7e-05

SWAP = [(d, d ^ 1) for d in range(NXY * NZ * NC)]
XY_GROUPS = [[(i * NZ + z) * NC + c for i in range(NXY)] for z in range(NZ) for c in range(NC)]
Z_GROUPS = [[(i * NZ + z) * NC + c for z in range(NZ)] for i in range(NXY) for c in range(NC)]


def frame_keep(time_start, time_width):
    position = jnp.arange(LEN, dtype=jnp.int32)
    inside = (position[None, None, :] >= time_start[:, :, None]) & (
        position[None, None, :] < (time_start + time_width)[:, :, None]
    )
    masked = jnp.any(inside, axis=1).reshape(-1)
    return jnp.where(masked, 0.0, 1.0).astype(jnp.bfloat16)


def split(value):
    high = value.astype(jnp.bfloat16)
    low = (value - high.astype(jnp.float32)).astype(jnp.bfloat16)
    return jnp.concatenate([high, low], axis=0)


def body(activations, grad_key, grad_value, time_start, time_width, bases, old_factors):
    f32, bf16 = jnp.float32, jnp.bfloat16
    index = lax.axis_index("dp")
    core = index % NC
    first = core == 0
    tokens = activations.shape[0] * lax.axis_size("dp")
    keep = frame_keep(time_start, time_width)[:, None]
    x = (activations * keep, grad_key * keep, grad_value * keep)

    def gram(a, b):
        return jnp.dot(a.T, b, preferred_element_type=f32).astype(bf16)

    g = [gram(x[0], x[1]), gram(x[0], x[2])]
    f = [gram(v, v) for v in x]
    whole0 = jnp.concatenate([g[0], f[0], f[2][:, : D // 2]], axis=1)
    whole1 = jnp.concatenate([g[1], f[1], f[2][:, D // 2 :]], axis=1)
    mine = jnp.where(first, whole0, whole1)
    other = jnp.where(first, whole1, whole0)
    received = lax.ppermute(other, "dp", SWAP)

    share = (1.0 - decay) / tokens
    my_rows = lax.dynamic_slice_in_dim(bases, 2 * index, 2, 1).astype(f32)
    lam = []
    for k in range(3):
        image = jnp.dot(f[k], bases[k], preferred_element_type=f32)
        part = jnp.sum(bases[k].astype(f32) * image, axis=0) * share
        old_image = jnp.dot(old_factors[:, k, :], bases[k].astype(f32), precision=lax.Precision.HIGHEST)
        lam.append(part + decay * jnp.sum(my_rows[k] * old_image, axis=0))
    lam = jnp.stack(lam)
    lam = lam + lax.ppermute(lam, "dp", SWAP)
    lam = jnp.stack([lam[0], jnp.where(first, lam[1], lam[2])])

    chip = (mine.astype(f32) + received.astype(f32)).astype(bf16)
    parts = lax.all_to_all(chip.reshape(NXY, ROWS_XY, 1280), "dp", 0, 0, axis_index_groups=XY_GROUPS, tiled=True)
    plane = jnp.sum(parts.astype(f32), axis=0).astype(bf16)

    send = jnp.concatenate(
        [
            jnp.broadcast_to(plane[None, :, :D], (NZ, ROWS_XY, D)),
            plane[:, D:].reshape(NZ, 6, D),
            jnp.broadcast_to(split(lam)[None], (NZ, 4, D)),
        ],
        axis=1,
    )
    got = lax.all_to_all(send, "dp", 0, 0, axis_index_groups=Z_GROUPS, tiled=True)
    got = jnp.sum(got.astype(f32), axis=0)
    grad = got[:ROWS_XY]
    factors = got[ROWS_XY : ROWS_XY + 6].reshape(ROWS_Z, 768) * (1.0 / tokens)
    lam = got[38:40] + got[40:42]

    basis_in = bases[0]
    basis_out = lax.dynamic_index_in_dim(bases, 1 + core, 0, keepdims=False)
    rot_out = jnp.dot(grad.astype(bf16), basis_out, preferred_element_type=f32).astype(bf16)
    send = jnp.concatenate([rot_out, split(lam)], axis=0)
    send = jnp.broadcast_to(send[None], (NXY,) + send.shape)
    got = lax.all_to_all(send, "dp", 0, 0, axis_index_groups=XY_GROUPS, tiled=True)
    rot_all = got[:, :ROWS_XY].reshape(D, D)
    lam = jnp.sum(got[:, ROWS_XY:].astype(f32), axis=0)
    lam = lam[:2] + lam[2:]
    rotated = lax.dot_general(basis_in, rot_all, (((0,), (0,)), ((), ())), preferred_element_type=f32)
    scaled = (rotated / (lam[0][:, None] * lam[1][None, :] + damping)).astype(bf16)
    curve = jnp.sum(scaled.astype(f32) * rotated)
    chip_index = index // NC
    rows_in = lax.dynamic_slice_in_dim(basis_in, chip_index * ROWS_Z, ROWS_Z, 0)
    back = jnp.dot(rows_in, scaled, preferred_element_type=f32).astype(bf16)
    prec = lax.dot_general(back, basis_out, (((1,), (1,)), ((), ())), preferred_element_type=f32)
    prec = prec.astype(bf16).astype(f32)

    def mine_theirs(rows):
        low, high = rows[:2], rows[2:4]
        return jnp.where(first, low, high), jnp.where(first, high, low)

    prec_mine, prec_theirs = mine_theirs(prec)
    extra = lax.ppermute(jnp.concatenate([prec_theirs, jnp.broadcast_to(curve, (1, D))], axis=0), "dp", SWAP)
    factor = jnp.sqrt(kl_clip / (learn_rate * learn_rate * (curve + extra[2, 0])))
    prec_other = extra[:2]
    updates = jnp.stack(
        [jnp.where(first, prec_mine, prec_other), jnp.where(first, prec_other, prec_mine)]
    )
    updates = (factor * updates).astype(bf16)

    z = (index // NC) % NZ
    grad_rows = lax.dynamic_slice_in_dim(grad, z * ROWS_Z, ROWS_Z, 0)
    rows_mine, rows_theirs = mine_theirs(jnp.concatenate([grad_rows, factors], axis=1))
    rows_other = lax.ppermute(rows_theirs, "dp", SWAP)
    rows0 = jnp.where(first, rows_mine, rows_other)
    rows1 = jnp.where(first, rows_other, rows_mine)
    gradients = jnp.stack([rows0[:, :D], rows1[:, :D]], axis=1)
    last = jnp.concatenate([rows0[:, 1024:], rows1[:, 1024:]], axis=1)
    batch = jnp.stack([rows0[:, D:1024], rows1[:, D:1024], last], axis=1)
    new_factors = decay * old_factors + (1.0 - decay) * batch
    return (new_factors, gradients, updates)


def solution(mesh):
    in_specs = (
        P("dp", None),
        P("dp", None),
        P("dp", None),
        P("dp", None),
        P("dp", None),
        P(),
        P("dp", None, None),
    )
    out_specs = (P("dp", None, None), P("dp", None, None), P(None, "dp", None))
    return jax.shard_map(body, mesh=mesh, in_specs=in_specs, out_specs=out_specs, check_vma=False)
```

```python
import functools

import jax
import jax.numpy as jnp
from jax import lax
from jax.experimental import pallas as pl
from jax.experimental.pallas import tpu as pltpu
from jax.sharding import PartitionSpec as P

LEN = 128
NX, NY, NZ, NC = 4, 4, 8, 2
NXY = NX * NY
D = 512
HALF = D // 2
PAIR = 2
WIDE = NXY * PAIR
DEEP = NZ // PAIR
ROWS = D // WIDE
COLS = D + D + HALF
LANES = 128
FR = ROWS // DEEP
GT, FT = D // LANES, (D + HALF) // LANES
MB = 1 << 20

decay = 0.8
damping = 0.001
kl_clip = 0.001
learn_rate = 7e-05

f32, bf16 = jnp.float32, jnp.bfloat16


def device(xy, z, c):
    return (xy * NZ + z) * NC + c


SWAP = [(d, d ^ 1) for d in range(NXY * NZ * NC)]
WIDE_GROUPS = [
    [device(i, k * PAIR + l, c) for i in range(NXY) for l in range(PAIR)]
    for k in range(DEEP)
    for c in range(NC)
]
DEEP_GROUPS = [
    [device(i, k * PAIR + l, c) for k in range(DEEP)] for i in range(NXY) for l in range(PAIR) for c in range(NC)
]
HOME = [
    (device(i, k * PAIR + l, c), device(i, l * DEEP + k, c))
    for i in range(NXY)
    for k in range(DEEP)
    for l in range(PAIR)
    for c in range(NC)
]
HOME_CROSS = [(a, b ^ 1) for a, b in HOME]

VMEM = pl.BlockSpec(memory_space=pltpu.VMEM)
SMEM = pl.BlockSpec(memory_space=pltpu.SMEM)
ANY = pl.BlockSpec(memory_space=pl.ANY)


def call(kernel, outs, in_specs, scratch=(), limit=16, flops=0, moved=0):
    return pl.pallas_call(
        kernel,
        out_shape=outs,
        in_specs=in_specs,
        out_specs=jax.tree.map(lambda _: VMEM, outs),
        scratch_shapes=list(scratch),
        compiler_params=pltpu.CompilerParams(vmem_limit_bytes=limit * MB),
        cost_estimate=pl.CostEstimate(flops=flops, bytes_accessed=moved, transcendentals=0),
    )


def shape(dims, dtype):
    return jax.ShapeDtypeStruct(dims, dtype)


def dot(a, b):
    return jnp.dot(a, b, preferred_element_type=f32)


def apply_mask(buf, slot, start, width):
    position = lax.broadcasted_iota(jnp.int32, (LEN, LANES), 0)
    for u in range(start.shape[0]):
        keep = None
        for m in range(start.shape[1]):
            s = start[u, m]
            outside = (position < s) | (position >= s + width[u, m])
            keep = outside if keep is None else keep & outside
        keep = jnp.where(keep, 1.0, 0.0).astype(bf16)
        for j in range(GT):
            view = (slot, pl.ds(u * LEN, LEN), pl.ds(j * LANES, LANES))
            buf[view] = buf[view] * keep


def grams(pick, start, width, x0, xk, xv, out, buf, sem):
    first = pltpu.make_async_copy(x0, buf.at[0], sem.at[0])
    first.start()

    @pl.when(pick == 0)
    def _():
        pltpu.make_async_copy(xk, buf.at[1], sem.at[1]).start()

    @pl.when(pick != 0)
    def _():
        pltpu.make_async_copy(xv, buf.at[1], sem.at[1]).start()

    first.wait()
    apply_mask(buf, 0, start, width)
    pltpu.make_async_copy(xk, buf.at[1], sem.at[1]).wait()
    apply_mask(buf, 1, start, width)
    block = 256
    half = pl.ds(pl.multiple_of(pick * HALF, HALF), HALF)
    for r in range(D // block):
        places = pl.ds(r * (block // ROWS), block // ROWS)

        def put(value, begin):
            size = value.shape[1]
            out[places, :, pl.ds(begin, size)] = value.astype(bf16).reshape(block // ROWS, ROWS, size)

        left = buf[0, :, pl.ds(r * block, block)].T
        put(dot(left, buf[1]), 0)
        put(dot(left, buf[0, :, half]), 2 * D)
        left = buf[1, :, pl.ds(r * block, block)].T
        put(dot(left, buf[1]), D)


def theirs_kernel(core, start, width, x0, xk, xv, out, buf, sem):
    grams(1 - core[0], start, width, x0, xk, xv, out, buf, sem)


def mine_kernel(share, core, start, width, x0, xk, xv, other, bases, out, keep_lam, send_lam, buf, sem):
    c = core[0]
    grams(c, start, width, x0, xk, xv, out, buf, sem)

    def image(source, begin, size, basis):
        return dot(source[:, :, pl.ds(begin, size)].reshape(D, size), basis)

    def values(index, product):
        return jnp.sum(bases[index].astype(f32) * product, axis=0, keepdims=True) * share

    near = pl.ds(pl.multiple_of(c * HALF, HALF), HALF)
    far = pl.ds(pl.multiple_of((1 - c) * HALF, HALF), HALF)
    lam0 = values(0, image(out, 2 * D, HALF, bases[0, near, :]) + image(other, 2 * D, HALF, bases[0, far, :]))
    keep_lam[0:1, :] = lam0
    send_lam[0:1, :] = lam0
    keep_lam[1:2, :] = values(1 + c, image(out, D, D, bases[1 + c]))
    send_lam[1:2, :] = values(2 - c, image(other, D, D, bases[2 - c]))


def split(value):
    high = value.astype(bf16)
    return high.astype(f32), value - high.astype(f32)


def lam_rows(lam):
    high, low = split(lam)
    pieces = []
    for j in range(GT):
        tile = slice(j * LANES, (j + 1) * LANES)
        pieces += [high[:, tile], low[:, tile]]
    return jnp.concatenate(pieces, axis=0)


def read_lam(rows):
    tiles = [rows[4 * j : 4 * j + 2] + rows[4 * j + 2 : 4 * j + 4] for j in range(GT)]
    return jnp.concatenate(tiles, axis=1)


LAMR = 4 * GT
TAIL = ((FT * FR + LAMR + 15) // 16) * 16
DEEP_ROWS = GT * ROWS + TAIL
GATHER_ROWS = GT * ROWS + LAMR


def pack_kernel(parts, keep_lam, send_lam, out):
    total = parts[0].astype(f32)
    for i in range(1, WIDE):
        total = total + parts[i].astype(f32)
    lam = lam_rows(keep_lam[...] + send_lam[...])
    for j in range(GT):
        tile = total[:, j * LANES : (j + 1) * LANES].astype(bf16)
        for k in range(DEEP):
            out[k, pl.ds(j * ROWS, ROWS), :] = tile
    pad = jnp.zeros((TAIL - FT * FR - LAMR, LANES), f32)
    for k in range(DEEP):
        rows = total[k * FR : (k + 1) * FR]
        pieces = [rows[:, D + t * LANES : D + (t + 1) * LANES] for t in range(FT)]
        out[k, pl.ds(GT * ROWS, TAIL), :] = jnp.concatenate(pieces + [lam, pad], axis=0).astype(bf16)


def rotate_kernel(place, got, basis, out, stay, cross):
    total = got[0].astype(f32)
    for i in range(1, DEEP):
        total = total + got[i].astype(f32)
    grad = jnp.concatenate([total[j * ROWS : (j + 1) * ROWS] for j in range(GT)], axis=1)
    rot = dot(grad.astype(bf16), basis[...]).astype(bf16)
    base = GT * ROWS
    lam = lam_rows(read_lam(total[base + FT * FR : base + FT * FR + LAMR])).astype(bf16)
    for j in range(GT):
        tile = rot[:, j * LANES : (j + 1) * LANES]
        for i in range(WIDE):
            out[i, pl.ds(j * ROWS, ROWS), :] = tile
    for i in range(WIDE):
        out[i, pl.ds(base, LAMR), :] = lam
    k, c = place[0], place[1]
    rows = grad[0:FR]
    for other in range(1, DEEP):
        rows = jnp.where(k == other, grad[other * FR : (other + 1) * FR], rows)
    factors = [total[base + t * FR : base + (t + 1) * FR] for t in range(FT)]
    rows = jnp.concatenate([rows] + factors, axis=1)
    low, high = rows[0:2], rows[2:4]
    stay[...] = jnp.where(c == 0, low, high)
    cross[...] = jnp.where(c == 0, high, low)


def solve_kernel(got, basis_in_t, basis_out, rows_in, stay, cross, scaled):
    base = GT * ROWS
    lam = got[0, pl.ds(base, LAMR), :].astype(f32)
    for i in range(1, WIDE):
        lam = lam + got[i, pl.ds(base, LAMR), :].astype(f32)
    lam = read_lam(lam)
    column = jnp.broadcast_to(lam[0:1], (8, D)).T[:, 0:1]
    column = jnp.broadcast_to(column, (D, LANES))
    curve = jnp.zeros((8, LANES), f32)
    for j in range(GT):
        rot = got[:, pl.ds(j * ROWS, ROWS), :].reshape(D, LANES)
        rotated = dot(basis_in_t[...], rot)
        low = (rotated / (column * lam[1:2, j * LANES : (j + 1) * LANES] + damping)).astype(bf16)
        scaled[:, pl.ds(j * LANES, LANES)] = low
        curve = curve + jnp.sum((low.astype(f32) * rotated).reshape(D // 8, 8, LANES), axis=0)
    curve = jnp.sum(jnp.sum(curve, axis=1, keepdims=True), axis=0, keepdims=True)
    back = dot(rows_in[...], scaled[...]).astype(bf16)
    prec = lax.dot_general(back, basis_out[...], (((1,), (1,)), ((), ())), preferred_element_type=f32)
    prec = prec.astype(bf16).astype(f32)
    curve = jnp.broadcast_to(curve, (6, D))
    stay[...] = jnp.concatenate([prec[0:2], curve], axis=0)
    cross[...] = jnp.concatenate([prec[2:4], curve], axis=0)


def finish_kernel(scale, place, mine, theirs, same, cross, old, new_factors, gradients, updates):
    first = place[1] == 0
    curve = mine[2:3, :] + theirs[2:3, :]
    factor = jnp.sqrt(kl_clip / (learn_rate * learn_rate * curve))
    own = mine[0:2, :] * factor
    their = theirs[0:2, :] * factor
    updates[0] = jnp.where(first, own, their).astype(bf16)
    updates[1] = jnp.where(first, their, own).astype(bf16)
    rows0 = jnp.where(first, same[...], cross[...])
    rows1 = jnp.where(first, cross[...], same[...])
    gradients[:, 0, :] = rows0[:, :D]
    gradients[:, 1, :] = rows1[:, :D]
    batch = (
        jnp.concatenate([rows0[:, 2 * D :], rows1[:, 2 * D :]], axis=1),
        rows0[:, D : 2 * D],
        rows1[:, D : 2 * D],
    )
    for f in range(3):
        new_factors[:, f, :] = decay * old[:, f, :] + scale * batch[f]


def exchange(value, groups):
    return lax.all_to_all(value, "dp", 0, 0, axis_index_groups=groups, tiled=True)


def body(activations, grad_key, grad_value, time_start, time_width, bases, old_factors):
    index = lax.axis_index("dp").astype(jnp.int32)
    core = index % NC
    first = core == 0
    z = (index // NC) % NZ
    place = jnp.stack([z // PAIR, core])
    tokens_here = activations.shape[0]
    share = (1.0 - decay) / (tokens_here * lax.axis_size("dp"))

    inputs = (core[None], time_start, time_width, activations, grad_key, grad_value)
    specs = [SMEM, SMEM, SMEM, ANY, ANY, ANY]
    scratch = [pltpu.VMEM((2, tokens_here, D), bf16), pltpu.SemaphoreType.DMA((2,))]
    partial = shape((WIDE, ROWS, COLS), bf16)
    work = 2 * D * tokens_here * COLS
    with jax.named_scope("grams_theirs"):
        other = call(theirs_kernel, partial, specs, scratch, flops=work, moved=4 * MB)(*inputs)
    received = lax.ppermute(other, "dp", SWAP)
    lam_shape = shape((2, D), f32)
    with jax.named_scope("grams_mine"):
        mine, keep_lam, send_lam = call(
            functools.partial(mine_kernel, share),
            (partial, lam_shape, lam_shape),
            specs + [VMEM, VMEM],
            scratch,
            limit=24,
            flops=work,
            moved=6 * MB,
        )(*inputs, other, bases)
    old_lam = []
    my_rows = lax.dynamic_slice_in_dim(bases, 2 * index, 2, 1).astype(f32)
    for f in range(3):
        old_image = jnp.dot(old_factors[:, f, :], bases[f].astype(f32), precision=lax.Precision.HIGHEST)
        old_lam.append(decay * jnp.sum(my_rows[f] * old_image, axis=0))
    keep_lam = keep_lam + jnp.stack([old_lam[0], jnp.where(first, old_lam[1], old_lam[2])])
    send_lam = send_lam + jnp.stack([old_lam[0], jnp.where(first, old_lam[2], old_lam[1])])
    sent_lam = lax.ppermute(send_lam, "dp", SWAP)

    with jax.named_scope("chip_sum"):
        chip = (mine.astype(f32) + received.astype(f32)).astype(bf16)
    with jax.named_scope("wide_sum"):
        parts = exchange(chip, WIDE_GROUPS)
    with jax.named_scope("pack"):
        packed = call(pack_kernel, shape((DEEP, DEEP_ROWS, LANES), bf16), [VMEM] * 3)(parts, keep_lam, sent_lam)
    with jax.named_scope("deep_sum"):
        got = exchange(packed, DEEP_GROUPS)
    basis_out = lax.dynamic_index_in_dim(bases, 1 + core, 0, keepdims=False)
    row_shape = shape((2, COLS), f32)
    with jax.named_scope("rotate"):
        spread, stay, cross = call(
            rotate_kernel,
            (shape((WIDE, GATHER_ROWS, LANES), bf16), row_shape, row_shape),
            [SMEM, VMEM, VMEM],
        )(place, got, basis_out)
    with jax.named_scope("gather"):
        gathered = exchange(spread, WIDE_GROUPS)
    same = lax.ppermute(stay, "dp", HOME)
    cross = lax.ppermute(cross, "dp", HOME_CROSS)
    rows_in = lax.dynamic_slice_in_dim(bases[0], (index // NC) * FR, FR, 0)
    rows_in = jnp.where(first, rows_in, jnp.roll(rows_in, 2, axis=0))
    rows_in = jnp.pad(rows_in, ((0, 16 - FR), (0, 0)))
    result = shape((8, D), f32)
    with jax.named_scope("solve"):
        own, their = call(solve_kernel, (result, result), [VMEM] * 4, [pltpu.VMEM((D, D), bf16)])(
            gathered, bases[0].T, basis_out, rows_in
        )
    got_own = lax.ppermute(their, "dp", SWAP)
    with jax.named_scope("finish"):
        return call(
            functools.partial(finish_kernel, share),
            (shape((2, 3, D), f32), shape((2, 2, D), f32), shape((2, 2, D), bf16)),
            [SMEM] + [VMEM] * 5,
        )(place, own, got_own, same, cross, old_factors)


def solution(mesh):
    in_specs = (
        P("dp", None),
        P("dp", None),
        P("dp", None),
        P("dp", None),
        P("dp", None),
        P(),
        P("dp", None, None),
    )
    out_specs = (P("dp", None, None), P("dp", None, None), P(None, "dp", None))
    return jax.shard_map(body, mesh=mesh, in_specs=in_specs, out_specs=out_specs, check_vma=False)
```

```python
import functools

import jax
import jax.numpy as jnp
from jax import lax
from jax.experimental import pallas as pl
from jax.experimental.pallas import tpu as pltpu
from jax.sharding import PartitionSpec as P

LEN = 128
NX, NY, NZ, NC = 4, 4, 8, 2
NXY = NX * NY
D = 512
HALF = D // 2
PAIR = 2
WIDE = NXY * PAIR
DEEP = NZ // PAIR
ROWS = D // WIDE
COLS = D + D + HALF
LANES = 128
FR = ROWS // DEEP
GT, FT = D // LANES, (D + HALF) // LANES
MB = 1 << 20

decay = 0.8
damping = 0.001
kl_clip = 0.001
learn_rate = 7e-05

f32, bf16 = jnp.float32, jnp.bfloat16


def device(xy, z, c):
    return (xy * NZ + z) * NC + c


SWAP = [(d, d ^ 1) for d in range(NXY * NZ * NC)]
WIDE_GROUPS = [
    [device(i, k * PAIR + l, c) for i in range(NXY) for l in range(PAIR)]
    for k in range(DEEP)
    for c in range(NC)
]
DEEP_GROUPS = [
    [device(i, k * PAIR + l, c) for k in range(DEEP)] for i in range(NXY) for l in range(PAIR) for c in range(NC)
]
VMEM = pl.BlockSpec(memory_space=pltpu.VMEM)
SMEM = pl.BlockSpec(memory_space=pltpu.SMEM)
HBM = pl.BlockSpec(memory_space=pltpu.HBM)
CHUNKS = 4


def call(kernel, outs, in_specs, scratch=(), limit=16, flops=0, moved=0):
    return pl.pallas_call(
        kernel,
        out_shape=outs,
        in_specs=in_specs,
        out_specs=jax.tree.map(lambda _: VMEM, outs),
        scratch_shapes=list(scratch),
        compiler_params=pltpu.CompilerParams(vmem_limit_bytes=limit * MB),
        cost_estimate=pl.CostEstimate(flops=flops, bytes_accessed=moved, transcendentals=0),
    )


def shape(dims, dtype):
    return jax.ShapeDtypeStruct(dims, dtype)


def dot(a, b):
    return jnp.dot(a, b, preferred_element_type=f32)


def arrange(value):
    size = value.shape[1]
    pairs = value.reshape(value.shape[0] // 16, 2, 8, size)
    even, odd = pairs[:, 0], pairs[:, 1]
    upper = lax.broadcasted_iota(jnp.int32, even.shape, 1) < FR
    low = jnp.where(upper, even, pltpu.roll(odd, FR, 1))
    high = jnp.where(upper, pltpu.roll(even, FR, 1), odd)
    blocks = (value.shape[0] // (PAIR * ROWS), ROWS, size)
    return low.reshape(blocks), high.reshape(blocks)


def apply_mask(source, target, start, width, first, count):
    position = lax.broadcasted_iota(jnp.int32, (LEN, LANES), 0)
    for u in range(first, first + count):
        keep = None
        for m in range(start.shape[0]):
            s = start[m : m + 1, u : u + 1]
            outside = (position < s) | (position >= s + width[m : m + 1, u : u + 1])
            keep = outside if keep is None else keep & outside
        keep = jnp.where(keep, 1.0, 0.0).astype(bf16)
        for j in range(GT):
            view = (pl.ds(u * LEN, LEN), pl.ds(j * LANES, LANES))
            target[view] = source[view] * keep


def fetch(source, target, sems):
    rows = source.shape[0] // CHUNKS
    return [
        pltpu.make_async_copy(source.at[pl.ds(q * rows, rows)], target.at[pl.ds(q * rows, rows)], sems.at[q])
        for q in range(CHUNKS)
    ]


def fetch_picked(pick, xk, xv, target, sems):
    @pl.when(pick == 0)
    def _():
        for copy in fetch(xk, target, sems):
            copy.start()

    @pl.when(pick != 0)
    def _():
        for copy in fetch(xv, target, sems):
            copy.start()

    return fetch(xk, target, sems)


BLOCK = 256


def put(out, r, value, begin):
    places, cols = pl.ds(r * (BLOCK // (PAIR * ROWS)), BLOCK // (PAIR * ROWS)), pl.ds(begin, value.shape[1])
    low, high = arrange(value)
    out[places, 0, :, cols] = low.astype(bf16)
    out[places, 1, :, cols] = high.astype(bf16)


def grams(pick, x0, x1, ready, out):
    half = pl.ds(pl.multiple_of(pick * HALF, HALF), HALF)
    lefts = []
    for r in range(D // BLOCK):
        lefts.append(x0[:, pl.ds(r * BLOCK, BLOCK)].T)
        put(out, r, dot(lefts[r], x0[:, half]), 2 * D)
    ready()
    for r in range(D // BLOCK):
        put(out, r, dot(lefts[r], x1[...]), 0)
    for r in range(D // BLOCK):
        left = x1[:, pl.ds(r * BLOCK, BLOCK)].T
        put(out, r, dot(left, x1[...]), D)


def theirs_kernel(core, start, width, x0, xk, xv, out, kept, buf0, buf1, masks, sem0, sem1, sem2):
    pick = 1 - core[0]
    copies0 = fetch(x0, buf0, sem0)
    small = [pltpu.make_async_copy(v, masks.at[i], sem2.at[i]) for i, v in enumerate((start, width))]
    for copy in small + copies0:
        copy.start()
    copies1 = fetch_picked(pick, xk, xv, buf1, sem1)
    for copy in small:
        copy.wait()
    count = buf0.shape[0] // LEN // CHUNKS
    for q in range(CHUNKS):
        copies0[q].wait()
        apply_mask(buf0, kept, masks.at[0], masks.at[1], q * count, count)

    def ready():
        for q in range(CHUNKS):
            copies1[q].wait()
            apply_mask(buf1, buf1, masks.at[0], masks.at[1], q * count, count)

    grams(pick, kept, buf1, ready, out)


def mine_kernel(core, start, width, x0, xk, xv, out, buf1, masks, sem1, sem2):
    pick = core[0]
    small = [pltpu.make_async_copy(v, masks.at[i], sem2.at[i]) for i, v in enumerate((start, width))]
    for copy in small:
        copy.start()
    copies1 = fetch_picked(pick, xk, xv, buf1, sem1)
    count = buf1.shape[0] // LEN // CHUNKS

    def ready():
        for copy in small:
            copy.wait()
        for q in range(CHUNKS):
            copies1[q].wait()
            apply_mask(buf1, buf1, masks.at[0], masks.at[1], q * count, count)

    grams(pick, x0, buf1, ready, out)


def lam_kernel(share, core, mine, other, bases, keep_lam, send_lam, basis_in_t):
    c = core[0]

    def image(source, begin, size, basis):
        return dot(source[:, :, pl.ds(begin, size)].reshape(D, size), basis)

    def arranged(index):
        low, high = arrange(bases[index].astype(f32))
        return jnp.concatenate([low, high], axis=1).reshape(D, D)

    def values(basis, product):
        return jnp.sum(basis * product, axis=0, keepdims=True) * share

    near = pl.ds(pl.multiple_of(c * HALF, HALF), HALF)
    far = pl.ds(pl.multiple_of((1 - c) * HALF, HALF), HALF)
    basis = arranged(0)
    basis_in_t[...] = basis.T.astype(bf16)
    lam0 = values(basis, image(mine, 2 * D, HALF, bases[0, near, :]) + image(other, 2 * D, HALF, bases[0, far, :]))
    keep_lam[0:1, :] = lam0
    send_lam[0:1, :] = lam0
    keep_lam[1:2, :] = values(arranged(1 + c), image(mine, D, D, bases[1 + c]))
    send_lam[1:2, :] = values(arranged(2 - c), image(other, D, D, bases[2 - c]))


def split(value):
    high = value.astype(bf16)
    return high.astype(f32), value - high.astype(f32)


def lam_rows(lam):
    high, low = split(lam)
    pieces = []
    for j in range(GT):
        tile = slice(j * LANES, (j + 1) * LANES)
        pieces += [high[:, tile], low[:, tile]]
    return jnp.concatenate(pieces, axis=0)


def read_lam(rows):
    tiles = [rows[4 * j : 4 * j + 2] + rows[4 * j + 2 : 4 * j + 4] for j in range(GT)]
    return jnp.concatenate(tiles, axis=1)


LAMR = 4 * GT
TAIL = ((FT * FR + LAMR + 15) // 16) * 16
DEEP_ROWS = GT * ROWS + TAIL
GATHER_ROWS = GT * ROWS + LAMR


def pack_kernel(parts, keep_lam, send_lam, out):
    total = parts[0].astype(f32)
    for i in range(1, WIDE):
        total = total + parts[i].astype(f32)
    lam = lam_rows(keep_lam[...] + send_lam[...])
    for j in range(GT):
        tile = total[:, j * LANES : (j + 1) * LANES].astype(bf16)
        for k in range(DEEP):
            out[k, pl.ds(j * ROWS, ROWS), :] = tile
    pad = jnp.zeros((TAIL - FT * FR - LAMR, LANES), f32)
    for k in range(DEEP):
        rows = total[k * FR : (k + 1) * FR]
        pieces = [rows[:, D + t * LANES : D + (t + 1) * LANES] for t in range(FT)]
        out[k, pl.ds(GT * ROWS, TAIL), :] = jnp.concatenate(pieces + [lam, pad], axis=0).astype(bf16)


def rotate_kernel(place, got, basis, out, stay, cross):
    total = got[0].astype(f32)
    for i in range(1, DEEP):
        total = total + got[i].astype(f32)
    grad = jnp.concatenate([total[j * ROWS : (j + 1) * ROWS] for j in range(GT)], axis=1)
    rot = dot(grad.astype(bf16), basis[...]).astype(bf16)
    base = GT * ROWS
    lam = lam_rows(read_lam(total[base + FT * FR : base + FT * FR + LAMR])).astype(bf16)
    for j in range(GT):
        tile = rot[:, j * LANES : (j + 1) * LANES]
        for i in range(WIDE):
            out[i, pl.ds(j * ROWS, ROWS), :] = tile
    for i in range(WIDE):
        out[i, pl.ds(base, LAMR), :] = lam
    k, c = place[0], place[1]
    rows = grad[0:FR]
    for other in range(1, DEEP):
        rows = jnp.where(k == other, grad[other * FR : (other + 1) * FR], rows)
    factors = [total[base + t * FR : base + (t + 1) * FR] for t in range(FT)]
    full = jnp.concatenate(factors[:GT], axis=1)
    part = jnp.concatenate(factors[GT:], axis=1)

    def lines(a):
        halves = jnp.concatenate([part[a : a + 1], part[a + 1 : a + 2]], axis=1)
        return jnp.concatenate([jnp.zeros((3, D), f32), rows[a : a + 2], full[a : a + 2], halves], axis=0)

    low, high = lines(0), lines(2)
    stay[...] = jnp.where(c == 0, low, high)
    cross[...] = jnp.where(c == 0, high, low)


def solve_kernel(got, basis_in_t, basis_out, rows_in, stay, cross, own, their, scaled):
    base = GT * ROWS
    lam = got[0, pl.ds(base, LAMR), :].astype(f32)
    for i in range(1, WIDE):
        lam = lam + got[i, pl.ds(base, LAMR), :].astype(f32)
    lam = read_lam(lam)
    column = jnp.broadcast_to(lam[0:1], (8, D)).T[:, 0:1]
    column = jnp.broadcast_to(column, (D, LANES))
    curve = jnp.zeros((8, LANES), f32)
    for j in range(GT):
        rot = got[:, pl.ds(j * ROWS, ROWS), :].reshape(D, LANES)
        rotated = dot(basis_in_t[...], rot)
        low = (rotated / (column * lam[1:2, j * LANES : (j + 1) * LANES] + damping)).astype(bf16)
        scaled[:, pl.ds(j * LANES, LANES)] = low
        curve = curve + jnp.sum((low.astype(f32) * rotated).reshape(D // 8, 8, LANES), axis=0)
    curve = jnp.sum(jnp.sum(curve, axis=1, keepdims=True), axis=0, keepdims=True)
    back = dot(rows_in[...], scaled[...]).astype(bf16)
    prec = lax.dot_general(back, basis_out[...], (((1,), (1,)), ((), ())), preferred_element_type=f32)
    prec = prec.astype(bf16).astype(f32)
    curve = jnp.broadcast_to(curve, (1, D))
    own[...] = jnp.concatenate([prec[0:2], curve, stay[3:8, :]], axis=0)
    their[...] = jnp.concatenate([prec[2:4], curve, cross[3:8, :]], axis=0)


def finish_kernel(scale, core, own, got, old, new_factors, gradients, updates):
    first = core[0] == 0
    curve = own[2:3, :] + got[2:3, :]
    factor = jnp.sqrt(kl_clip / (learn_rate * learn_rate * curve))
    side0 = jnp.where(first, own[...], got[...])
    side1 = jnp.where(first, got[...], own[...])
    updates[0] = (side0[0:2] * factor).astype(bf16)
    updates[1] = (side1[0:2] * factor).astype(bf16)
    gradients[:, 0, :] = side0[3:5]
    gradients[:, 1, :] = side1[3:5]
    left, right = side0[7:8], side1[7:8]
    batch = (
        jnp.concatenate(
            [
                jnp.concatenate([left[:, :HALF], right[:, :HALF]], axis=1),
                jnp.concatenate([left[:, HALF:], right[:, HALF:]], axis=1),
            ],
            axis=0,
        ),
        side0[5:7],
        side1[5:7],
    )
    for f in range(3):
        new_factors[f] = decay * old[f] + scale * batch[f]


def exchange(value, groups):
    return lax.all_to_all(value, "dp", 0, 0, axis_index_groups=groups, tiled=True)


def body(activations, grad_key, grad_value, time_start, time_width, bases, old_factors):
    index = lax.axis_index("dp").astype(jnp.int32)
    core = index % NC
    first = core == 0
    z = (index // NC) % NZ
    place = jnp.stack([z // PAIR, core])
    tokens_here = activations.shape[0]
    share = (1.0 - decay) / (tokens_here * lax.axis_size("dp"))

    def in_hbm(value):
        return pltpu.with_memory_space_constraint(value, pltpu.HBM)

    masks = (in_hbm(time_start.T), in_hbm(time_width.T))
    frames, keys, vals = in_hbm(activations), in_hbm(grad_key), in_hbm(grad_value)
    mask_buf = pltpu.VMEM((2,) + time_start.shape[::-1], jnp.int32)
    buf = pltpu.VMEM((tokens_here, D), bf16)
    sems = pltpu.SemaphoreType.DMA((CHUNKS,))
    pair = pltpu.SemaphoreType.DMA((2,))
    partial = shape((NXY, PAIR, ROWS, COLS), bf16)
    work = 2 * D * tokens_here * COLS
    with jax.named_scope("grams_theirs"):
        other, kept = call(
            theirs_kernel,
            (partial, shape((tokens_here, D), bf16)),
            [SMEM] + [HBM] * 5,
            [buf, buf, mask_buf, sems, sems, pair],
            flops=work,
            moved=4 * MB,
        )(core[None], *masks, frames, keys, vals)
    received = lax.ppermute(other, "dp", SWAP)
    with jax.named_scope("grams_mine"):
        mine = call(
            mine_kernel,
            partial,
            [SMEM, HBM, HBM, VMEM, HBM, HBM],
            [buf, mask_buf, sems, pair],
            flops=work,
            moved=4 * MB,
        )(core[None], *masks, kept, keys, vals)
    with jax.named_scope("chip_sum"):
        chip = (mine.astype(f32) + received.astype(f32)).astype(bf16).reshape(WIDE, ROWS, COLS)
    with jax.named_scope("wide_sum"):
        parts = exchange(chip, WIDE_GROUPS)

    lam_shape = shape((2, D), f32)
    with jax.named_scope("lam"):
        keep_lam, send_lam, basis_in_t = call(
            functools.partial(lam_kernel, share),
            (lam_shape, lam_shape, shape((D, D), bf16)),
            [SMEM] + [VMEM] * 3,
            flops=6 * D * D * D,
            moved=4 * MB,
        )(core[None], mine.reshape(WIDE, ROWS, COLS), other.reshape(WIDE, ROWS, COLS), bases)
    old_lam = []
    my_rows = lax.dynamic_slice_in_dim(bases, 2 * index, 2, 1).astype(f32)
    for f in range(3):
        old_image = jnp.dot(old_factors[:, f, :], bases[f].astype(f32), precision=lax.Precision.HIGHEST)
        old_lam.append(decay * jnp.sum(my_rows[f] * old_image, axis=0))
    keep_lam = keep_lam + jnp.stack([old_lam[0], jnp.where(first, old_lam[1], old_lam[2])])
    send_lam = send_lam + jnp.stack([old_lam[0], jnp.where(first, old_lam[2], old_lam[1])])
    sent_lam = lax.ppermute(send_lam, "dp", SWAP)

    with jax.named_scope("pack"):
        packed = call(pack_kernel, shape((DEEP, DEEP_ROWS, LANES), bf16), [VMEM] * 3)(parts, keep_lam, sent_lam)
    with jax.named_scope("deep_sum"):
        got = exchange(packed, DEEP_GROUPS)
    basis_out = lax.dynamic_index_in_dim(bases, 1 + core, 0, keepdims=False)
    lines = shape((8, D), f32)
    with jax.named_scope("rotate"):
        spread, stay, cross = call(
            rotate_kernel,
            (shape((WIDE, GATHER_ROWS, LANES), bf16), lines, lines),
            [SMEM, VMEM, VMEM],
        )(place, got, basis_out)
    with jax.named_scope("gather"):
        gathered = exchange(spread, WIDE_GROUPS)
    rows_in = lax.dynamic_slice_in_dim(bases[0], (index // NC) * FR, FR, 0)
    rows_in = jnp.where(first, rows_in, jnp.roll(rows_in, 2, axis=0))
    rows_in = jnp.pad(rows_in, ((0, 16 - FR), (0, 0)))
    with jax.named_scope("solve"):
        own, their = call(solve_kernel, (lines, lines), [VMEM] * 6, [pltpu.VMEM((D, D), bf16)])(
            gathered, basis_in_t, basis_out, rows_in, stay, cross
        )
    theirs = lax.ppermute(their, "dp", SWAP)
    with jax.named_scope("finish"):
        new_factors, gradients, updates = call(
            functools.partial(finish_kernel, share),
            (shape((3, 2, D), f32), shape((2, 2, D), f32), shape((2, 2, D), bf16)),
            [SMEM] + [VMEM] * 3,
        )(core[None], own, theirs, jnp.transpose(old_factors, (1, 0, 2)))
    return (jnp.transpose(new_factors, (1, 0, 2)), gradients, updates)


def solution(mesh):
    in_specs = (
        P("dp", None),
        P("dp", None),
        P("dp", None),
        P("dp", None),
        P("dp", None),
        P(),
        P("dp", None, None),
    )
    out_specs = (P("dp", None, None), P("dp", None, None), P(None, "dp", None))
    return jax.shard_map(body, mesh=mesh, in_specs=in_specs, out_specs=out_specs, check_vma=False)
```

```python
import functools

import jax
import jax.numpy as jnp
from jax import lax
from jax.experimental import pallas as pl
from jax.experimental.pallas import tpu as pltpu
from jax.sharding import PartitionSpec as P

LEN = 128
NX, NY, NZ, NC = 4, 4, 8, 2
NXY = NX * NY
D = 512
HALF = D // 2
PAIR = 2
WIDE = NXY * PAIR
DEEP = NZ // PAIR
ROWS = D // WIDE
COLS = D + D + HALF
LANES = 128
FR = ROWS // DEEP
GT, FT = D // LANES, (D + HALF) // LANES
MB = 1 << 20

decay = 0.8
damping = 0.001
kl_clip = 0.001
learn_rate = 7e-05

f32, bf16 = jnp.float32, jnp.bfloat16


def device(xy, z, c):
    return (xy * NZ + z) * NC + c


SWAP = [(d, d ^ 1) for d in range(NXY * NZ * NC)]
WIDE_GROUPS = [
    [device(i, k * PAIR + l, c) for i in range(NXY) for l in range(PAIR)]
    for k in range(DEEP)
    for c in range(NC)
]
DEEP_GROUPS = [
    [device(i, k * PAIR + l, c) for k in range(DEEP)] for i in range(NXY) for l in range(PAIR) for c in range(NC)
]
VMEM = pl.BlockSpec(memory_space=pltpu.VMEM)
SMEM = pl.BlockSpec(memory_space=pltpu.SMEM)
HBM = pl.BlockSpec(memory_space=pltpu.HBM)
CHUNKS = 2


def call(kernel, outs, in_specs, scratch=(), limit=16, flops=0, moved=0):
    return pl.pallas_call(
        kernel,
        out_shape=outs,
        in_specs=in_specs,
        out_specs=jax.tree.map(lambda _: VMEM, outs),
        scratch_shapes=list(scratch),
        compiler_params=pltpu.CompilerParams(vmem_limit_bytes=limit * MB),
        cost_estimate=pl.CostEstimate(flops=flops, bytes_accessed=moved, transcendentals=0),
    )


def shape(dims, dtype):
    return jax.ShapeDtypeStruct(dims, dtype)


def dot(a, b):
    return jnp.dot(a, b, preferred_element_type=f32)


def arrange(value):
    size = value.shape[1]
    pairs = value.reshape(value.shape[0] // 16, 2, 8, size)
    even, odd = pairs[:, 0], pairs[:, 1]
    upper = lax.broadcasted_iota(jnp.int32, even.shape, 1) < FR
    low = jnp.where(upper, even, pltpu.roll(odd, FR, 1))
    high = jnp.where(upper, pltpu.roll(even, FR, 1), odd)
    blocks = (value.shape[0] // (PAIR * ROWS), ROWS, size)
    return low.reshape(blocks), high.reshape(blocks)


def build_keep(start, width, keep):
    position = lax.broadcasted_iota(jnp.int32, (LEN, LANES), 0)
    for u in range(start.shape[1]):
        inside = None
        for m in range(start.shape[0]):
            s = start[m : m + 1, u : u + 1]
            here = (position >= s) & (position < s + width[m : m + 1, u : u + 1])
            inside = here if inside is None else inside | here
        keep[pl.ds(u * LEN, LEN), :] = jnp.where(inside, 0.0, 1.0).astype(bf16)


def apply_mask(source, target, keep, q):
    rows = pl.ds(q * (source.shape[0] // CHUNKS), source.shape[0] // CHUNKS)
    for j in range(GT):
        view = (rows, pl.ds(j * LANES, LANES))
        target[view] = source[view] * keep[rows, :]


def fetch(source, target, sems):
    rows = source.shape[0] // CHUNKS
    return [
        pltpu.make_async_copy(source.at[pl.ds(q * rows, rows)], target.at[pl.ds(q * rows, rows)], sems.at[q])
        for q in range(CHUNKS)
    ]


def fetch_picked(pick, xk, xv, target, sems):
    @pl.when(pick == 0)
    def _():
        for copy in fetch(xk, target, sems):
            copy.start()

    @pl.when(pick != 0)
    def _():
        for copy in fetch(xv, target, sems):
            copy.start()

    return fetch(xk, target, sems)


BLOCK = 256


def put(out, r, value, begin):
    places, cols = pl.ds(r * (BLOCK // (PAIR * ROWS)), BLOCK // (PAIR * ROWS)), pl.ds(begin, value.shape[1])
    low, high = arrange(value)
    out[places, 0, :, cols] = low.astype(bf16)
    out[places, 1, :, cols] = high.astype(bf16)


def grams(pick, x0, x1, ready, out):
    half = pl.ds(pl.multiple_of(pick * HALF, HALF), HALF)
    lefts = []
    for r in range(D // BLOCK):
        lefts.append(x0[:, pl.ds(r * BLOCK, BLOCK)].T)
        put(out, r, dot(lefts[r], x0[:, half]), 2 * D)
    ready()
    for r in range(D // BLOCK):
        put(out, r, dot(lefts[r], x1[...]), 0)
    for r in range(D // BLOCK):
        left = x1[:, pl.ds(r * BLOCK, BLOCK)].T
        put(out, r, dot(left, x1[...]), D)


def theirs_kernel(core, start, width, x0, xk, xv, out, kept, keep, buf0, buf1, masks, sem0, sem1, sem2):
    pick = 1 - core[0]
    small = [pltpu.make_async_copy(v, masks.at[i], sem2.at[i]) for i, v in enumerate((start, width))]
    copies0 = fetch(x0, buf0, sem0)
    for copy in small + copies0:
        copy.start()
    copies1 = fetch_picked(pick, xk, xv, buf1, sem1)
    for copy in small:
        copy.wait()
    build_keep(masks.at[0], masks.at[1], keep)
    for q in range(CHUNKS):
        copies0[q].wait()
        apply_mask(buf0, kept, keep, q)

    def ready():
        for q in range(CHUNKS):
            copies1[q].wait()
            apply_mask(buf1, buf1, keep, q)

    grams(pick, kept, buf1, ready, out)


def mine_kernel(core, keep, x0, xk, xv, out, buf1, sem1):
    pick = core[0]
    copies1 = fetch_picked(pick, xk, xv, buf1, sem1)

    def ready():
        for q in range(CHUNKS):
            copies1[q].wait()
            apply_mask(buf1, buf1, keep, q)

    grams(pick, x0, buf1, ready, out)


def add_kernel(mine, received, out):
    for i in range(NXY):
        for j in range(PAIR):
            out[i, j] = mine[i, j] + received[i, j]


def lam_kernel(share, core, mine, other, bases, keep_lam, send_lam, basis_in_t):
    c = core[0]

    def image(source, begin, size, basis):
        return dot(source[:, :, pl.ds(begin, size)].reshape(D, size), basis)

    def arranged(index):
        low, high = arrange(bases[index].astype(f32))
        return jnp.concatenate([low, high], axis=1).reshape(D, D)

    def values(basis, product):
        return jnp.sum(basis * product, axis=0, keepdims=True) * share

    near = pl.ds(pl.multiple_of(c * HALF, HALF), HALF)
    far = pl.ds(pl.multiple_of((1 - c) * HALF, HALF), HALF)
    basis = arranged(0)
    basis_in_t[...] = basis.T.astype(bf16)
    lam0 = values(basis, image(mine, 2 * D, HALF, bases[0, near, :]) + image(other, 2 * D, HALF, bases[0, far, :]))
    keep_lam[0:1, :] = lam0
    send_lam[0:1, :] = lam0
    keep_lam[1:2, :] = values(arranged(1 + c), image(mine, D, D, bases[1 + c]))
    send_lam[1:2, :] = values(arranged(2 - c), image(other, D, D, bases[2 - c]))


def split(value):
    high = value.astype(bf16)
    return high.astype(f32), value - high.astype(f32)


def lam_rows(lam):
    return jnp.concatenate(split(jnp.concatenate([lam[:, j * LANES : (j + 1) * LANES] for j in range(GT)], axis=0)), axis=0)


def add_lam(rows):
    return rows[: 2 * GT] + rows[2 * GT :]


def lam_row(total, index):
    return jnp.concatenate([total[2 * j + index : 2 * j + index + 1] for j in range(GT)], axis=1)


LAMR = 4 * GT
TAIL = ((FT * FR + LAMR + 15) // 16) * 16
DEEP_ROWS = GT * ROWS + TAIL
GATHER_ROWS = GT * ROWS + LAMR


def pack_kernel(parts, keep_lam, send_lam, out):
    total = parts[0].astype(f32)
    for i in range(1, WIDE):
        total = total + parts[i].astype(f32)
    lam = lam_rows(keep_lam[...] + send_lam[...])
    for j in range(GT):
        tile = total[:, j * LANES : (j + 1) * LANES].astype(bf16)
        for k in range(DEEP):
            out[k, pl.ds(j * ROWS, ROWS), :] = tile
    pad = jnp.zeros((TAIL - FT * FR - LAMR, LANES), f32)
    for k in range(DEEP):
        rows = total[k * FR : (k + 1) * FR]
        pieces = [rows[:, D + t * LANES : D + (t + 1) * LANES] for t in range(FT)]
        out[k, pl.ds(GT * ROWS, TAIL), :] = jnp.concatenate(pieces + [lam, pad], axis=0).astype(bf16)


def rotate_kernel(got, basis, out):
    total = got[0].astype(f32)
    for i in range(1, DEEP):
        total = total + got[i].astype(f32)
    grad = jnp.concatenate([total[j * ROWS : (j + 1) * ROWS] for j in range(GT)], axis=1)
    rot = dot(grad.astype(bf16), basis[...]).astype(bf16)
    base = GT * ROWS
    lam = add_lam(total[base + FT * FR : base + FT * FR + LAMR])
    lam = jnp.concatenate(split(lam), axis=0).astype(bf16)
    for i in range(WIDE):
        out[i, pl.ds(base, LAMR), :] = lam
    for j in range(GT):
        tile = rot[:, j * LANES : (j + 1) * LANES]
        for i in range(WIDE):
            out[i, pl.ds(j * ROWS, ROWS), :] = tile


def rows_kernel(place, got, stay, cross):
    total = got[0].astype(f32)
    for i in range(1, DEEP):
        total = total + got[i].astype(f32)
    grad = jnp.concatenate([total[j * ROWS : (j + 1) * ROWS] for j in range(GT)], axis=1)
    base = GT * ROWS
    k, c = place[0], place[1]
    rows = grad[0:FR]
    for other in range(1, DEEP):
        rows = jnp.where(k == other, grad[other * FR : (other + 1) * FR], rows)
    factors = [total[base + t * FR : base + (t + 1) * FR] for t in range(FT)]
    full = jnp.concatenate(factors[:GT], axis=1)
    part = jnp.concatenate(factors[GT:], axis=1)

    def lines(a):
        halves = jnp.concatenate([part[a : a + 1], part[a + 1 : a + 2]], axis=1)
        return jnp.concatenate([jnp.zeros((3, D), f32), rows[a : a + 2], full[a : a + 2], halves], axis=0)

    low, high = lines(0), lines(2)
    stay[...] = jnp.where(c == 0, low, high)
    cross[...] = jnp.where(c == 0, high, low)


def solve_kernel(got, basis_in_t, basis_out, rows_in, stay, cross, own, their, scaled):
    base = GT * ROWS
    lam = got[0, pl.ds(base, LAMR), :].astype(f32)
    for i in range(1, WIDE):
        lam = lam + got[i, pl.ds(base, LAMR), :].astype(f32)
    lam = add_lam(lam)
    column = jnp.broadcast_to(lam_row(lam, 0), (8, D)).T[:, 0:1]
    column = jnp.broadcast_to(column, (D, LANES))
    curve = jnp.zeros((8, LANES), f32)
    for j in range(GT):
        rot = got[:, pl.ds(j * ROWS, ROWS), :].reshape(D, LANES)
        rotated = dot(basis_in_t[...], rot)
        low = (rotated / (column * lam[2 * j + 1 : 2 * j + 2] + damping)).astype(bf16)
        scaled[:, pl.ds(j * LANES, LANES)] = low
        curve = curve + jnp.sum((low.astype(f32) * rotated).reshape(D // 8, 8, LANES), axis=0)
    curve = jnp.sum(jnp.sum(curve, axis=1, keepdims=True), axis=0, keepdims=True)
    back = dot(rows_in[...], scaled[...]).astype(bf16)
    prec = lax.dot_general(back, basis_out[...], (((1,), (1,)), ((), ())), preferred_element_type=f32)
    prec = prec.astype(bf16).astype(f32)
    curve = jnp.broadcast_to(curve, (1, D))
    own[...] = jnp.concatenate([prec[0:2], curve, stay[3:8, :]], axis=0)
    their[...] = jnp.concatenate([prec[2:4], curve, cross[3:8, :]], axis=0)


def finish_kernel(scale, core, own, got, old, new_factors, gradients, updates):
    first = core[0] == 0
    curve = own[2:3, :] + got[2:3, :]
    factor = jnp.sqrt(kl_clip / (learn_rate * learn_rate * curve))
    side0 = jnp.where(first, own[...], got[...])
    side1 = jnp.where(first, got[...], own[...])
    updates[0] = (side0[0:2] * factor).astype(bf16)
    updates[1] = (side1[0:2] * factor).astype(bf16)
    gradients[:, 0, :] = side0[3:5]
    gradients[:, 1, :] = side1[3:5]
    left, right = side0[7:8], side1[7:8]
    batch = (
        jnp.concatenate(
            [
                jnp.concatenate([left[:, :HALF], right[:, :HALF]], axis=1),
                jnp.concatenate([left[:, HALF:], right[:, HALF:]], axis=1),
            ],
            axis=0,
        ),
        side0[5:7],
        side1[5:7],
    )
    for f in range(3):
        new_factors[f] = decay * old[f] + scale * batch[f]


def exchange(value, groups):
    return lax.all_to_all(value, "dp", 0, 0, axis_index_groups=groups, tiled=True)


def body(activations, grad_key, grad_value, time_start, time_width, bases, old_factors):
    index = lax.axis_index("dp").astype(jnp.int32)
    core = index % NC
    first = core == 0
    z = (index // NC) % NZ
    place = jnp.stack([z // PAIR, core])
    tokens_here = activations.shape[0]
    share = (1.0 - decay) / (tokens_here * lax.axis_size("dp"))

    def in_hbm(value):
        return pltpu.with_memory_space_constraint(value, pltpu.HBM)

    masks = (in_hbm(time_start.T), in_hbm(time_width.T))
    frames, keys, vals = in_hbm(activations), in_hbm(grad_key), in_hbm(grad_value)
    mask_buf = pltpu.VMEM((2,) + time_start.shape[::-1], jnp.int32)
    buf = pltpu.VMEM((tokens_here, D), bf16)
    sems = pltpu.SemaphoreType.DMA((CHUNKS,))
    pair = pltpu.SemaphoreType.DMA((2,))
    partial = shape((NXY, PAIR, ROWS, COLS), bf16)
    work = 2 * D * tokens_here * COLS
    with jax.named_scope("grams_theirs"):
        other, kept, keep = call(
            theirs_kernel,
            (partial, shape((tokens_here, D), bf16), shape((tokens_here, LANES), bf16)),
            [SMEM] + [HBM] * 5,
            [buf, buf, mask_buf, sems, sems, pair],
            flops=work,
            moved=4 * MB,
        )(core[None], *masks, frames, keys, vals)
    received = lax.ppermute(other, "dp", SWAP)
    with jax.named_scope("grams_mine"):
        mine = call(
            mine_kernel,
            partial,
            [SMEM, VMEM, VMEM, HBM, HBM],
            [buf, sems],
            flops=work,
            moved=4 * MB,
        )(core[None], keep, kept, keys, vals)
    with jax.named_scope("chip_sum"):
        chip = call(add_kernel, partial, [VMEM] * 2)(mine, received).reshape(WIDE, ROWS, COLS)
    with jax.named_scope("wide_sum"):
        parts = exchange(chip, WIDE_GROUPS)

    lam_shape = shape((2, D), f32)
    with jax.named_scope("lam"):
        keep_lam, send_lam, basis_in_t = call(
            functools.partial(lam_kernel, share),
            (lam_shape, lam_shape, shape((D, D), bf16)),
            [SMEM] + [VMEM] * 3,
            flops=6 * D * D * D,
            moved=4 * MB,
        )(core[None], mine.reshape(WIDE, ROWS, COLS), other.reshape(WIDE, ROWS, COLS), bases)
    old_lam = []
    my_rows = lax.dynamic_slice_in_dim(bases, 2 * index, 2, 1).astype(f32)
    for f in range(3):
        old_image = jnp.dot(old_factors[:, f, :], bases[f].astype(f32), precision=lax.Precision.HIGHEST)
        old_lam.append(decay * jnp.sum(my_rows[f] * old_image, axis=0))
    keep_lam = keep_lam + jnp.stack([old_lam[0], jnp.where(first, old_lam[1], old_lam[2])])
    send_lam = send_lam + jnp.stack([old_lam[0], jnp.where(first, old_lam[2], old_lam[1])])
    sent_lam = lax.ppermute(send_lam, "dp", SWAP)

    with jax.named_scope("pack"):
        packed = call(pack_kernel, shape((DEEP, DEEP_ROWS, LANES), bf16), [VMEM] * 3)(parts, keep_lam, sent_lam)
    with jax.named_scope("deep_sum"):
        got = exchange(packed, DEEP_GROUPS)
    basis_out = lax.dynamic_index_in_dim(bases, 1 + core, 0, keepdims=False)
    lines = shape((8, D), f32)
    with jax.named_scope("rotate"):
        spread = call(rotate_kernel, shape((WIDE, GATHER_ROWS, LANES), bf16), [VMEM] * 2)(got, basis_out)
    with jax.named_scope("gather"):
        gathered = exchange(spread, WIDE_GROUPS)
    with jax.named_scope("rows"):
        stay, cross = call(rows_kernel, (lines, lines), [SMEM, VMEM])(place, got)
    rows_in = lax.dynamic_slice_in_dim(bases[0], (index // NC) * FR, FR, 0)
    rows_in = jnp.where(first, rows_in, jnp.roll(rows_in, 2, axis=0))
    rows_in = jnp.pad(rows_in, ((0, 16 - FR), (0, 0)))
    with jax.named_scope("solve"):
        own, their = call(solve_kernel, (lines, lines), [VMEM] * 6, [pltpu.VMEM((D, D), bf16)])(
            gathered, basis_in_t, basis_out, rows_in, stay, cross
        )
    theirs = lax.ppermute(their, "dp", SWAP)
    with jax.named_scope("finish"):
        new_factors, gradients, updates = call(
            functools.partial(finish_kernel, share),
            (shape((3, 2, D), f32), shape((2, 2, D), f32), shape((2, 2, D), bf16)),
            [SMEM] + [VMEM] * 3,
        )(core[None], own, theirs, jnp.transpose(old_factors, (1, 0, 2)))
    return (jnp.transpose(new_factors, (1, 0, 2)), gradients, updates)


def solution(mesh):
    in_specs = (
        P("dp", None),
        P("dp", None),
        P("dp", None),
        P("dp", None),
        P("dp", None),
        P(),
        P("dp", None, None),
    )
    out_specs = (P("dp", None, None), P("dp", None, None), P(None, "dp", None))
    return jax.shard_map(body, mesh=mesh, in_specs=in_specs, out_specs=out_specs, check_vma=False)
```

```python
import functools

import jax
import jax.numpy as jnp
from jax import lax
from jax.experimental import pallas as pl
from jax.experimental.pallas import tpu as pltpu
from jax.sharding import PartitionSpec as P

LEN = 128
NX, NY, NZ, NC = 4, 4, 8, 2
NXY = NX * NY
D = 512
HALF = D // 2
PAIR = 2
WIDE = NXY * PAIR
DEEP = NZ // PAIR
ROWS = D // WIDE
COLS = D + D + HALF
LANES = 128
FR = ROWS // DEEP
GT, FT = D // LANES, (D + HALF) // LANES
MB = 1 << 20

decay = 0.8
damping = 0.001
kl_clip = 0.001
learn_rate = 7e-05

f32, bf16 = jnp.float32, jnp.bfloat16


def device(xy, z, c):
    return (xy * NZ + z) * NC + c


SWAP = [(d, d ^ 1) for d in range(NXY * NZ * NC)]
WIDE_GROUPS = [
    [device(i, k * PAIR + l, c) for i in range(NXY) for l in range(PAIR)]
    for k in range(DEEP)
    for c in range(NC)
]
DEEP_GROUPS = [
    [device(i, k * PAIR + l, c) for k in range(DEEP)] for i in range(NXY) for l in range(PAIR) for c in range(NC)
]
VMEM = pl.BlockSpec(memory_space=pltpu.VMEM)
SMEM = pl.BlockSpec(memory_space=pltpu.SMEM)
HBM = pl.BlockSpec(memory_space=pltpu.HBM)
CHUNKS = 2


def call(kernel, outs, in_specs, scratch=(), limit=16, flops=0, moved=0):
    return pl.pallas_call(
        kernel,
        out_shape=outs,
        in_specs=in_specs,
        out_specs=jax.tree.map(lambda out: HBM if isinstance(out, pl.MemoryRef) else VMEM, outs),
        scratch_shapes=list(scratch),
        compiler_params=pltpu.CompilerParams(vmem_limit_bytes=limit * MB),
        cost_estimate=pl.CostEstimate(flops=flops, bytes_accessed=moved, transcendentals=0),
    )


def shape(dims, dtype):
    return jax.ShapeDtypeStruct(dims, dtype)


def dot(a, b):
    return jnp.dot(a, b, preferred_element_type=f32)


def arrange(value):
    size = value.shape[1]
    pairs = value.reshape(value.shape[0] // 16, 2, 8, size)
    even, odd = pairs[:, 0], pairs[:, 1]
    upper = lax.broadcasted_iota(jnp.int32, even.shape, 1) < FR
    low = jnp.where(upper, even, pltpu.roll(odd, FR, 1))
    high = jnp.where(upper, pltpu.roll(even, FR, 1), odd)
    blocks = (value.shape[0] // (PAIR * ROWS), ROWS, size)
    return low.reshape(blocks), high.reshape(blocks)


def build_keep(start, width, keep):
    position = lax.broadcasted_iota(jnp.int32, (LEN, LANES), 0)
    for u in range(start.shape[1]):
        inside = None
        for m in range(start.shape[0]):
            s = start[m : m + 1, u : u + 1]
            here = (position >= s) & (position < s + width[m : m + 1, u : u + 1])
            inside = here if inside is None else inside | here
        keep[pl.ds(u * LEN, LEN), :] = jnp.where(inside, 0.0, 1.0).astype(bf16)


def apply_mask(source, target, keep, q):
    rows = pl.ds(q * (source.shape[0] // CHUNKS), source.shape[0] // CHUNKS)
    for j in range(GT):
        view = (rows, pl.ds(j * LANES, LANES))
        target[view] = source[view] * keep[rows, :]


def fetch(source, target, sems):
    rows = source.shape[0] // CHUNKS
    return [
        pltpu.make_async_copy(source.at[pl.ds(q * rows, rows)], target.at[pl.ds(q * rows, rows)], sems.at[q])
        for q in range(CHUNKS)
    ]


def fetch_picked(pick, xk, xv, target, sems):
    @pl.when(pick == 0)
    def _():
        for copy in fetch(xk, target, sems):
            copy.start()

    @pl.when(pick != 0)
    def _():
        for copy in fetch(xv, target, sems):
            copy.start()

    return fetch(xk, target, sems)


BLOCK = 256


def put(out, r, value, begin):
    places, cols = pl.ds(r * (BLOCK // (PAIR * ROWS)), BLOCK // (PAIR * ROWS)), pl.ds(begin, value.shape[1])
    low, high = arrange(value)
    out[places, 0, :, cols] = low.astype(bf16)
    out[places, 1, :, cols] = high.astype(bf16)


def grams(pick, x0, x1, ready, out):
    half = pl.ds(pl.multiple_of(pick * HALF, HALF), HALF)
    lefts = []
    for r in range(D // BLOCK):
        lefts.append(x0[:, pl.ds(r * BLOCK, BLOCK)].T)
        put(out, r, dot(lefts[r], x0[:, half]), 2 * D)
    ready()
    for r in range(D // BLOCK):
        put(out, r, dot(lefts[r], x1[...]), 0)
    for r in range(D // BLOCK):
        left = x1[:, pl.ds(r * BLOCK, BLOCK)].T
        put(out, r, dot(left, x1[...]), D)


def theirs_kernel(core, start, width, x0, xk, xv, out, kept, keep, buf0, buf1, masks, sem0, sem1, sem2):
    pick = 1 - core[0]
    small = [pltpu.make_async_copy(v, masks.at[i], sem2.at[i]) for i, v in enumerate((start, width))]
    copies0 = fetch(x0, buf0, sem0)
    for copy in small + copies0:
        copy.start()
    copies1 = fetch_picked(pick, xk, xv, buf1, sem1)
    for copy in small:
        copy.wait()
    build_keep(masks.at[0], masks.at[1], keep)
    for q in range(CHUNKS):
        copies0[q].wait()
        apply_mask(buf0, kept, keep, q)

    def ready():
        for q in range(CHUNKS):
            copies1[q].wait()
            apply_mask(buf1, buf1, keep, q)

    grams(pick, kept, buf1, ready, out)


def mine_kernel(core, keep, x0, xk, xv, out, buf1, sem1):
    pick = core[0]
    copies1 = fetch_picked(pick, xk, xv, buf1, sem1)

    def ready():
        for q in range(CHUNKS):
            copies1[q].wait()
            apply_mask(buf1, buf1, keep, q)

    grams(pick, x0, buf1, ready, out)


PIECES = 4


def add_kernel(mine, received, out, buf, sems):
    size = NXY // PIECES
    copies = []
    for q in range(PIECES):
        for i in range(q * size, (q + 1) * size):
            for j in range(PAIR):
                buf[i, j] = mine[i, j] + received[i, j]
        part = pl.ds(q * size, size)
        copies.append(pltpu.make_async_copy(buf.at[part], out.at[part], sems.at[q]))
        copies[q].start()
    for copy in copies:
        copy.wait()


def lam_kernel(share, core, chip, bases, keep_lam, send_lam, basis_in_t, buf, sem):
    c = core[0]
    fetched = pltpu.make_async_copy(chip.at[:, :, pl.ds(D, D + HALF)], buf, sem)
    fetched.start()

    def image(begin, size, basis):
        return dot(buf[:, :, pl.ds(begin, size)].reshape(D, size), basis)

    def arranged(index):
        low, high = arrange(bases[index].astype(f32))
        return jnp.concatenate([low, high], axis=1).reshape(D, D)

    def values(basis, product):
        return jnp.sum(basis * product, axis=0, keepdims=True) * share

    near = pl.ds(pl.multiple_of(c * HALF, HALF), HALF)
    basis = arranged(0)
    basis_in_t[...] = basis.T.astype(bf16)
    fetched.wait()
    lam0 = values(basis, image(D, HALF, bases[0, near, :]))
    keep_lam[0:1, :] = lam0
    keep_lam[1:2, :] = values(arranged(1 + c), image(0, D, bases[1 + c]))
    send_lam[0:1, :] = lam0
    send_lam[1:2, :] = jnp.zeros((1, D), f32)


def split(value):
    high = value.astype(bf16)
    return high.astype(f32), value - high.astype(f32)


def lam_rows(lam):
    return jnp.concatenate(split(jnp.concatenate([lam[:, j * LANES : (j + 1) * LANES] for j in range(GT)], axis=0)), axis=0)


def add_lam(rows):
    return rows[: 2 * GT] + rows[2 * GT :]


def lam_row(total, index):
    return jnp.concatenate([total[2 * j + index : 2 * j + index + 1] for j in range(GT)], axis=1)


LAMR = 4 * GT
TAIL = ((FT * FR + LAMR + 15) // 16) * 16
DEEP_ROWS = GT * ROWS + TAIL
GATHER_ROWS = GT * ROWS + LAMR


def pack_kernel(parts, keep_lam, send_lam, out):
    total = parts[0].astype(f32)
    for i in range(1, WIDE):
        total = total + parts[i].astype(f32)
    lam = lam_rows(keep_lam[...] + send_lam[...])
    for j in range(GT):
        tile = total[:, j * LANES : (j + 1) * LANES].astype(bf16)
        for k in range(DEEP):
            out[k, pl.ds(j * ROWS, ROWS), :] = tile
    pad = jnp.zeros((TAIL - FT * FR - LAMR, LANES), f32)
    for k in range(DEEP):
        rows = total[k * FR : (k + 1) * FR]
        pieces = [rows[:, D + t * LANES : D + (t + 1) * LANES] for t in range(FT)]
        out[k, pl.ds(GT * ROWS, TAIL), :] = jnp.concatenate(pieces + [lam, pad], axis=0).astype(bf16)


def rotate_kernel(got, basis, out):
    total = got[0].astype(f32)
    for i in range(1, DEEP):
        total = total + got[i].astype(f32)
    grad = jnp.concatenate([total[j * ROWS : (j + 1) * ROWS] for j in range(GT)], axis=1)
    rot = dot(grad.astype(bf16), basis[...]).astype(bf16)
    base = GT * ROWS
    lam = add_lam(total[base + FT * FR : base + FT * FR + LAMR])
    lam = jnp.concatenate(split(lam), axis=0).astype(bf16)
    for i in range(WIDE):
        out[i, pl.ds(base, LAMR), :] = lam
    for j in range(GT):
        tile = rot[:, j * LANES : (j + 1) * LANES]
        for i in range(WIDE):
            out[i, pl.ds(j * ROWS, ROWS), :] = tile


def rows_kernel(place, got, stay, cross):
    total = got[0].astype(f32)
    for i in range(1, DEEP):
        total = total + got[i].astype(f32)
    grad = jnp.concatenate([total[j * ROWS : (j + 1) * ROWS] for j in range(GT)], axis=1)
    base = GT * ROWS
    k, c = place[0], place[1]
    rows = grad[0:FR]
    for other in range(1, DEEP):
        rows = jnp.where(k == other, grad[other * FR : (other + 1) * FR], rows)
    factors = [total[base + t * FR : base + (t + 1) * FR] for t in range(FT)]
    full = jnp.concatenate(factors[:GT], axis=1)
    part = jnp.concatenate(factors[GT:], axis=1)

    def lines(a):
        halves = jnp.concatenate([part[a : a + 1], part[a + 1 : a + 2]], axis=1)
        return jnp.concatenate([jnp.zeros((3, D), f32), rows[a : a + 2], full[a : a + 2], halves], axis=0)

    low, high = lines(0), lines(2)
    stay[...] = jnp.where(c == 0, low, high)
    cross[...] = jnp.where(c == 0, high, low)


def solve_kernel(got, basis_in_t, basis_out, rows_in, stay, cross, own, their, scaled):
    base = GT * ROWS
    lam = got[0, pl.ds(base, LAMR), :].astype(f32)
    for i in range(1, WIDE):
        lam = lam + got[i, pl.ds(base, LAMR), :].astype(f32)
    lam = add_lam(lam)
    column = jnp.broadcast_to(lam_row(lam, 0), (8, D)).T[:, 0:1]
    column = jnp.broadcast_to(column, (D, LANES))
    curve = jnp.zeros((8, LANES), f32)
    for j in range(GT):
        rot = got[:, pl.ds(j * ROWS, ROWS), :].reshape(D, LANES)
        rotated = dot(basis_in_t[...], rot)
        low = (rotated / (column * lam[2 * j + 1 : 2 * j + 2] + damping)).astype(bf16)
        scaled[:, pl.ds(j * LANES, LANES)] = low
        curve = curve + jnp.sum((low.astype(f32) * rotated).reshape(D // 8, 8, LANES), axis=0)
    curve = jnp.sum(jnp.sum(curve, axis=1, keepdims=True), axis=0, keepdims=True)
    back = dot(rows_in[...], scaled[...]).astype(bf16)
    prec = lax.dot_general(back, basis_out[...], (((1,), (1,)), ((), ())), preferred_element_type=f32)
    prec = prec.astype(bf16).astype(f32)
    curve = jnp.broadcast_to(curve, (1, D))
    own[...] = jnp.concatenate([prec[0:2], curve, stay[3:8, :]], axis=0)
    their[...] = jnp.concatenate([prec[2:4], curve, cross[3:8, :]], axis=0)


def finish_kernel(scale, core, own, got, old, new_factors, gradients, updates):
    first = core[0] == 0
    curve = own[2:3, :] + got[2:3, :]
    factor = jnp.sqrt(kl_clip / (learn_rate * learn_rate * curve))
    side0 = jnp.where(first, own[...], got[...])
    side1 = jnp.where(first, got[...], own[...])
    updates[0] = (side0[0:2] * factor).astype(bf16)
    updates[1] = (side1[0:2] * factor).astype(bf16)
    gradients[:, 0, :] = side0[3:5]
    gradients[:, 1, :] = side1[3:5]
    left, right = side0[7:8], side1[7:8]
    batch = (
        jnp.concatenate(
            [
                jnp.concatenate([left[:, :HALF], right[:, :HALF]], axis=1),
                jnp.concatenate([left[:, HALF:], right[:, HALF:]], axis=1),
            ],
            axis=0,
        ),
        side0[5:7],
        side1[5:7],
    )
    for f in range(3):
        new_factors[f] = decay * old[f] + scale * batch[f]


def exchange(value, groups):
    return lax.all_to_all(value, "dp", 0, 0, axis_index_groups=groups, tiled=True)


def body(activations, grad_key, grad_value, time_start, time_width, bases, old_factors):
    index = lax.axis_index("dp").astype(jnp.int32)
    core = index % NC
    first = core == 0
    z = (index // NC) % NZ
    place = jnp.stack([z // PAIR, core])
    tokens_here = activations.shape[0]
    share = (1.0 - decay) / (tokens_here * lax.axis_size("dp"))

    def in_hbm(value):
        return pltpu.with_memory_space_constraint(value, pltpu.HBM)

    masks = (in_hbm(time_start.T), in_hbm(time_width.T))
    frames, keys, vals = in_hbm(activations), in_hbm(grad_key), in_hbm(grad_value)
    mask_buf = pltpu.VMEM((2,) + time_start.shape[::-1], jnp.int32)
    buf = pltpu.VMEM((tokens_here, D), bf16)
    sems = pltpu.SemaphoreType.DMA((CHUNKS,))
    pair = pltpu.SemaphoreType.DMA((2,))
    partial = shape((NXY, PAIR, ROWS, COLS), bf16)
    work = 2 * D * tokens_here * COLS
    with jax.named_scope("grams_theirs"):
        other, kept, keep = call(
            theirs_kernel,
            (partial, shape((tokens_here, D), bf16), shape((tokens_here, LANES), bf16)),
            [SMEM] + [HBM] * 5,
            [buf, buf, mask_buf, sems, sems, pair],
            flops=work,
            moved=4 * MB,
        )(core[None], *masks, frames, keys, vals)
    received = lax.ppermute(other, "dp", SWAP)
    with jax.named_scope("grams_mine"):
        mine = call(
            mine_kernel,
            partial,
            [SMEM, VMEM, VMEM, HBM, HBM],
            [buf, sems],
            flops=work,
            moved=4 * MB,
        )(core[None], keep, kept, keys, vals)
    with jax.named_scope("chip_sum"):
        chip = call(
            add_kernel,
            pltpu.HBM(partial.shape, bf16),
            [VMEM] * 2,
            [pltpu.VMEM(partial.shape, bf16), pltpu.SemaphoreType.DMA((PIECES,))],
        )(mine, received).reshape(WIDE, ROWS, COLS)
    with jax.named_scope("wide_sum"):
        parts = exchange(chip, WIDE_GROUPS)

    lam_shape = shape((2, D), f32)
    with jax.named_scope("lam"):
        keep_lam, send_lam, basis_in_t = call(
            functools.partial(lam_kernel, share),
            (lam_shape, lam_shape, shape((D, D), bf16)),
            [SMEM, HBM, VMEM],
            [pltpu.VMEM((WIDE, ROWS, D + HALF), bf16), pltpu.SemaphoreType.DMA],
            flops=3 * D * D * D,
            moved=3 * MB,
        )(core[None], in_hbm(chip), bases)
    old_lam = []
    my_rows = lax.dynamic_slice_in_dim(bases, 2 * index, 2, 1).astype(f32)
    for f in range(3):
        old_image = jnp.dot(old_factors[:, f, :], bases[f].astype(f32), precision=lax.Precision.HIGHEST)
        old_lam.append(decay * jnp.sum(my_rows[f] * old_image, axis=0))
    keep_lam = keep_lam + jnp.stack([old_lam[0], jnp.where(first, old_lam[1], old_lam[2])])
    send_lam = send_lam + jnp.stack([old_lam[0], jnp.where(first, old_lam[2], old_lam[1])])
    sent_lam = lax.ppermute(send_lam, "dp", SWAP)

    with jax.named_scope("pack"):
        packed = call(pack_kernel, shape((DEEP, DEEP_ROWS, LANES), bf16), [VMEM] * 3)(parts, keep_lam, sent_lam)
    with jax.named_scope("deep_sum"):
        got = exchange(packed, DEEP_GROUPS)
    basis_out = lax.dynamic_index_in_dim(bases, 1 + core, 0, keepdims=False)
    lines = shape((8, D), f32)
    with jax.named_scope("rotate"):
        spread = call(rotate_kernel, shape((WIDE, GATHER_ROWS, LANES), bf16), [VMEM] * 2)(got, basis_out)
    with jax.named_scope("gather"):
        gathered = exchange(spread, WIDE_GROUPS)
    with jax.named_scope("rows"):
        stay, cross = call(rows_kernel, (lines, lines), [SMEM, VMEM])(place, got)
    rows_in = lax.dynamic_slice_in_dim(bases[0], (index // NC) * FR, FR, 0)
    rows_in = jnp.where(first, rows_in, jnp.roll(rows_in, 2, axis=0))
    rows_in = jnp.pad(rows_in, ((0, 16 - FR), (0, 0)))
    with jax.named_scope("solve"):
        own, their = call(solve_kernel, (lines, lines), [VMEM] * 6, [pltpu.VMEM((D, D), bf16)])(
            gathered, basis_in_t, basis_out, rows_in, stay, cross
        )
    theirs = lax.ppermute(their, "dp", SWAP)
    with jax.named_scope("finish"):
        new_factors, gradients, updates = call(
            functools.partial(finish_kernel, share),
            (shape((3, 2, D), f32), shape((2, 2, D), f32), shape((2, 2, D), bf16)),
            [SMEM] + [VMEM] * 3,
        )(core[None], own, theirs, jnp.transpose(old_factors, (1, 0, 2)))
    return (jnp.transpose(new_factors, (1, 0, 2)), gradients, updates)


def solution(mesh):
    in_specs = (
        P("dp", None),
        P("dp", None),
        P("dp", None),
        P("dp", None),
        P("dp", None),
        P(),
        P("dp", None, None),
    )
    out_specs = (P("dp", None, None), P("dp", None, None), P(None, "dp", None))
    return jax.shard_map(body, mesh=mesh, in_specs=in_specs, out_specs=out_specs, check_vma=False)
```

```python
import functools

import jax
import jax.numpy as jnp
from jax import lax
from jax.experimental import pallas as pl
from jax.experimental.pallas import tpu as pltpu
from jax.sharding import PartitionSpec as P

LEN = 128
NX, NY, NZ, NC = 4, 4, 8, 2
NXY = NX * NY
D = 512
HALF = D // 2
PAIR = 2
WIDE = NXY * PAIR
DEEP = NZ // PAIR
ROWS = D // WIDE
LANES = 128
FR = ROWS // DEEP
GT = D // LANES
BLK = D // NXY
FA, F0, FL = GT * ROWS, (GT + 2) * ROWS, (GT + 3) * ROWS
WROWS = FL + ROWS // 2
MB = 1 << 20

decay = 0.8
damping = 0.001
kl_clip = 0.001
learn_rate = 7e-05

f32, bf16 = jnp.float32, jnp.bfloat16


def device(xy, z, c):
    return (xy * NZ + z) * NC + c


SWAP = [(d, d ^ 1) for d in range(NXY * NZ * NC)]
WIDE_GROUPS = [
    [device(i, k * PAIR + l, c) for i in range(NXY) for l in range(PAIR)]
    for k in range(DEEP)
    for c in range(NC)
]
DEEP_GROUPS = [
    [device(i, k * PAIR + l, c) for k in range(DEEP)] for i in range(NXY) for l in range(PAIR) for c in range(NC)
]
VMEM = pl.BlockSpec(memory_space=pltpu.VMEM)
SMEM = pl.BlockSpec(memory_space=pltpu.SMEM)
HBM = pl.BlockSpec(memory_space=pltpu.HBM)
CHUNKS = 2


def call(kernel, outs, in_specs, scratch=(), limit=16, flops=0, moved=0):
    return pl.pallas_call(
        kernel,
        out_shape=outs,
        in_specs=in_specs,
        out_specs=jax.tree.map(lambda out: HBM if isinstance(out, pl.MemoryRef) else VMEM, outs),
        scratch_shapes=list(scratch),
        compiler_params=pltpu.CompilerParams(vmem_limit_bytes=limit * MB),
        cost_estimate=pl.CostEstimate(flops=flops, bytes_accessed=moved, transcendentals=0),
    )


def shape(dims, dtype):
    return jax.ShapeDtypeStruct(dims, dtype)


def dot(a, b):
    return jnp.dot(a, b, preferred_element_type=f32)


def arrange(value):
    size = value.shape[1]
    pairs = value.reshape(value.shape[0] // 16, 2, 8, size)
    even, odd = pairs[:, 0], pairs[:, 1]
    upper = lax.broadcasted_iota(jnp.int32, even.shape, 1) < FR
    low = jnp.where(upper, even, pltpu.roll(odd, FR, 1))
    high = jnp.where(upper, pltpu.roll(even, FR, 1), odd)
    blocks = (value.shape[0] // (PAIR * ROWS), ROWS, size)
    return low.reshape(blocks), high.reshape(blocks)


def build_keep(start, width, keep):
    position = lax.broadcasted_iota(jnp.int32, (LEN, LANES), 0)
    for u in range(start.shape[1]):
        inside = None
        for m in range(start.shape[0]):
            s = start[m : m + 1, u : u + 1]
            here = (position >= s) & (position < s + width[m : m + 1, u : u + 1])
            inside = here if inside is None else inside | here
        keep[pl.ds(u * LEN, LEN), :] = jnp.where(inside, 0.0, 1.0).astype(bf16)


def apply_mask(source, target, keep, q):
    rows = pl.ds(q * (source.shape[0] // CHUNKS), source.shape[0] // CHUNKS)
    for j in range(GT):
        view = (rows, pl.ds(j * LANES, LANES))
        target[view] = source[view] * keep[rows, :]


def fetch(source, target, sems):
    rows = source.shape[0] // CHUNKS
    return [
        pltpu.make_async_copy(source.at[pl.ds(q * rows, rows)], target.at[pl.ds(q * rows, rows)], sems.at[q])
        for q in range(CHUNKS)
    ]


def fetch_picked(pick, xk, xv, target, sems):
    @pl.when(pick == 0)
    def _():
        for copy in fetch(xk, target, sems):
            copy.start()

    @pl.when(pick != 0)
    def _():
        for copy in fetch(xv, target, sems):
            copy.start()

    return fetch(xk, target, sems)


BLOCK = 256


def put(out, r, value, begin):
    places = pl.ds(r * (BLOCK // BLK), BLOCK // BLK)
    for half, rows in enumerate(arrange(value)):
        for j in range(value.shape[1] // LANES):
            out[places, half, pl.ds(begin + j * ROWS, ROWS), :] = rows[:, :, j * LANES : (j + 1) * LANES].astype(bf16)


def put_folded(out, r, value, begin):
    places = pl.ds(r * (BLOCK // BLK), BLOCK // BLK)
    for half, rows in enumerate(arrange(value)):
        upper, lower = rows[:, : ROWS // 2], pltpu.roll(rows[:, ROWS // 2 :], LANES // 2, 2)
        lane = lax.broadcasted_iota(jnp.int32, upper.shape, 2)
        out[places, half, pl.ds(begin, ROWS // 2), :] = jnp.where(lane < LANES // 2, upper, lower).astype(bf16)


def circulate(value, r):
    rows = []
    for b in range(BLOCK // BLK):
        shift = (D - BLK * (r * (BLOCK // BLK) + b)) % D
        piece = value[b * BLK : (b + 1) * BLK]
        rows.append(pltpu.roll(piece, shift, 1) if shift else piece)
    return [jnp.concatenate([p[:, t * LANES : (t + 1) * LANES] for p in rows], axis=0) for t in range(3)]


def grams(pick, x0, x1, ready, out):
    lefts, rests = [], []
    for r in range(D // BLOCK):
        lefts.append(x0[:, pl.ds(r * BLOCK, BLOCK)].T)
        tiles = circulate(dot(lefts[r], x0[...]), r)
        put(out, r, jnp.where(pick == 0, tiles[0], tiles[1]), F0)
        rests.append(pltpu.roll(jnp.where(pick == 0, tiles[1], tiles[2]), BLK, 1))
    ready()
    for r in range(D // BLOCK):
        put(out, r, dot(lefts[r], x1[...]), 0)
    for r in range(D // BLOCK):
        left = x1[:, pl.ds(r * BLOCK, BLOCK)].T
        tiles = circulate(dot(left, x1[...]), r)
        put(out, r, jnp.concatenate(tiles[:2], axis=1), FA)
        lane = lax.broadcasted_iota(jnp.int32, tiles[2].shape, 1)
        put_folded(out, r, jnp.where(lane < BLK, tiles[2], rests[r]), FL)


def theirs_kernel(core, start, width, x0, xk, xv, out, kept, keep, buf0, buf1, masks, sem0, sem1, sem2):
    pick = 1 - core[0]
    small = [pltpu.make_async_copy(v, masks.at[i], sem2.at[i]) for i, v in enumerate((start, width))]
    copies0 = fetch(x0, buf0, sem0)
    for copy in small + copies0:
        copy.start()
    copies1 = fetch_picked(pick, xk, xv, buf1, sem1)
    for copy in small:
        copy.wait()
    build_keep(masks.at[0], masks.at[1], keep)
    for q in range(CHUNKS):
        copies0[q].wait()
        apply_mask(buf0, kept, keep, q)

    def ready():
        for q in range(CHUNKS):
            copies1[q].wait()
            apply_mask(buf1, buf1, keep, q)

    grams(pick, kept, buf1, ready, out)


def mine_kernel(core, keep, x0, xk, xv, out, buf1, sem1):
    pick = core[0]
    copies1 = fetch_picked(pick, xk, xv, buf1, sem1)

    def ready():
        for q in range(CHUNKS):
            copies1[q].wait()
            apply_mask(buf1, buf1, keep, q)

    grams(pick, x0, buf1, ready, out)


PIECES = 4


def add_kernel(mine, received, out, buf, sems):
    size = NXY // PIECES
    copies = []
    for q in range(PIECES):
        for i in range(q * size, (q + 1) * size):
            for j in range(PAIR):
                buf[i, j] = mine[i, j] + received[i, j]
        part = pl.ds(q * size, size)
        copies.append(pltpu.make_async_copy(buf.at[part], out.at[part], sems.at[q]))
        copies[q].start()
    for copy in copies:
        copy.wait()


def lam_kernel(share, core, keep, x0, xk, xv, bases, keep_lam, send_lam, basis_in_t, mirror, b0, b1, b2, sem0, sem1, sem2):
    c = core[0]
    bufs = (b0, b1, b2)
    copies = [fetch(x, buf, sem) for x, buf, sem in zip((x0, xk, xv), bufs, (sem0, sem1, sem2))]
    for group in copies:
        for copy in group:
            copy.start()
    low, high = arrange(bases[0].astype(f32))
    basis_in_t[...] = jnp.concatenate([low, high], axis=1).reshape(D, D).T.astype(bf16)
    lane = lax.broadcasted_iota(jnp.int32, (LANES, D), 0)
    column = lax.broadcasted_iota(jnp.int32, (LANES, D), 1)
    for half in range(PAIR):
        home = (D - BLK * (lane >> 4) + 8 * ((lane >> 2) & 3) + FR * half + (lane & 3)) & (D - 1)
        mirror[half] = jnp.where(column == home, 1.0, 0.0).astype(bf16)
    lam = []
    for f in range(3):
        total = jnp.zeros((8, D), f32)
        for q in range(CHUNKS):
            copies[f][q].wait()
            apply_mask(bufs[f], bufs[f], keep, q)
        for q in range(bufs[f].shape[0] // BLOCK):
            product = dot(bufs[f][pl.ds(q * BLOCK, BLOCK), :], bases[f])
            total = total + jnp.sum((product * product).reshape(BLOCK // 8, 8, D), axis=0)
        lam.append(jnp.sum(total, axis=0, keepdims=True) * share)
    keep_lam[0:1, :] = lam[0]
    send_lam[0:1, :] = lam[0]
    keep_lam[1:2, :] = jnp.where(c == 0, lam[1], lam[2])
    send_lam[1:2, :] = jnp.where(c == 0, lam[2], lam[1])


def split(value):
    high = value.astype(bf16)
    return high.astype(f32), value - high.astype(f32)


def lam_rows(lam):
    return jnp.concatenate(split(jnp.concatenate([lam[:, j * LANES : (j + 1) * LANES] for j in range(GT)], axis=0)), axis=0)


def add_lam(rows):
    return rows[: 2 * GT] + rows[2 * GT :]


def lam_row(total, index):
    return jnp.concatenate([total[2 * j + index : 2 * j + index + 1] for j in range(GT)], axis=1)


LAMR = 4 * GT
DIRECT = GT * ROWS
TURNED = DIRECT + 4 * FR
DEEP_LAM = TURNED + 16
DEEP_ROWS = DEEP_LAM + LAMR
GATHER_LAM = GT * ROWS
GATHER_TURNED = GATHER_LAM + LAMR
GATHER_ROWS = GATHER_TURNED + 8


def pack_kernel(parts, keep_lam, send_lam, out):
    total = parts[0].astype(f32)
    for i in range(1, WIDE):
        total = total + parts[i].astype(f32)
    lam = lam_rows(keep_lam[...] + send_lam[...]).astype(bf16)
    for j in range(GT):
        tile = total[j * ROWS : (j + 1) * ROWS].astype(bf16)
        for k in range(DEEP):
            out[k, pl.ds(j * ROWS, ROWS), :] = tile
    near, mid, zero = total[FA : FA + ROWS], total[FA + ROWS : F0], total[F0:FL]
    last = total[FL:]
    last = jnp.concatenate([last, pltpu.roll(last, LANES // 2, 1)], axis=0)
    empty = jnp.zeros((LANES - ROWS, LANES), f32)
    turned = [jnp.concatenate([v, empty], axis=0).T for v in (near, mid, zero)]
    for k in range(DEEP):
        rows = slice(k * FR, (k + 1) * FR)
        direct = jnp.concatenate([v[rows] for v in (near, mid, zero, last)], axis=0)
        out[k, pl.ds(DIRECT, 4 * FR), :] = direct.astype(bf16)

        def pieces(sources):
            result = None
            for n in range(4 * len(sources)):
                piece = sources[n // 4][(n % 4) * BLK + 8 * k : (n % 4) * BLK + 8 * k + 8]
                piece = pltpu.roll(piece, ROWS * n, 1) if n else piece
                result = piece if result is None else result + piece
            return result

        mirrored = jnp.concatenate([pieces(turned[:2]), pieces(turned[2:])], axis=0)
        out[k, pl.ds(TURNED, 16), :] = mirrored.astype(bf16)
        out[k, pl.ds(DEEP_LAM, LAMR), :] = lam


def deep_total(got):
    total = got[0].astype(f32)
    for i in range(1, DEEP):
        total = total + got[i].astype(f32)
    return total, jnp.concatenate([total[j * ROWS : (j + 1) * ROWS] for j in range(GT)], axis=1)


def rotate_kernel(got, basis, out):
    total, grad = deep_total(got)
    rot = dot(grad.astype(bf16), basis[...]).astype(bf16)
    lam = add_lam(total[DEEP_LAM:])
    lam = jnp.concatenate(split(lam), axis=0).astype(bf16)
    picked, zero = total[TURNED : TURNED + 8], total[TURNED + 8 : TURNED + 16]
    for half in range(PAIR):
        rows = slice(half * FR, (half + 1) * FR)
        mirrored = jnp.concatenate([picked[rows], zero[rows]], axis=0).astype(bf16)
        for i in range(half, WIDE, PAIR):
            out[i, pl.ds(GATHER_LAM, LAMR), :] = lam
            out[i, pl.ds(GATHER_TURNED, 8), :] = mirrored
    for j in range(GT):
        tile = rot[:, j * LANES : (j + 1) * LANES]
        for i in range(WIDE):
            out[i, pl.ds(j * ROWS, ROWS), :] = tile


def rows_kernel(place, got, out):
    total, grad = deep_total(got)
    k, c = place[0], place[1]
    rows = grad[0:FR]
    for other in range(1, DEEP):
        rows = jnp.where(k == other, grad[other * FR : (other + 1) * FR], rows)
    near, mid, zero, last = [total[DIRECT + t * FR : DIRECT + (t + 1) * FR] for t in range(4)]
    lane = lax.broadcasted_iota(jnp.int32, last.shape, 1)
    none = jnp.zeros_like(last)
    end = jnp.where(lane < BLK, last, none)
    end0 = jnp.where(lane < BLK, pltpu.roll(last, LANES - BLK, 1), none)
    picked = jnp.concatenate([near, mid, end, none], axis=1)
    zero = jnp.where(
        c == 0,
        jnp.concatenate([zero, none, none, none], axis=1),
        jnp.concatenate([none, zero, end0, none], axis=1),
    )
    out[...] = jnp.concatenate([rows, picked, zero, jnp.zeros_like(rows)], axis=0)


def mirrored_rows(place, got, mirror):
    c, block = place[1], place[2]
    row = lax.broadcasted_iota(jnp.int32, (8, LANES), 0)
    group = (lax.broadcasted_iota(jnp.int32, (8, LANES), 1) >> 4) + jnp.where(row >= FR, 4 * c, 0)
    placed = None
    for half in range(PAIR):
        own = jnp.zeros((8, LANES), f32)
        for i in range(NXY):
            distance = (block - i) & (NXY - 1)
            wanted = jnp.where((distance >= 1) & (distance < 8), distance, -1)
            piece = got[PAIR * i + half, pl.ds(GATHER_TURNED, 8), :].astype(f32)
            own = jnp.where(group == wanted, piece, own)
        value = dot(own.astype(bf16), mirror[half])
        placed = value if placed is None else placed + value
    moved = jnp.concatenate([placed[:, LANES:], placed[:, :LANES]], axis=1)
    row = lax.broadcasted_iota(jnp.int32, (8, D), 0)
    return jnp.where((row >= FR) & (c != 0), moved, placed)


def solve_kernel(place, got, basis_in_t, basis_out, rows_in, mirror, rows, own, their, scaled):
    lam = got[0, pl.ds(GATHER_LAM, LAMR), :].astype(f32)
    for i in range(1, WIDE):
        lam = lam + got[i, pl.ds(GATHER_LAM, LAMR), :].astype(f32)
    lam = add_lam(lam)
    column = jnp.broadcast_to(lam_row(lam, 0), (8, D)).T[:, 0:1]
    column = jnp.broadcast_to(column, (D, LANES))
    curve = jnp.zeros((8, LANES), f32)
    for j in range(GT):
        rot = got[:, pl.ds(j * ROWS, ROWS), :].reshape(D, LANES)
        rotated = dot(basis_in_t[...], rot)
        low = (rotated / (column * lam[2 * j + 1 : 2 * j + 2] + damping)).astype(bf16)
        scaled[:, pl.ds(j * LANES, LANES)] = low
        curve = curve + jnp.sum((low.astype(f32) * rotated).reshape(D // 8, 8, LANES), axis=0)
    curve = jnp.sum(jnp.sum(curve, axis=1, keepdims=True), axis=0, keepdims=True)
    back = dot(rows_in[...], scaled[...]).astype(bf16)
    prec = lax.dot_general(back, basis_out[...], (((1,), (1,)), ((), ())), preferred_element_type=f32)
    prec = prec.astype(bf16).astype(f32)
    curve = jnp.broadcast_to(curve, (2, D))
    factors = pltpu.roll(rows[4:12, :] + mirrored_rows(place, got, mirror), BLK * place[2], 1)
    low = jnp.concatenate([rows[0:2, :], factors[0:2], factors[4:6]], axis=0)
    high = jnp.concatenate([rows[2:4, :], factors[2:4], factors[6:8]], axis=0)
    first = place[1] == 0
    pad = jnp.zeros((6, D), f32)
    own[...] = jnp.concatenate([prec[0:2], curve, jnp.where(first, low, high), pad], axis=0)
    their[...] = jnp.concatenate([prec[2:4], curve, jnp.where(first, high, low), pad], axis=0)


def finish_kernel(scale, core, own, got, old, new_factors, gradients, updates):
    first = core[0] == 0
    curve = own[2:3, :] + got[2:3, :]
    factor = jnp.sqrt(kl_clip / (learn_rate * learn_rate * curve))
    side0 = jnp.where(first, own[...], got[...])
    side1 = jnp.where(first, got[...], own[...])
    updates[0] = (side0[0:2] * factor).astype(bf16)
    updates[1] = (side1[0:2] * factor).astype(bf16)
    gradients[:, 0, :] = side0[4:6]
    gradients[:, 1, :] = side1[4:6]
    batch = (side0[8:10] + side1[8:10], side0[6:8], side1[6:8])
    for f in range(3):
        new_factors[f] = decay * old[f] + scale * batch[f]


def exchange(value, groups):
    return lax.all_to_all(value, "dp", 0, 0, axis_index_groups=groups, tiled=True)


def body(activations, grad_key, grad_value, time_start, time_width, bases, old_factors):
    index = lax.axis_index("dp").astype(jnp.int32)
    core = index % NC
    first = core == 0
    z = (index // NC) % NZ
    place = jnp.stack([z // PAIR, core, index // (NC * NZ)])
    tokens_here = activations.shape[0]
    share = (1.0 - decay) / (tokens_here * lax.axis_size("dp"))

    def in_hbm(value):
        return pltpu.with_memory_space_constraint(value, pltpu.HBM)

    masks = (in_hbm(time_start.T), in_hbm(time_width.T))
    frames, keys, vals = in_hbm(activations), in_hbm(grad_key), in_hbm(grad_value)
    mask_buf = pltpu.VMEM((2,) + time_start.shape[::-1], jnp.int32)
    buf = pltpu.VMEM((tokens_here, D), bf16)
    sems = pltpu.SemaphoreType.DMA((CHUNKS,))
    pair = pltpu.SemaphoreType.DMA((2,))
    partial = shape((NXY, PAIR, WROWS, LANES), bf16)
    work = 6 * D * D * tokens_here
    with jax.named_scope("grams_theirs"):
        other, kept, keep = call(
            theirs_kernel,
            (partial, shape((tokens_here, D), bf16), shape((tokens_here, LANES), bf16)),
            [SMEM] + [HBM] * 5,
            [buf, buf, mask_buf, sems, sems, pair],
            flops=work,
            moved=4 * MB,
        )(core[None], *masks, frames, keys, vals)
    received = lax.ppermute(other, "dp", SWAP)
    with jax.named_scope("grams_mine"):
        mine = call(
            mine_kernel,
            partial,
            [SMEM, VMEM, VMEM, HBM, HBM],
            [buf, sems],
            flops=work,
            moved=4 * MB,
        )(core[None], keep, kept, keys, vals)
    with jax.named_scope("chip_sum"):
        chip = call(
            add_kernel,
            pltpu.HBM(partial.shape, bf16),
            [VMEM] * 2,
            [pltpu.VMEM(partial.shape, bf16), pltpu.SemaphoreType.DMA((PIECES,))],
        )(mine, received).reshape(WIDE, WROWS, LANES)
    with jax.named_scope("wide_sum"):
        parts = exchange(chip, WIDE_GROUPS)

    lam_shape = shape((2, D), f32)
    with jax.named_scope("lam"):
        keep_lam, send_lam, basis_in_t, mirror = call(
            functools.partial(lam_kernel, share),
            (lam_shape, lam_shape, shape((D, D), bf16), shape((PAIR, LANES, D), bf16)),
            [SMEM, VMEM, HBM, HBM, HBM, VMEM],
            [buf] * 3 + [sems] * 3,
            flops=work,
            moved=4 * MB,
        )(core[None], keep, frames, keys, vals, bases)
    old_lam = []
    my_rows = lax.dynamic_slice_in_dim(bases, 2 * index, 2, 1).astype(f32)
    for f in range(3):
        old_image = jnp.dot(old_factors[:, f, :], bases[f].astype(f32), precision=lax.Precision.HIGHEST)
        old_lam.append(decay * jnp.sum(my_rows[f] * old_image, axis=0))
    keep_lam = keep_lam + jnp.stack([old_lam[0], jnp.where(first, old_lam[1], old_lam[2])])
    send_lam = send_lam + jnp.stack([old_lam[0], jnp.where(first, old_lam[2], old_lam[1])])
    sent_lam = lax.ppermute(send_lam, "dp", SWAP)

    with jax.named_scope("pack"):
        packed = call(pack_kernel, shape((DEEP, DEEP_ROWS, LANES), bf16), [VMEM] * 3)(parts, keep_lam, sent_lam)
    with jax.named_scope("deep_sum"):
        got = exchange(packed, DEEP_GROUPS)
    basis_out = lax.dynamic_index_in_dim(bases, 1 + core, 0, keepdims=False)
    lines = shape((16, D), f32)
    with jax.named_scope("rotate"):
        spread = call(rotate_kernel, shape((WIDE, GATHER_ROWS, LANES), bf16), [VMEM] * 2)(got, basis_out)
    with jax.named_scope("gather"):
        gathered = exchange(spread, WIDE_GROUPS)
    with jax.named_scope("rows"):
        rows = call(rows_kernel, lines, [SMEM, VMEM])(place, got)
    rows_in = lax.dynamic_slice_in_dim(bases[0], (index // NC) * FR, FR, 0)
    rows_in = jnp.where(first, rows_in, jnp.roll(rows_in, 2, axis=0))
    rows_in = jnp.pad(rows_in, ((0, 16 - FR), (0, 0)))
    with jax.named_scope("solve"):
        own, their = call(solve_kernel, (lines, lines), [SMEM] + [VMEM] * 6, [pltpu.VMEM((D, D), bf16)])(
            place, gathered, basis_in_t, basis_out, rows_in, mirror, rows
        )
    theirs = lax.ppermute(their, "dp", SWAP)
    with jax.named_scope("finish"):
        new_factors, gradients, updates = call(
            functools.partial(finish_kernel, share),
            (shape((3, 2, D), f32), shape((2, 2, D), f32), shape((2, 2, D), bf16)),
            [SMEM] + [VMEM] * 3,
        )(core[None], own, theirs, jnp.transpose(old_factors, (1, 0, 2)))
    return (jnp.transpose(new_factors, (1, 0, 2)), gradients, updates)


def solution(mesh):
    in_specs = (
        P("dp", None),
        P("dp", None),
        P("dp", None),
        P("dp", None),
        P("dp", None),
        P(),
        P("dp", None, None),
    )
    out_specs = (P("dp", None, None), P("dp", None, None), P(None, "dp", None))
    return jax.shard_map(body, mesh=mesh, in_specs=in_specs, out_specs=out_specs, check_vma=False)
```

```python
import functools

import jax
import jax.numpy as jnp
from jax import lax
from jax.experimental import pallas as pl
from jax.experimental.pallas import tpu as pltpu
from jax.sharding import PartitionSpec as P

LEN = 128
NX, NY, NZ, NC = 4, 4, 8, 2
NXY = NX * NY
D = 512
HALF = D // 2
PAIR = 2
WIDE = NXY * PAIR
DEEP = NZ // PAIR
ROWS = D // WIDE
LANES = 128
FR = ROWS // DEEP
GT = D // LANES
BLK = D // NXY
FA, F0, FL = GT * ROWS, (GT + 2) * ROWS, (GT + 3) * ROWS
WROWS = FL + ROWS // 2
MB = 1 << 20

decay = 0.8
damping = 0.001
kl_clip = 0.001
learn_rate = 7e-05

f32, bf16 = jnp.float32, jnp.bfloat16


def device(xy, z, c):
    return (xy * NZ + z) * NC + c


SWAP = [(d, d ^ 1) for d in range(NXY * NZ * NC)]
WIDE_GROUPS = [
    [device(i, k * PAIR + l, c) for i in range(NXY) for l in range(PAIR)]
    for k in range(DEEP)
    for c in range(NC)
]
DEEP_GROUPS = [
    [device(i, k * PAIR + l, c) for k in range(DEEP)] for i in range(NXY) for l in range(PAIR) for c in range(NC)
]
VMEM = pl.BlockSpec(memory_space=pltpu.VMEM)
SMEM = pl.BlockSpec(memory_space=pltpu.SMEM)
HBM = pl.BlockSpec(memory_space=pltpu.HBM)
CHUNKS = 2


def call(kernel, outs, in_specs, scratch=(), limit=16, flops=0, moved=0):
    return pl.pallas_call(
        kernel,
        out_shape=outs,
        in_specs=in_specs,
        out_specs=jax.tree.map(lambda out: HBM if isinstance(out, pl.MemoryRef) else VMEM, outs),
        scratch_shapes=list(scratch),
        compiler_params=pltpu.CompilerParams(vmem_limit_bytes=limit * MB),
        cost_estimate=pl.CostEstimate(flops=flops, bytes_accessed=moved, transcendentals=0),
    )


def shape(dims, dtype):
    return jax.ShapeDtypeStruct(dims, dtype)


def dot(a, b):
    return jnp.dot(a, b, preferred_element_type=f32)


def arrange(value):
    size = value.shape[1]
    pairs = value.reshape(value.shape[0] // 16, 2, 8, size)
    even, odd = pairs[:, 0], pairs[:, 1]
    upper = lax.broadcasted_iota(jnp.int32, even.shape, 1) < FR
    low = jnp.where(upper, even, pltpu.roll(odd, FR, 1))
    high = jnp.where(upper, pltpu.roll(even, FR, 1), odd)
    blocks = (value.shape[0] // (PAIR * ROWS), ROWS, size)
    return low.reshape(blocks), high.reshape(blocks)


def build_keep(start, width, keep):
    position = lax.broadcasted_iota(jnp.int32, (LEN, LANES), 0)
    for u in range(start.shape[1]):
        inside = None
        for m in range(start.shape[0]):
            s = start[m : m + 1, u : u + 1]
            here = (position >= s) & (position < s + width[m : m + 1, u : u + 1])
            inside = here if inside is None else inside | here
        keep[pl.ds(u * LEN, LEN), :] = jnp.where(inside, 0.0, 1.0).astype(bf16)


def apply_mask(source, target, keep, q):
    rows = pl.ds(q * (source.shape[0] // CHUNKS), source.shape[0] // CHUNKS)
    for j in range(GT):
        view = (rows, pl.ds(j * LANES, LANES))
        target[view] = source[view] * keep[rows, :]


def fetch(source, target, sems):
    rows = source.shape[0] // CHUNKS
    return [
        pltpu.make_async_copy(source.at[pl.ds(q * rows, rows)], target.at[pl.ds(q * rows, rows)], sems.at[q])
        for q in range(CHUNKS)
    ]


def fetch_picked(pick, xk, xv, target, sems):
    @pl.when(pick == 0)
    def _():
        for copy in fetch(xk, target, sems):
            copy.start()

    @pl.when(pick != 0)
    def _():
        for copy in fetch(xv, target, sems):
            copy.start()

    return fetch(xk, target, sems)


BLOCK = 256


def put(out, r, value, begin):
    places = pl.ds(r * (BLOCK // BLK), BLOCK // BLK)
    for half, rows in enumerate(arrange(value)):
        for j in range(value.shape[1] // LANES):
            out[places, half, pl.ds(begin + j * ROWS, ROWS), :] = rows[:, :, j * LANES : (j + 1) * LANES].astype(bf16)


def put_folded(out, r, value, begin):
    places = pl.ds(r * (BLOCK // BLK), BLOCK // BLK)
    for half, rows in enumerate(arrange(value)):
        upper, lower = rows[:, : ROWS // 2], pltpu.roll(rows[:, ROWS // 2 :], LANES // 2, 2)
        lane = lax.broadcasted_iota(jnp.int32, upper.shape, 2)
        out[places, half, pl.ds(begin, ROWS // 2), :] = jnp.where(lane < LANES // 2, upper, lower).astype(bf16)


def end_lanes(value):
    lane = lax.broadcasted_iota(jnp.int32, value.shape, 1)
    return jnp.where(lane < BLK, value, 0.0)


def circulate(value, r):
    rows = []
    for b in range(BLOCK // BLK):
        shift = (D - BLK * (r * (BLOCK // BLK) + b)) % D
        piece = value[b * BLK : (b + 1) * BLK]
        rows.append(pltpu.roll(piece, shift, 1) if shift else piece)
    return [jnp.concatenate([p[:, t * LANES : (t + 1) * LANES] for p in rows], axis=0) for t in range(3)]


def zero_grams(pick, x0, out, spare):
    lefts, rests = [], []
    for r in range(D // BLOCK):
        lefts.append(x0[:, pl.ds(r * BLOCK, BLOCK)].T)
        tiles = circulate(dot(lefts[r], x0[...]), r)
        put(out, r, jnp.where(pick == 0, tiles[0], tiles[1]), F0)
        put(spare, r, jnp.where(pick == 0, tiles[1], tiles[0]), 0)
        last = pltpu.roll(end_lanes(tiles[2]), BLK, 1)
        rests.append(jnp.where(pick == 0, 0.0, last))
        put_folded(spare, r, jnp.where(pick == 0, last, 0.0), ROWS)
    return lefts, rests


def picked_grams(lefts, x1, rests, out, end):
    for r in range(D // BLOCK):
        put(out, r, dot(lefts[r], x1[...]), 0)
    for r in range(D // BLOCK):
        left = x1[:, pl.ds(r * BLOCK, BLOCK)].T
        tiles = circulate(dot(left, x1[...]), r)
        put(out, r, jnp.concatenate(tiles[:2], axis=1), FA)
        last = end_lanes(tiles[2])
        put_folded(out, r, last if rests is None else last + rests[r], end)


def theirs_kernel(core, start, width, x0, xk, xv, out, spare, kept, keep, buf0, buf1, masks, sem0, sem1, sem2):
    pick = 1 - core[0]
    small = [pltpu.make_async_copy(v, masks.at[i], sem2.at[i]) for i, v in enumerate((start, width))]
    copies0 = fetch(x0, buf0, sem0)
    for copy in small + copies0:
        copy.start()
    copies1 = fetch_picked(pick, xk, xv, buf1, sem1)
    for copy in small:
        copy.wait()
    build_keep(masks.at[0], masks.at[1], keep)
    for q in range(CHUNKS):
        copies0[q].wait()
        apply_mask(buf0, kept, keep, q)
    lefts, rests = zero_grams(pick, kept, out, spare)
    for q in range(CHUNKS):
        copies1[q].wait()
        apply_mask(buf1, buf1, keep, q)
    picked_grams(lefts, buf1, rests, out, FL)


def mine_kernel(core, keep, x0, xk, xv, out, buf1, sem1):
    pick = core[0]
    copies1 = fetch_picked(pick, xk, xv, buf1, sem1)
    lefts = [x0[:, pl.ds(r * BLOCK, BLOCK)].T for r in range(D // BLOCK)]
    for q in range(CHUNKS):
        copies1[q].wait()
        apply_mask(buf1, buf1, keep, q)
    picked_grams(lefts, buf1, None, out, F0)


PIECES = 4


def add_kernel(mine, spare, received, out, buf, sems):
    size = NXY // PIECES
    copies = []
    main, zero, last = slice(0, F0), slice(F0, FL), slice(FL, WROWS)
    for q in range(PIECES):
        for i in range(q * size, (q + 1) * size):
            for j in range(PAIR):
                buf[i, j, main] = mine[i, j, main] + received[i, j, main]
                buf[i, j, zero] = spare[i, j, :ROWS] + received[i, j, zero]
                ends = mine[i, j, F0:] + spare[i, j, ROWS:]
                buf[i, j, last] = ends + received[i, j, last]
        part = pl.ds(q * size, size)
        copies.append(pltpu.make_async_copy(buf.at[part], out.at[part], sems.at[q]))
        copies[q].start()
    for copy in copies:
        copy.wait()


def lam_kernel(share, place, keep, x0, xk, xv, bases, keep_lam, send_lam, basis_in_t, mirror, b0, b1, b2, sem0, sem1, sem2):
    c = place[1]
    bufs = (b0, b1, b2)
    copies = [fetch(x, buf, sem) for x, buf, sem in zip((x0, xk, xv), bufs, (sem0, sem1, sem2))]
    for group in copies:
        for copy in group:
            copy.start()
    low, high = arrange(bases[0].astype(f32))
    basis_in_t[...] = jnp.concatenate([low, high], axis=1).reshape(D, D).T.astype(bf16)
    lane = lax.broadcasted_iota(jnp.int32, (LANES, D), 0)
    column = lax.broadcasted_iota(jnp.int32, (LANES, D), 1)
    for half in range(PAIR):
        home = 8 * ((lane >> 2) & 3) + FR * half + (lane & 3) + 2 * D
        for kind in range(2):
            distance = (lane >> 4) + (4 * c if kind else 0)
            there = (home + BLK * (place[2] - distance)) & (D - 1)
            one = jnp.where(column == there, 1.0, 0.0).astype(bf16)
            mirror[pl.ds((2 * half + kind) * LANES, LANES), :] = one
    lam = []
    for f in range(3):
        total = jnp.zeros((8, D), f32)
        for q in range(CHUNKS):
            copies[f][q].wait()
            apply_mask(bufs[f], bufs[f], keep, q)
        for q in range(bufs[f].shape[0] // BLOCK):
            product = dot(bufs[f][pl.ds(q * BLOCK, BLOCK), :], bases[f])
            total = total + jnp.sum((product * product).reshape(BLOCK // 8, 8, D), axis=0)
        lam.append(jnp.sum(total, axis=0, keepdims=True) * share)
    keep_lam[0:1, :] = lam[0]
    send_lam[0:1, :] = lam[0]
    keep_lam[1:2, :] = jnp.where(c == 0, lam[1], lam[2])
    send_lam[1:2, :] = jnp.where(c == 0, lam[2], lam[1])


def split(value):
    high = value.astype(bf16)
    return high.astype(f32), value - high.astype(f32)


def lam_rows(lam):
    return jnp.concatenate(split(jnp.concatenate([lam[:, j * LANES : (j + 1) * LANES] for j in range(GT)], axis=0)), axis=0)


def add_lam(rows):
    return rows[: 2 * GT] + rows[2 * GT :]


def lam_row(total, index):
    return jnp.concatenate([total[2 * j + index : 2 * j + index + 1] for j in range(GT)], axis=1)


LAMR = 4 * GT
DIRECT = GT * ROWS
TURNED = DIRECT + 4 * FR
DEEP_LAM = TURNED + 16
DEEP_ROWS = DEEP_LAM + LAMR
GATHER_LAM = GT * ROWS
GATHER_TURNED = GATHER_LAM + 2 * GT
GATHER_ROWS = GATHER_TURNED + 8


def pack_kernel(parts, keep_lam, send_lam, out):
    total = parts[0].astype(f32)
    for i in range(1, WIDE):
        total = total + parts[i].astype(f32)
    lam = lam_rows(keep_lam[...] + send_lam[...]).astype(bf16)
    for j in range(GT):
        tile = total[j * ROWS : (j + 1) * ROWS].astype(bf16)
        for k in range(DEEP):
            out[k, pl.ds(j * ROWS, ROWS), :] = tile
    near, mid, zero = total[FA : FA + ROWS], total[FA + ROWS : F0], total[F0:FL]
    last = total[FL:]
    last = jnp.concatenate([last, pltpu.roll(last, LANES // 2, 1)], axis=0)
    empty = jnp.zeros((LANES - ROWS, LANES), f32)
    turned = [jnp.concatenate([v, empty], axis=0).T for v in (near, mid, zero)]
    for k in range(DEEP):
        rows = slice(k * FR, (k + 1) * FR)
        direct = jnp.concatenate([v[rows] for v in (near, mid, zero, last)], axis=0)
        out[k, pl.ds(DIRECT, 4 * FR), :] = direct.astype(bf16)

        def pieces(sources):
            result = None
            for n in range(4 * len(sources)):
                piece = sources[n // 4][(n % 4) * BLK + 8 * k : (n % 4) * BLK + 8 * k + 8]
                piece = pltpu.roll(piece, ROWS * n, 1) if n else piece
                result = piece if result is None else result + piece
            return result

        mirrored = jnp.concatenate([pieces(turned[:2]), pieces(turned[2:])], axis=0)
        out[k, pl.ds(TURNED, 16), :] = mirrored.astype(bf16)
        out[k, pl.ds(DEEP_LAM, LAMR), :] = lam


def deep_total(got):
    total = got[0].astype(f32)
    for i in range(1, DEEP):
        total = total + got[i].astype(f32)
    return total, jnp.concatenate([total[j * ROWS : (j + 1) * ROWS] for j in range(GT)], axis=1)


def rotate_kernel(got, basis, out):
    total, grad = deep_total(got)
    rot = dot(grad.astype(bf16), basis[...]).astype(bf16)
    lam = add_lam(total[DEEP_LAM:])
    picked, zero = total[TURNED : TURNED + 8], total[TURNED + 8 : TURNED + 16]
    for half in range(PAIR):
        rows = slice(half * FR, (half + 1) * FR)
        tail = jnp.concatenate([lam, picked[rows], zero[rows]], axis=0).astype(bf16)
        for i in range(half, WIDE, PAIR):
            out[i, pl.ds(GATHER_LAM, ROWS), :] = tail
    for j in range(GT):
        tile = rot[:, j * LANES : (j + 1) * LANES]
        for i in range(WIDE):
            out[i, pl.ds(j * ROWS, ROWS), :] = tile


def rows_kernel(place, got, out):
    total, grad = deep_total(got)
    k, c = place[0], place[1]
    rows = grad[0:FR]
    for other in range(1, DEEP):
        rows = jnp.where(k == other, grad[other * FR : (other + 1) * FR], rows)
    near, mid, zero, last = [total[DIRECT + t * FR : DIRECT + (t + 1) * FR] for t in range(4)]
    lane = lax.broadcasted_iota(jnp.int32, last.shape, 1)
    none = jnp.zeros_like(last)
    end = jnp.where(lane < BLK, last, none)
    end0 = jnp.where(lane < BLK, pltpu.roll(last, LANES - BLK, 1), none)
    picked = jnp.concatenate([near, mid, end, none], axis=1)
    zero = jnp.where(
        c == 0,
        jnp.concatenate([zero, none, none, none], axis=1),
        jnp.concatenate([none, zero, end0, none], axis=1),
    )
    factors = pltpu.roll(jnp.concatenate([picked, zero], axis=0), BLK * place[2], 1)
    out[...] = jnp.concatenate([rows, factors, jnp.zeros_like(rows)], axis=0)


def mirrored_rows(place, tails, mirror):
    c, block = place[1], place[2]
    row = lax.broadcasted_iota(jnp.int32, (8, LANES), 0)
    group = (lax.broadcasted_iota(jnp.int32, (8, LANES), 1) >> 4) + jnp.where(row >= FR, 4 * c, 0)
    parts = []
    for half in range(PAIR):
        own = jnp.zeros((8, LANES), f32)
        for i in range(NXY):
            distance = (block - i) & (NXY - 1)
            wanted = jnp.where((distance >= 1) & (distance < 8), distance, -1)
            own = jnp.where(group == wanted, tails[PAIR * i + half][8:], own)
        parts += [jnp.where(row < FR, own, 0.0), jnp.where(row < FR, 0.0, own)]
    return dot(jnp.concatenate(parts, axis=1).astype(bf16), mirror[...])


def solve_kernel(place, got, basis_in_t, basis_out, rows_in, mirror, rows, own, their, scaled):
    tails = [got[i, pl.ds(GATHER_LAM, ROWS), :].astype(f32) for i in range(WIDE)]
    lam = tails[0][:8]
    for tail in tails[1:]:
        lam = lam + tail[:8]
    column = jnp.broadcast_to(lam_row(lam, 0), (8, D)).T[:, 0:1]
    column = jnp.broadcast_to(column, (D, LANES))
    curve = jnp.zeros((8, LANES), f32)
    for j in range(GT):
        rot = got[:, pl.ds(j * ROWS, ROWS), :].reshape(D, LANES)
        rotated = dot(basis_in_t[...], rot)
        low = (rotated / (column * lam[2 * j + 1 : 2 * j + 2] + damping)).astype(bf16)
        scaled[:, pl.ds(j * LANES, LANES)] = low
        curve = curve + jnp.sum((low.astype(f32) * rotated).reshape(D // 8, 8, LANES), axis=0)
    curve = jnp.sum(jnp.sum(curve, axis=1, keepdims=True), axis=0, keepdims=True)
    back = dot(rows_in[...], scaled[...]).astype(bf16)
    prec = lax.dot_general(back, basis_out[...], (((1,), (1,)), ((), ())), preferred_element_type=f32)
    prec = prec.astype(bf16).astype(f32)
    curve = jnp.broadcast_to(curve, (2, D))
    factors = rows[4:12, :] + mirrored_rows(place, tails, mirror)
    low = jnp.concatenate([rows[0:2, :], factors[0:2], factors[4:6]], axis=0)
    high = jnp.concatenate([rows[2:4, :], factors[2:4], factors[6:8]], axis=0)
    first = place[1] == 0
    pad = jnp.zeros((6, D), f32)
    own[...] = jnp.concatenate([prec[0:2], curve, jnp.where(first, low, high), pad], axis=0)
    their[...] = jnp.concatenate([prec[2:4], curve, jnp.where(first, high, low), pad], axis=0)


def finish_kernel(scale, core, own, got, old, new_factors, gradients, updates):
    first = core[0] == 0
    curve = own[2:3, :] + got[2:3, :]
    factor = jnp.sqrt(kl_clip / (learn_rate * learn_rate * curve))
    side0 = jnp.where(first, own[...], got[...])
    side1 = jnp.where(first, got[...], own[...])
    updates[0] = (side0[0:2] * factor).astype(bf16)
    updates[1] = (side1[0:2] * factor).astype(bf16)
    gradients[:, 0, :] = side0[4:6]
    gradients[:, 1, :] = side1[4:6]
    batch = (side0[8:10] + side1[8:10], side0[6:8], side1[6:8])
    for f in range(3):
        new_factors[f] = decay * old[f] + scale * batch[f]


def exchange(value, groups):
    return lax.all_to_all(value, "dp", 0, 0, axis_index_groups=groups, tiled=True)


def body(activations, grad_key, grad_value, time_start, time_width, bases, old_factors):
    index = lax.axis_index("dp").astype(jnp.int32)
    core = index % NC
    first = core == 0
    z = (index // NC) % NZ
    place = jnp.stack([z // PAIR, core, index // (NC * NZ)])
    tokens_here = activations.shape[0]
    share = (1.0 - decay) / (tokens_here * lax.axis_size("dp"))

    def in_hbm(value):
        return pltpu.with_memory_space_constraint(value, pltpu.HBM)

    masks = (in_hbm(time_start.T), in_hbm(time_width.T))
    frames, keys, vals = in_hbm(activations), in_hbm(grad_key), in_hbm(grad_value)
    mask_buf = pltpu.VMEM((2,) + time_start.shape[::-1], jnp.int32)
    buf = pltpu.VMEM((tokens_here, D), bf16)
    sems = pltpu.SemaphoreType.DMA((CHUNKS,))
    pair = pltpu.SemaphoreType.DMA((2,))
    partial = shape((NXY, PAIR, WROWS, LANES), bf16)
    work = 6 * D * D * tokens_here
    with jax.named_scope("grams_theirs"):
        other, spare, kept, keep = call(
            theirs_kernel,
            (partial, shape((NXY, PAIR, ROWS + ROWS // 2, LANES), bf16), shape((tokens_here, D), bf16), shape((tokens_here, LANES), bf16)),
            [SMEM] + [HBM] * 5,
            [buf, buf, mask_buf, sems, sems, pair],
            flops=work,
            moved=4 * MB,
        )(core[None], *masks, frames, keys, vals)
    received = lax.ppermute(other, "dp", SWAP)
    with jax.named_scope("grams_mine"):
        mine = call(
            mine_kernel,
            shape((NXY, PAIR, F0 + ROWS // 2, LANES), bf16),
            [SMEM, VMEM, VMEM, HBM, HBM],
            [buf, sems],
            flops=work,
            moved=4 * MB,
        )(core[None], keep, kept, keys, vals)
    with jax.named_scope("chip_sum"):
        chip = call(
            add_kernel,
            pltpu.HBM(partial.shape, bf16),
            [VMEM] * 3,
            [pltpu.VMEM(partial.shape, bf16), pltpu.SemaphoreType.DMA((PIECES,))],
        )(mine, spare, received).reshape(WIDE, WROWS, LANES)
    with jax.named_scope("wide_sum"):
        parts = exchange(chip, WIDE_GROUPS)

    lam_shape = shape((2, D), f32)
    with jax.named_scope("lam"):
        keep_lam, send_lam, basis_in_t, mirror = call(
            functools.partial(lam_kernel, share),
            (lam_shape, lam_shape, shape((D, D), bf16), shape((2 * PAIR * LANES, D), bf16)),
            [SMEM, VMEM, HBM, HBM, HBM, VMEM],
            [buf] * 3 + [sems] * 3,
            flops=work,
            moved=4 * MB,
        )(place, keep, frames, keys, vals, bases)
    old_lam = []
    my_rows = lax.dynamic_slice_in_dim(bases, 2 * index, 2, 1).astype(f32)
    for f in range(3):
        old_image = jnp.dot(old_factors[:, f, :], bases[f].astype(f32), precision=lax.Precision.HIGHEST)
        old_lam.append(decay * jnp.sum(my_rows[f] * old_image, axis=0))
    keep_lam = keep_lam + jnp.stack([old_lam[0], jnp.where(first, old_lam[1], old_lam[2])])
    send_lam = send_lam + jnp.stack([old_lam[0], jnp.where(first, old_lam[2], old_lam[1])])
    sent_lam = lax.ppermute(send_lam, "dp", SWAP)

    with jax.named_scope("pack"):
        packed = call(pack_kernel, shape((DEEP, DEEP_ROWS, LANES), bf16), [VMEM] * 3)(parts, keep_lam, sent_lam)
    with jax.named_scope("deep_sum"):
        got = exchange(packed, DEEP_GROUPS)
    basis_out = lax.dynamic_index_in_dim(bases, 1 + core, 0, keepdims=False)
    lines = shape((16, D), f32)
    with jax.named_scope("rotate"):
        spread = call(rotate_kernel, shape((WIDE, GATHER_ROWS, LANES), bf16), [VMEM] * 2)(got, basis_out)
    with jax.named_scope("gather"):
        gathered = exchange(spread, WIDE_GROUPS)
    with jax.named_scope("rows"):
        rows = call(rows_kernel, lines, [SMEM, VMEM])(place, got)
    rows_in = lax.dynamic_slice_in_dim(bases[0], (index // NC) * FR, FR, 0)
    rows_in = jnp.where(first, rows_in, jnp.roll(rows_in, 2, axis=0))
    rows_in = jnp.pad(rows_in, ((0, 16 - FR), (0, 0)))
    with jax.named_scope("solve"):
        own, their = call(solve_kernel, (lines, lines), [SMEM] + [VMEM] * 6, [pltpu.VMEM((D, D), bf16)])(
            place, gathered, basis_in_t, basis_out, rows_in, mirror, rows
        )
    theirs = lax.ppermute(their, "dp", SWAP)
    with jax.named_scope("finish"):
        new_factors, gradients, updates = call(
            functools.partial(finish_kernel, share),
            (shape((3, 2, D), f32), shape((2, 2, D), f32), shape((2, 2, D), bf16)),
            [SMEM] + [VMEM] * 3,
        )(core[None], own, theirs, jnp.transpose(old_factors, (1, 0, 2)))
    return (jnp.transpose(new_factors, (1, 0, 2)), gradients, updates)


def solution(mesh):
    in_specs = (
        P("dp", None),
        P("dp", None),
        P("dp", None),
        P("dp", None),
        P("dp", None),
        P(),
        P("dp", None, None),
    )
    out_specs = (P("dp", None, None), P("dp", None, None), P(None, "dp", None))
    return jax.shard_map(body, mesh=mesh, in_specs=in_specs, out_specs=out_specs, check_vma=False)
```

```python
import functools

import jax
import jax.numpy as jnp
from jax import lax
from jax.experimental import pallas as pl
from jax.experimental.pallas import tpu as pltpu
from jax.sharding import PartitionSpec as P

LEN = 128
NX, NY, NZ, NC = 4, 4, 8, 2
NXY = NX * NY
D = 512
HALF = D // 2
PAIR = 2
WIDE = NXY * PAIR
DEEP = NZ // PAIR
ROWS = D // WIDE
LANES = 128
FR = ROWS // DEEP
GT = D // LANES
BLK = D // NXY
FA, F0, FL = GT * ROWS, (GT + 2) * ROWS, (GT + 3) * ROWS
WROWS = FL + ROWS // 2
MB = 1 << 20

decay = 0.8
damping = 0.001
kl_clip = 0.001
learn_rate = 7e-05

f32, bf16 = jnp.float32, jnp.bfloat16


def device(xy, z, c):
    return (xy * NZ + z) * NC + c


SWAP = [(d, d ^ 1) for d in range(NXY * NZ * NC)]
WIDE_GROUPS = [
    [device(i, k * PAIR + l, c) for i in range(NXY) for l in range(PAIR)]
    for k in range(DEEP)
    for c in range(NC)
]
DEEP_GROUPS = [
    [device(i, k * PAIR + l, c) for k in range(DEEP)] for i in range(NXY) for l in range(PAIR) for c in range(NC)
]
VMEM = pl.BlockSpec(memory_space=pltpu.VMEM)
SMEM = pl.BlockSpec(memory_space=pltpu.SMEM)
HBM = pl.BlockSpec(memory_space=pltpu.HBM)
CHUNKS = 2


def call(kernel, outs, in_specs, scratch=(), limit=16, flops=0, moved=0):
    return pl.pallas_call(
        kernel,
        out_shape=outs,
        in_specs=in_specs,
        out_specs=jax.tree.map(lambda out: HBM if isinstance(out, pl.MemoryRef) else VMEM, outs),
        scratch_shapes=list(scratch),
        compiler_params=pltpu.CompilerParams(vmem_limit_bytes=limit * MB),
        cost_estimate=pl.CostEstimate(flops=flops, bytes_accessed=moved, transcendentals=0),
    )


def shape(dims, dtype):
    return jax.ShapeDtypeStruct(dims, dtype)


def dot(a, b):
    return jnp.dot(a, b, preferred_element_type=f32)


def arrange(value):
    size = value.shape[1]
    pairs = value.reshape(value.shape[0] // 16, 2, 8, size)
    even, odd = pairs[:, 0], pairs[:, 1]
    upper = lax.broadcasted_iota(jnp.int32, even.shape, 1) < FR
    low = jnp.where(upper, even, pltpu.roll(odd, FR, 1))
    high = jnp.where(upper, pltpu.roll(even, FR, 1), odd)
    blocks = (value.shape[0] // (PAIR * ROWS), ROWS, size)
    return low.reshape(blocks), high.reshape(blocks)


def build_keep(start, width, keep):
    position = lax.broadcasted_iota(jnp.int32, (LEN, LANES), 0)
    for u in range(start.shape[1]):
        inside = None
        for m in range(start.shape[0]):
            s = start[m : m + 1, u : u + 1]
            here = (position >= s) & (position < s + width[m : m + 1, u : u + 1])
            inside = here if inside is None else inside | here
        keep[pl.ds(u * LEN, LEN), :] = jnp.where(inside, 0.0, 1.0).astype(bf16)


def apply_mask(source, target, keep, q):
    rows = pl.ds(q * (source.shape[0] // CHUNKS), source.shape[0] // CHUNKS)
    for j in range(GT):
        view = (rows, pl.ds(j * LANES, LANES))
        target[view] = source[view] * keep[rows, :]


def fetch(source, target, sems):
    rows = source.shape[0] // CHUNKS
    return [
        pltpu.make_async_copy(source.at[pl.ds(q * rows, rows)], target.at[pl.ds(q * rows, rows)], sems.at[q])
        for q in range(CHUNKS)
    ]


def fetch_picked(pick, xk, xv, target, sems):
    @pl.when(pick == 0)
    def _():
        for copy in fetch(xk, target, sems):
            copy.start()

    @pl.when(pick != 0)
    def _():
        for copy in fetch(xv, target, sems):
            copy.start()

    return fetch(xk, target, sems)


BLOCK = 256


def put(out, r, value, begin):
    places = pl.ds(r * (BLOCK // BLK), BLOCK // BLK)
    for half, rows in enumerate(arrange(value)):
        for j in range(value.shape[1] // LANES):
            out[places, half, pl.ds(begin + j * ROWS, ROWS), :] = rows[:, :, j * LANES : (j + 1) * LANES].astype(bf16)


def put_folded(out, r, value, begin):
    places = pl.ds(r * (BLOCK // BLK), BLOCK // BLK)
    for half, rows in enumerate(arrange(value)):
        upper, lower = rows[:, : ROWS // 2], pltpu.roll(rows[:, ROWS // 2 :], LANES // 2, 2)
        lane = lax.broadcasted_iota(jnp.int32, upper.shape, 2)
        out[places, half, pl.ds(begin, ROWS // 2), :] = jnp.where(lane < LANES // 2, upper, lower).astype(bf16)


def end_lanes(value):
    lane = lax.broadcasted_iota(jnp.int32, value.shape, 1)
    return jnp.where(lane < BLK, value, 0.0)


def circulate(value, r):
    rows = []
    for b in range(BLOCK // BLK):
        shift = (D - BLK * (r * (BLOCK // BLK) + b)) % D
        piece = value[b * BLK : (b + 1) * BLK]
        rows.append(pltpu.roll(piece, shift, 1) if shift else piece)
    return [jnp.concatenate([p[:, t * LANES : (t + 1) * LANES] for p in rows], axis=0) for t in range(3)]


def zero_grams(pick, x0, out, spare):
    lefts, rests = [], []
    for r in range(D // BLOCK):
        lefts.append(x0[:, pl.ds(r * BLOCK, BLOCK)].T)
        tiles = circulate(dot(lefts[r], x0[...]), r)
        put(out, r, jnp.where(pick == 0, tiles[0], tiles[1]), F0)
        put(spare, r, jnp.where(pick == 0, tiles[1], tiles[0]), 0)
        last = pltpu.roll(end_lanes(tiles[2]), BLK, 1)
        rests.append(jnp.where(pick == 0, 0.0, last))
        put_folded(spare, r, jnp.where(pick == 0, last, 0.0), ROWS)
    return lefts, rests


def picked_grams(lefts, x1, rests, out, end):
    for r in range(D // BLOCK):
        put(out, r, dot(lefts[r], x1[...]), 0)
    for r in range(D // BLOCK):
        left = x1[:, pl.ds(r * BLOCK, BLOCK)].T
        tiles = circulate(dot(left, x1[...]), r)
        put(out, r, jnp.concatenate(tiles[:2], axis=1), FA)
        last = end_lanes(tiles[2])
        put_folded(out, r, last if rests is None else last + rests[r], end)


def theirs_kernel(core, start, width, x0, xk, xv, out, spare, kept, keep, buf0, buf1, masks, sem0, sem1, sem2):
    pick = 1 - core[0]
    small = [pltpu.make_async_copy(v, masks.at[i], sem2.at[i]) for i, v in enumerate((start, width))]
    copies0 = fetch(x0, buf0, sem0)
    for copy in small + copies0:
        copy.start()
    for copy in small:
        copy.wait()
    build_keep(masks.at[0], masks.at[1], keep)
    for q in range(CHUNKS):
        copies0[q].wait()
        if q == 0:
            copies1 = fetch_picked(pick, xk, xv, buf1, sem1)
        apply_mask(buf0, kept, keep, q)
    lefts, rests = zero_grams(pick, kept, out, spare)
    for q in range(CHUNKS):
        copies1[q].wait()
        apply_mask(buf1, buf1, keep, q)
    picked_grams(lefts, buf1, rests, out, FL)


def mine_kernel(core, keep, x0, xk, xv, out, buf1, sem1):
    pick = core[0]
    copies1 = fetch_picked(pick, xk, xv, buf1, sem1)
    lefts = [x0[:, pl.ds(r * BLOCK, BLOCK)].T for r in range(D // BLOCK)]
    for q in range(CHUNKS):
        copies1[q].wait()
        apply_mask(buf1, buf1, keep, q)
    picked_grams(lefts, buf1, None, out, F0)


PIECES = 4


def add_kernel(mine, spare, received, out, buf, sems):
    size = NXY // PIECES
    copies = []
    main, zero, last = slice(0, F0), slice(F0, FL), slice(FL, WROWS)
    for q in range(PIECES):
        for i in range(q * size, (q + 1) * size):
            for j in range(PAIR):
                buf[i, j, main] = mine[i, j, main] + received[i, j, main]
                buf[i, j, zero] = spare[i, j, :ROWS] + received[i, j, zero]
                ends = mine[i, j, F0:] + spare[i, j, ROWS:]
                buf[i, j, last] = ends + received[i, j, last]
        part = pl.ds(q * size, size)
        copies.append(pltpu.make_async_copy(buf.at[part], out.at[part], sems.at[q]))
        copies[q].start()
    for copy in copies:
        copy.wait()


def lam_kernel(share, core, block, keep, x0, xk, xv, bases, keep_lam, send_lam, basis_in_t, mirror, b0, b1, b2, sem0, sem1, sem2):
    c = core[0]
    bufs = (b0, b1, b2)
    copies = [fetch(x, buf, sem) for x, buf, sem in zip((x0, xk, xv), bufs, (sem0, sem1, sem2))]
    for group in copies:
        for copy in group:
            copy.start()
    low, high = arrange(bases[0].astype(f32))
    basis_in_t[...] = jnp.concatenate([low, high], axis=1).reshape(D, D).T.astype(bf16)
    lane = lax.broadcasted_iota(jnp.int32, (LANES, D), 0)
    column = lax.broadcasted_iota(jnp.int32, (LANES, D), 1)
    for half in range(PAIR):
        home = 8 * ((lane >> 2) & 3) + FR * half + (lane & 3) + 2 * D
        for kind in range(2):
            distance = (lane >> 4) + (4 * c if kind else 0)
            there = (home + BLK * (block[0] - distance)) & (D - 1)
            one = jnp.where(column == there, 1.0, 0.0).astype(bf16)
            mirror[pl.ds((2 * half + kind) * LANES, LANES), :] = one
    lam = []
    for f in range(3):
        total = jnp.zeros((8, D), f32)
        for q in range(CHUNKS):
            copies[f][q].wait()
            apply_mask(bufs[f], bufs[f], keep, q)
        for q in range(bufs[f].shape[0] // BLOCK):
            product = dot(bufs[f][pl.ds(q * BLOCK, BLOCK), :], bases[f])
            total = total + jnp.sum((product * product).reshape(BLOCK // 8, 8, D), axis=0)
        lam.append(jnp.sum(total, axis=0, keepdims=True) * share)
    keep_lam[0:1, :] = lam[0]
    send_lam[0:1, :] = lam[0]
    keep_lam[1:2, :] = jnp.where(c == 0, lam[1], lam[2])
    send_lam[1:2, :] = jnp.where(c == 0, lam[2], lam[1])


def split(value):
    high = value.astype(bf16)
    return high.astype(f32), value - high.astype(f32)


def lam_rows(lam):
    return jnp.concatenate(split(jnp.concatenate([lam[:, j * LANES : (j + 1) * LANES] for j in range(GT)], axis=0)), axis=0)


def add_lam(rows):
    return rows[: 2 * GT] + rows[2 * GT :]


def lam_row(total, index):
    return jnp.concatenate([total[2 * j + index : 2 * j + index + 1] for j in range(GT)], axis=1)


LAMR = 4 * GT
DIRECT = GT * ROWS
TURNED = DIRECT + 4 * FR
DEEP_LAM = TURNED + 16
DEEP_ROWS = DEEP_LAM + LAMR
GATHER_LAM = GT * ROWS
GATHER_TURNED = GATHER_LAM + 2 * GT
GATHER_ROWS = GATHER_TURNED + 8


def pack_kernel(parts, keep_lam, send_lam, out):
    total = parts[0].astype(f32)
    for i in range(1, WIDE):
        total = total + parts[i].astype(f32)
    lam = lam_rows(keep_lam[...] + send_lam[...]).astype(bf16)
    for j in range(GT):
        tile = total[j * ROWS : (j + 1) * ROWS].astype(bf16)
        for k in range(DEEP):
            out[k, pl.ds(j * ROWS, ROWS), :] = tile
    near, mid, zero = total[FA : FA + ROWS], total[FA + ROWS : F0], total[F0:FL]
    last = total[FL:]
    last = jnp.concatenate([last, pltpu.roll(last, LANES // 2, 1)], axis=0)
    empty = jnp.zeros((LANES - ROWS, LANES), f32)
    turned = [jnp.concatenate([v, empty], axis=0).T for v in (near, mid, zero)]
    for k in range(DEEP):
        rows = slice(k * FR, (k + 1) * FR)
        direct = jnp.concatenate([v[rows] for v in (near, mid, zero, last)], axis=0)
        out[k, pl.ds(DIRECT, 4 * FR), :] = direct.astype(bf16)

        def pieces(sources):
            result = None
            for n in range(4 * len(sources)):
                piece = sources[n // 4][(n % 4) * BLK + 8 * k : (n % 4) * BLK + 8 * k + 8]
                piece = pltpu.roll(piece, ROWS * n, 1) if n else piece
                result = piece if result is None else result + piece
            return result

        mirrored = jnp.concatenate([pieces(turned[:2]), pieces(turned[2:])], axis=0)
        out[k, pl.ds(TURNED, 16), :] = mirrored.astype(bf16)
        out[k, pl.ds(DEEP_LAM, LAMR), :] = lam


def deep_total(got):
    total = got[0].astype(f32)
    for i in range(1, DEEP):
        total = total + got[i].astype(f32)
    return total, jnp.concatenate([total[j * ROWS : (j + 1) * ROWS] for j in range(GT)], axis=1)


def rotate_kernel(got, basis, out):
    total, grad = deep_total(got)
    rot = dot(grad.astype(bf16), basis[...]).astype(bf16)
    lam = add_lam(total[DEEP_LAM:])
    picked, zero = total[TURNED : TURNED + 8], total[TURNED + 8 : TURNED + 16]
    for half in range(PAIR):
        rows = slice(half * FR, (half + 1) * FR)
        tail = jnp.concatenate([lam, picked[rows], zero[rows]], axis=0).astype(bf16)
        for i in range(half, WIDE, PAIR):
            out[i, pl.ds(GATHER_LAM, ROWS), :] = tail
    for j in range(GT):
        tile = rot[:, j * LANES : (j + 1) * LANES]
        for i in range(WIDE):
            out[i, pl.ds(j * ROWS, ROWS), :] = tile


def rows_kernel(deep, core, block, got, out):
    total, grad = deep_total(got)
    k, c = deep[0], core[0]
    rows = grad[0:FR]
    for other in range(1, DEEP):
        rows = jnp.where(k == other, grad[other * FR : (other + 1) * FR], rows)
    near, mid, zero, last = [total[DIRECT + t * FR : DIRECT + (t + 1) * FR] for t in range(4)]
    lane = lax.broadcasted_iota(jnp.int32, last.shape, 1)
    none = jnp.zeros_like(last)
    end = jnp.where(lane < BLK, last, none)
    end0 = jnp.where(lane < BLK, pltpu.roll(last, LANES - BLK, 1), none)
    picked = jnp.concatenate([near, mid, end, none], axis=1)
    zero = jnp.where(
        c == 0,
        jnp.concatenate([zero, none, none, none], axis=1),
        jnp.concatenate([none, zero, end0, none], axis=1),
    )
    factors = pltpu.roll(jnp.concatenate([picked, zero], axis=0), BLK * block[0], 1)
    out[...] = jnp.concatenate([rows, factors, jnp.zeros_like(rows)], axis=0)


def mirrored_rows(c, block, tails, mirror):
    row = lax.broadcasted_iota(jnp.int32, (8, LANES), 0)
    group = (lax.broadcasted_iota(jnp.int32, (8, LANES), 1) >> 4) + jnp.where(row >= FR, 4 * c, 0)
    parts = []
    for half in range(PAIR):
        own = jnp.zeros((8, LANES), f32)
        for i in range(NXY):
            distance = (block - i) & (NXY - 1)
            wanted = jnp.where((distance >= 1) & (distance < 8), distance, -1)
            own = jnp.where(group == wanted, tails[PAIR * i + half][8:], own)
        parts += [jnp.where(row < FR, own, 0.0), jnp.where(row < FR, 0.0, own)]
    return dot(jnp.concatenate(parts, axis=1).astype(bf16), mirror[...])


def solve_kernel(core, block, got, basis_in_t, basis_out, rows_in, mirror, rows, own, their, scaled):
    tails = [got[i, pl.ds(GATHER_LAM, ROWS), :].astype(f32) for i in range(WIDE)]
    lam = tails[0][:8]
    for tail in tails[1:]:
        lam = lam + tail[:8]
    column = jnp.broadcast_to(lam_row(lam, 0), (8, D)).T[:, 0:1]
    column = jnp.broadcast_to(column, (D, LANES))
    curve = jnp.zeros((8, LANES), f32)
    for j in range(GT):
        rot = got[:, pl.ds(j * ROWS, ROWS), :].reshape(D, LANES)
        rotated = dot(basis_in_t[...], rot)
        low = (rotated / (column * lam[2 * j + 1 : 2 * j + 2] + damping)).astype(bf16)
        scaled[:, pl.ds(j * LANES, LANES)] = low
        curve = curve + jnp.sum((low.astype(f32) * rotated).reshape(D // 8, 8, LANES), axis=0)
    curve = jnp.sum(jnp.sum(curve, axis=1, keepdims=True), axis=0, keepdims=True)
    back = dot(rows_in[...], scaled[...]).astype(bf16)
    prec = lax.dot_general(back, basis_out[...], (((1,), (1,)), ((), ())), preferred_element_type=f32)
    prec = prec.astype(bf16).astype(f32)
    curve = jnp.broadcast_to(curve, (2, D))
    factors = rows[4:12, :] + mirrored_rows(core[0], block[0], tails, mirror)
    low = jnp.concatenate([rows[0:2, :], factors[0:2], factors[4:6]], axis=0)
    high = jnp.concatenate([rows[2:4, :], factors[2:4], factors[6:8]], axis=0)
    first = core[0] == 0
    pad = jnp.zeros((6, D), f32)
    own[...] = jnp.concatenate([prec[0:2], curve, jnp.where(first, low, high), pad], axis=0)
    their[...] = jnp.concatenate([prec[2:4], curve, jnp.where(first, high, low), pad], axis=0)


def finish_kernel(scale, core, own, got, old, new_factors, gradients, updates):
    first = core[0] == 0
    curve = own[2:3, :] + got[2:3, :]
    factor = jnp.sqrt(kl_clip / (learn_rate * learn_rate * curve))
    side0 = jnp.where(first, own[...], got[...])
    side1 = jnp.where(first, got[...], own[...])
    updates[0] = (side0[0:2] * factor).astype(bf16)
    updates[1] = (side1[0:2] * factor).astype(bf16)
    gradients[:, 0, :] = side0[4:6]
    gradients[:, 1, :] = side1[4:6]
    batch = (side0[8:10] + side1[8:10], side0[6:8], side1[6:8])
    for f in range(3):
        new_factors[f] = decay * old[f] + scale * batch[f]


def exchange(value, groups):
    return lax.all_to_all(value, "dp", 0, 0, axis_index_groups=groups, tiled=True)


def body(activations, grad_key, grad_value, time_start, time_width, bases, old_factors):
    index = lax.axis_index("dp").astype(jnp.int32)
    core = index % NC
    first = core == 0
    z = (index // NC) % NZ
    here = ((z // PAIR)[None], core[None], (index // (NC * NZ))[None])
    tokens_here = activations.shape[0]
    share = (1.0 - decay) / (tokens_here * lax.axis_size("dp"))

    def in_hbm(value):
        return pltpu.with_memory_space_constraint(value, pltpu.HBM)

    masks = (in_hbm(time_start.T), in_hbm(time_width.T))
    frames, keys, vals = in_hbm(activations), in_hbm(grad_key), in_hbm(grad_value)
    mask_buf = pltpu.VMEM((2,) + time_start.shape[::-1], jnp.int32)
    buf = pltpu.VMEM((tokens_here, D), bf16)
    sems = pltpu.SemaphoreType.DMA((CHUNKS,))
    pair = pltpu.SemaphoreType.DMA((2,))
    partial = shape((NXY, PAIR, WROWS, LANES), bf16)
    work = 6 * D * D * tokens_here
    with jax.named_scope("grams_theirs"):
        other, spare, kept, keep = call(
            theirs_kernel,
            (partial, shape((NXY, PAIR, ROWS + ROWS // 2, LANES), bf16), shape((tokens_here, D), bf16), shape((tokens_here, LANES), bf16)),
            [SMEM] + [HBM] * 5,
            [buf, buf, mask_buf, sems, sems, pair],
            flops=work,
            moved=4 * MB,
        )(core[None], *masks, frames, keys, vals)
    received = lax.ppermute(other, "dp", SWAP)
    with jax.named_scope("grams_mine"):
        mine = call(
            mine_kernel,
            shape((NXY, PAIR, F0 + ROWS // 2, LANES), bf16),
            [SMEM, VMEM, VMEM, HBM, HBM],
            [buf, sems],
            flops=work,
            moved=4 * MB,
        )(core[None], keep, kept, keys, vals)
    with jax.named_scope("chip_sum"):
        chip = call(
            add_kernel,
            pltpu.HBM(partial.shape, bf16),
            [VMEM] * 3,
            [pltpu.VMEM(partial.shape, bf16), pltpu.SemaphoreType.DMA((PIECES,))],
        )(mine, spare, received).reshape(WIDE, WROWS, LANES)
    with jax.named_scope("wide_sum"):
        parts = exchange(chip, WIDE_GROUPS)

    lam_shape = shape((2, D), f32)
    with jax.named_scope("lam"):
        keep_lam, send_lam, basis_in_t, mirror = call(
            functools.partial(lam_kernel, share),
            (lam_shape, lam_shape, shape((D, D), bf16), shape((2 * PAIR * LANES, D), bf16)),
            [SMEM, SMEM, VMEM, HBM, HBM, HBM, VMEM],
            [buf] * 3 + [sems] * 3,
            flops=work,
            moved=4 * MB,
        )(*here[1:], keep, frames, keys, vals, bases)
    old_lam = []
    my_rows = lax.dynamic_slice_in_dim(bases, 2 * index, 2, 1).astype(f32)
    for f in range(3):
        old_image = jnp.dot(old_factors[:, f, :], bases[f].astype(f32), precision=lax.Precision.HIGHEST)
        old_lam.append(decay * jnp.sum(my_rows[f] * old_image, axis=0))
    keep_lam = keep_lam + jnp.stack([old_lam[0], jnp.where(first, old_lam[1], old_lam[2])])
    send_lam = send_lam + jnp.stack([old_lam[0], jnp.where(first, old_lam[2], old_lam[1])])
    sent_lam = lax.ppermute(send_lam, "dp", SWAP)

    with jax.named_scope("pack"):
        packed = call(pack_kernel, shape((DEEP, DEEP_ROWS, LANES), bf16), [VMEM] * 3)(parts, keep_lam, sent_lam)
    with jax.named_scope("deep_sum"):
        got = exchange(packed, DEEP_GROUPS)
    basis_out = lax.dynamic_index_in_dim(bases, 1 + core, 0, keepdims=False)
    lines = shape((16, D), f32)
    with jax.named_scope("rotate"):
        spread = call(rotate_kernel, shape((WIDE, GATHER_ROWS, LANES), bf16), [VMEM] * 2)(got, basis_out)
    with jax.named_scope("gather"):
        gathered = exchange(spread, WIDE_GROUPS)
    with jax.named_scope("rows"):
        rows = call(rows_kernel, lines, [SMEM] * 3 + [VMEM])(*here, got)
    rows_in = lax.dynamic_slice_in_dim(bases[0], (index // NC) * FR, FR, 0)
    rows_in = jnp.where(first, rows_in, jnp.roll(rows_in, 2, axis=0))
    rows_in = jnp.pad(rows_in, ((0, 16 - FR), (0, 0)))
    with jax.named_scope("solve"):
        own, their = call(solve_kernel, (lines, lines), [SMEM] * 2 + [VMEM] * 6, [pltpu.VMEM((D, D), bf16)])(
            *here[1:], gathered, basis_in_t, basis_out, rows_in, mirror, rows
        )
    theirs = lax.ppermute(their, "dp", SWAP)
    with jax.named_scope("finish"):
        new_factors, gradients, updates = call(
            functools.partial(finish_kernel, share),
            (shape((3, 2, D), f32), shape((2, 2, D), f32), shape((2, 2, D), bf16)),
            [SMEM] + [VMEM] * 3,
        )(core[None], own, theirs, jnp.transpose(old_factors, (1, 0, 2)))
    return (jnp.transpose(new_factors, (1, 0, 2)), gradients, updates)


def solution(mesh):
    in_specs = (
        P("dp", None),
        P("dp", None),
        P("dp", None),
        P("dp", None),
        P("dp", None),
        P(),
        P("dp", None, None),
    )
    out_specs = (P("dp", None, None), P("dp", None, None), P(None, "dp", None))
    return jax.shard_map(body, mesh=mesh, in_specs=in_specs, out_specs=out_specs, check_vma=False)
```

```python
import functools

import jax
import jax.numpy as jnp
from jax import lax
from jax.experimental import pallas as pl
from jax.experimental.pallas import tpu as pltpu
from jax.sharding import PartitionSpec as P

LEN = 128
NX, NY, NZ, NC = 4, 4, 8, 2
NXY = NX * NY
D = 512
HALF = D // 2
PAIR = 2
WIDE = NXY * PAIR
DEEP = NZ // PAIR
ROWS = D // WIDE
LANES = 128
FR = ROWS // DEEP
GT = D // LANES
BLK = D // NXY
FA, F0, FL = GT * ROWS, (GT + 2) * ROWS, (GT + 3) * ROWS
WROWS = FL + ROWS // 2
MB = 1 << 20

decay = 0.8
damping = 0.001
kl_clip = 0.001
learn_rate = 7e-05

f32, bf16 = jnp.float32, jnp.bfloat16


def device(xy, z, c):
    return (xy * NZ + z) * NC + c


SWAP = [(d, d ^ 1) for d in range(NXY * NZ * NC)]
WIDE_GROUPS = [
    [device(i, k * PAIR + l, c) for i in range(NXY) for l in range(PAIR)]
    for k in range(DEEP)
    for c in range(NC)
]
DEEP_GROUPS = [
    [device(i, k * PAIR + l, c) for k in range(DEEP)] for i in range(NXY) for l in range(PAIR) for c in range(NC)
]
VMEM = pl.BlockSpec(memory_space=pltpu.VMEM)
SMEM = pl.BlockSpec(memory_space=pltpu.SMEM)
HBM = pl.BlockSpec(memory_space=pltpu.HBM)
CHUNKS = 2


def call(kernel, outs, in_specs, scratch=(), limit=16, flops=0, moved=0):
    return pl.pallas_call(
        kernel,
        out_shape=outs,
        in_specs=in_specs,
        out_specs=jax.tree.map(lambda out: HBM if isinstance(out, pl.MemoryRef) else VMEM, outs),
        scratch_shapes=list(scratch),
        compiler_params=pltpu.CompilerParams(vmem_limit_bytes=limit * MB),
        cost_estimate=pl.CostEstimate(flops=flops, bytes_accessed=moved, transcendentals=0),
    )


def shape(dims, dtype):
    return jax.ShapeDtypeStruct(dims, dtype)


def dot(a, b):
    return jnp.dot(a, b, preferred_element_type=f32)


def arrange(value):
    size = value.shape[1]
    pairs = value.reshape(value.shape[0] // 16, 2, 8, size)
    even, odd = pairs[:, 0], pairs[:, 1]
    upper = lax.broadcasted_iota(jnp.int32, even.shape, 1) < FR
    low = jnp.where(upper, even, pltpu.roll(odd, FR, 1))
    high = jnp.where(upper, pltpu.roll(even, FR, 1), odd)
    blocks = (value.shape[0] // (PAIR * ROWS), ROWS, size)
    return low.reshape(blocks), high.reshape(blocks)


def build_keep(start, width, keep):
    position = lax.broadcasted_iota(jnp.int32, (LEN, LANES), 0)
    for u in range(start.shape[1]):
        outside = None
        for m in range(start.shape[0]):
            first = start[m, u]
            here = (position < first) | (position >= first + width[m, u])
            outside = here if outside is None else outside & here
        keep[pl.ds(u * LEN, LEN), :] = jnp.where(outside, 1.0, 0.0).astype(bf16)


def apply_mask(source, target, keep, q):
    rows = pl.ds(q * (source.shape[0] // CHUNKS), source.shape[0] // CHUNKS)
    for j in range(GT):
        view = (rows, pl.ds(j * LANES, LANES))
        target[view] = source[view] * keep[rows, :]


def fetch(source, target, sems):
    rows = source.shape[0] // CHUNKS
    return [
        pltpu.make_async_copy(source.at[pl.ds(q * rows, rows)], target.at[pl.ds(q * rows, rows)], sems.at[q])
        for q in range(CHUNKS)
    ]


def fetch_picked(pick, xk, xv, target, sems):
    @pl.when(pick == 0)
    def _():
        for copy in fetch(xk, target, sems):
            copy.start()

    @pl.when(pick != 0)
    def _():
        for copy in fetch(xv, target, sems):
            copy.start()

    return fetch(xk, target, sems)


BLOCK = 256


def put(out, r, value, begin):
    places = pl.ds(r * (BLOCK // BLK), BLOCK // BLK)
    for half, rows in enumerate(arrange(value)):
        for j in range(value.shape[1] // LANES):
            out[places, half, pl.ds(begin + j * ROWS, ROWS), :] = rows[:, :, j * LANES : (j + 1) * LANES].astype(bf16)


def put_folded(out, r, value, begin):
    places = pl.ds(r * (BLOCK // BLK), BLOCK // BLK)
    for half, rows in enumerate(arrange(value)):
        upper, lower = rows[:, : ROWS // 2], pltpu.roll(rows[:, ROWS // 2 :], LANES // 2, 2)
        lane = lax.broadcasted_iota(jnp.int32, upper.shape, 2)
        out[places, half, pl.ds(begin, ROWS // 2), :] = jnp.where(lane < LANES // 2, upper, lower).astype(bf16)


def end_lanes(value):
    lane = lax.broadcasted_iota(jnp.int32, value.shape, 1)
    return jnp.where(lane < BLK, value, 0.0)


def circulate(value, r):
    rows = []
    for b in range(BLOCK // BLK):
        shift = (D - BLK * (r * (BLOCK // BLK) + b)) % D
        piece = value[b * BLK : (b + 1) * BLK]
        rows.append(pltpu.roll(piece, shift, 1) if shift else piece)
    return [jnp.concatenate([p[:, t * LANES : (t + 1) * LANES] for p in rows], axis=0) for t in range(3)]


def zero_grams(pick, x0, out, spare):
    lefts, rests = [], []
    for r in range(D // BLOCK):
        lefts.append(x0[:, pl.ds(r * BLOCK, BLOCK)].T)
        tiles = circulate(dot(lefts[r], x0[...]), r)
        put(out, r, jnp.where(pick == 0, tiles[0], tiles[1]), F0)
        put(spare, r, jnp.where(pick == 0, tiles[1], tiles[0]), 0)
        last = pltpu.roll(end_lanes(tiles[2]), BLK, 1)
        rests.append(jnp.where(pick == 0, 0.0, last))
        put_folded(spare, r, jnp.where(pick == 0, last, 0.0), ROWS)
    return lefts, rests


def picked_grams(lefts, x1, keep, rests, out, end):
    for r in range(D // BLOCK):
        put(out, r, dot(lefts[r], x1[...]), 0)
    wide = jnp.concatenate([keep[...]] * (BLOCK // LANES), axis=1)
    for r in range(D // BLOCK):
        left = (x1[:, pl.ds(r * BLOCK, BLOCK)] * wide).T
        tiles = circulate(dot(left, x1[...]), r)
        put(out, r, jnp.concatenate(tiles[:2], axis=1), FA)
        last = end_lanes(tiles[2])
        put_folded(out, r, last if rests is None else last + rests[r], end)


def theirs_kernel(
    core, start, width, x0, xk, xv, out, spare, kept, keep, ahead, buf0, buf1, starts, widths, sem0, sem1, sem2, sem3
):
    pick = 1 - core[0]
    small = [pltpu.make_async_copy(v, w, sem2.at[i]) for i, (v, w) in enumerate(((start, starts), (width, widths)))]
    copies0 = fetch(x0, buf0, sem0)
    for copy in small + copies0:
        copy.start()
    for copy in small:
        copy.wait()
    build_keep(starts, widths, keep)
    for q in range(CHUNKS):
        copies0[q].wait()
        if q == 0:
            copies1 = fetch_picked(pick, xk, xv, buf1, sem1)
        apply_mask(buf0, kept, keep, q)
    lefts, rests = zero_grams(pick, kept, out, spare)
    for copy in copies1:
        copy.wait()
    copies2 = fetch_picked(core[0], xk, xv, ahead, sem3)
    picked_grams(lefts, buf1, keep, rests, out, FL)
    for copy in copies2:
        copy.wait()


def mine_kernel(keep, x0, x1, out):
    lefts = [x0[:, pl.ds(r * BLOCK, BLOCK)].T for r in range(D // BLOCK)]
    picked_grams(lefts, x1, keep, None, out, F0)


PIECES = 4


def add_kernel(mine, spare, received, out, buf, sems):
    size = NXY // PIECES
    copies = []
    main, zero, last = slice(0, F0), slice(F0, FL), slice(FL, WROWS)
    for q in range(PIECES):
        for i in range(q * size, (q + 1) * size):
            for j in range(PAIR):
                buf[i, j, main] = mine[i, j, main] + received[i, j, main]
                buf[i, j, zero] = spare[i, j, :ROWS] + received[i, j, zero]
                ends = mine[i, j, F0:] + spare[i, j, ROWS:]
                buf[i, j, last] = ends + received[i, j, last]
        part = pl.ds(q * size, size)
        copies.append(pltpu.make_async_copy(buf.at[part], out.at[part], sems.at[q]))
        copies[q].start()
    for copy in copies:
        copy.wait()


def lam_kernel(share, core, block, _, keep, x0, xk, xv, bases, keep_lam, send_lam, basis_in_t, mirror, b0, b1, b2, sem0, sem1, sem2):
    c = core[0]
    bufs = (b0, b1, b2)
    copies = [fetch(x, buf, sem) for x, buf, sem in zip((x0, xk, xv), bufs, (sem0, sem1, sem2))]
    for group in copies:
        for copy in group:
            copy.start()
    low, high = arrange(bases[0].astype(f32))
    basis_in_t[...] = jnp.concatenate([low, high], axis=1).reshape(D, D).T.astype(bf16)
    lane = lax.broadcasted_iota(jnp.int32, (LANES, D), 0)
    column = lax.broadcasted_iota(jnp.int32, (LANES, D), 1)
    for half in range(PAIR):
        home = 8 * ((lane >> 2) & 3) + FR * half + (lane & 3) + 2 * D
        for kind in range(2):
            distance = (lane >> 4) + (4 * c if kind else 0)
            there = (home + BLK * (block[0] - distance)) & (D - 1)
            one = jnp.where(column == there, 1.0, 0.0).astype(bf16)
            mirror[pl.ds((2 * half + kind) * LANES, LANES), :] = one
    lam = []
    for f in range(3):
        total = jnp.zeros((8, D), f32)
        for q in range(CHUNKS):
            copies[f][q].wait()
            apply_mask(bufs[f], bufs[f], keep, q)
        for q in range(bufs[f].shape[0] // BLOCK):
            product = dot(bufs[f][pl.ds(q * BLOCK, BLOCK), :], bases[f])
            total = total + jnp.sum((product * product).reshape(BLOCK // 8, 8, D), axis=0)
        lam.append(jnp.sum(total, axis=0, keepdims=True) * share)
    keep_lam[0:1, :] = lam[0]
    send_lam[0:1, :] = lam[0]
    keep_lam[1:2, :] = jnp.where(c == 0, lam[1], lam[2])
    send_lam[1:2, :] = jnp.where(c == 0, lam[2], lam[1])


def split(value):
    high = value.astype(bf16)
    return high.astype(f32), value - high.astype(f32)


def lam_rows(lam):
    return jnp.concatenate(split(jnp.concatenate([lam[:, j * LANES : (j + 1) * LANES] for j in range(GT)], axis=0)), axis=0)


def add_lam(rows):
    return rows[: 2 * GT] + rows[2 * GT :]


def lam_row(total, index):
    return jnp.concatenate([total[2 * j + index : 2 * j + index + 1] for j in range(GT)], axis=1)


LAMR = 4 * GT
DIRECT = GT * ROWS
TURNED = DIRECT + 4 * FR
DEEP_LAM = TURNED + 16
DEEP_ROWS = DEEP_LAM + LAMR
GATHER_LAM = GT * ROWS
GATHER_TURNED = GATHER_LAM + 2 * GT
GATHER_ROWS = GATHER_TURNED + 8


def pack_kernel(parts, keep_lam, send_lam, out):
    total = parts[0].astype(f32)
    for i in range(1, WIDE):
        total = total + parts[i].astype(f32)
    lam = lam_rows(keep_lam[...] + send_lam[...]).astype(bf16)
    for j in range(GT):
        tile = total[j * ROWS : (j + 1) * ROWS].astype(bf16)
        for k in range(DEEP):
            out[k, pl.ds(j * ROWS, ROWS), :] = tile
    near, mid, zero = total[FA : FA + ROWS], total[FA + ROWS : F0], total[F0:FL]
    last = total[FL:]
    last = jnp.concatenate([last, pltpu.roll(last, LANES // 2, 1)], axis=0)
    empty = jnp.zeros((LANES - ROWS, LANES), f32)
    turned = [jnp.concatenate([v, empty], axis=0).T for v in (near, mid, zero)]
    for k in range(DEEP):
        rows = slice(k * FR, (k + 1) * FR)
        direct = jnp.concatenate([v[rows] for v in (near, mid, zero, last)], axis=0)
        out[k, pl.ds(DIRECT, 4 * FR), :] = direct.astype(bf16)

        def pieces(sources):
            result = None
            for n in range(4 * len(sources)):
                piece = sources[n // 4][(n % 4) * BLK + 8 * k : (n % 4) * BLK + 8 * k + 8]
                piece = pltpu.roll(piece, ROWS * n, 1) if n else piece
                result = piece if result is None else result + piece
            return result

        mirrored = jnp.concatenate([pieces(turned[:2]), pieces(turned[2:])], axis=0)
        out[k, pl.ds(TURNED, 16), :] = mirrored.astype(bf16)
        out[k, pl.ds(DEEP_LAM, LAMR), :] = lam


def deep_total(got):
    total = got[0].astype(f32)
    for i in range(1, DEEP):
        total = total + got[i].astype(f32)
    return total, jnp.concatenate([total[j * ROWS : (j + 1) * ROWS] for j in range(GT)], axis=1)


def rotate_kernel(got, basis, out):
    total, grad = deep_total(got)
    rot = dot(grad.astype(bf16), basis[...]).astype(bf16)
    lam = add_lam(total[DEEP_LAM:])
    picked, zero = total[TURNED : TURNED + 8], total[TURNED + 8 : TURNED + 16]
    for half in range(PAIR):
        rows = slice(half * FR, (half + 1) * FR)
        tail = jnp.concatenate([lam, picked[rows], zero[rows]], axis=0).astype(bf16)
        for i in range(half, WIDE, PAIR):
            out[i, pl.ds(GATHER_LAM, ROWS), :] = tail
    for j in range(GT):
        tile = rot[:, j * LANES : (j + 1) * LANES]
        for i in range(WIDE):
            out[i, pl.ds(j * ROWS, ROWS), :] = tile


def rows_kernel(deep, core, block, got, out):
    total, grad = deep_total(got)
    k, c = deep[0], core[0]
    rows = grad[0:FR]
    for other in range(1, DEEP):
        rows = jnp.where(k == other, grad[other * FR : (other + 1) * FR], rows)
    near, mid, zero, last = [total[DIRECT + t * FR : DIRECT + (t + 1) * FR] for t in range(4)]
    lane = lax.broadcasted_iota(jnp.int32, last.shape, 1)
    none = jnp.zeros_like(last)
    end = jnp.where(lane < BLK, last, none)
    end0 = jnp.where(lane < BLK, pltpu.roll(last, LANES - BLK, 1), none)
    picked = jnp.concatenate([near, mid, end, none], axis=1)
    zero = jnp.where(
        c == 0,
        jnp.concatenate([zero, none, none, none], axis=1),
        jnp.concatenate([none, zero, end0, none], axis=1),
    )
    factors = pltpu.roll(jnp.concatenate([picked, zero], axis=0), BLK * block[0], 1)
    out[...] = jnp.concatenate([rows, factors, jnp.zeros_like(rows)], axis=0)


def mirrored_rows(c, block, tails, mirror):
    row = lax.broadcasted_iota(jnp.int32, (8, LANES), 0)
    group = (lax.broadcasted_iota(jnp.int32, (8, LANES), 1) >> 4) + jnp.where(row >= FR, 4 * c, 0)
    parts = []
    for half in range(PAIR):
        own = jnp.zeros((8, LANES), f32)
        for i in range(NXY):
            distance = (block - i) & (NXY - 1)
            wanted = jnp.where((distance >= 1) & (distance < 8), distance, -1)
            own = jnp.where(group == wanted, tails[PAIR * i + half][8:], own)
        parts += [jnp.where(row < FR, own, 0.0), jnp.where(row < FR, 0.0, own)]
    return dot(jnp.concatenate(parts, axis=1).astype(bf16), mirror[...])


def solve_kernel(core, block, got, basis_in_t, basis_out, rows_in, mirror, rows, own, their, scaled):
    tails = [got[i, pl.ds(GATHER_LAM, ROWS), :].astype(f32) for i in range(WIDE)]
    lam = tails[0][:8]
    for tail in tails[1:]:
        lam = lam + tail[:8]
    column = jnp.broadcast_to(lam_row(lam, 0), (8, D)).T[:, 0:1]
    column = jnp.broadcast_to(column, (D, LANES))
    curve = jnp.zeros((8, LANES), f32)
    for j in range(GT):
        rot = got[:, pl.ds(j * ROWS, ROWS), :].reshape(D, LANES)
        rotated = dot(basis_in_t[...], rot)
        low = (rotated / (column * lam[2 * j + 1 : 2 * j + 2] + damping)).astype(bf16)
        scaled[:, pl.ds(j * LANES, LANES)] = low
        curve = curve + jnp.sum((low.astype(f32) * rotated).reshape(D // 8, 8, LANES), axis=0)
    curve = jnp.sum(jnp.sum(curve, axis=1, keepdims=True), axis=0, keepdims=True)
    back = dot(rows_in[...], scaled[...]).astype(bf16)
    prec = lax.dot_general(back, basis_out[...], (((1,), (1,)), ((), ())), preferred_element_type=f32)
    prec = prec.astype(bf16).astype(f32)
    curve = jnp.broadcast_to(curve, (2, D))
    factors = rows[4:12, :] + mirrored_rows(core[0], block[0], tails, mirror)
    low = jnp.concatenate([rows[0:2, :], factors[0:2], factors[4:6]], axis=0)
    high = jnp.concatenate([rows[2:4, :], factors[2:4], factors[6:8]], axis=0)
    first = core[0] == 0
    pad = jnp.zeros((6, D), f32)
    own[...] = jnp.concatenate([prec[0:2], curve, jnp.where(first, low, high), pad], axis=0)
    their[...] = jnp.concatenate([prec[2:4], curve, jnp.where(first, high, low), pad], axis=0)


def finish_kernel(scale, core, own, got, old, new_factors, gradients, updates):
    first = core[0] == 0
    curve = own[2:3, :] + got[2:3, :]
    factor = jnp.sqrt(kl_clip / (learn_rate * learn_rate * curve))
    side0 = jnp.where(first, own[...], got[...])
    side1 = jnp.where(first, got[...], own[...])
    updates[0] = (side0[0:2] * factor).astype(bf16)
    updates[1] = (side1[0:2] * factor).astype(bf16)
    gradients[:, 0, :] = side0[4:6]
    gradients[:, 1, :] = side1[4:6]
    batch = (side0[8:10] + side1[8:10], side0[6:8], side1[6:8])
    for f in range(3):
        new_factors[f] = decay * old[f] + scale * batch[f]


def exchange(value, groups):
    return lax.all_to_all(value, "dp", 0, 0, axis_index_groups=groups, tiled=True)


def body(activations, grad_key, grad_value, time_start, time_width, bases, old_factors):
    index = lax.axis_index("dp").astype(jnp.int32)
    core = index % NC
    first = core == 0
    z = (index // NC) % NZ
    here = ((z // PAIR)[None], core[None], (index // (NC * NZ))[None])
    tokens_here = activations.shape[0]
    share = (1.0 - decay) / (tokens_here * lax.axis_size("dp"))

    def in_hbm(value):
        return pltpu.with_memory_space_constraint(value, pltpu.HBM)

    masks = (in_hbm(time_start.T), in_hbm(time_width.T))
    frames, keys, vals = in_hbm(activations), in_hbm(grad_key), in_hbm(grad_value)
    mask_buf = pltpu.SMEM(time_start.shape[::-1], jnp.int32)
    buf = pltpu.VMEM((tokens_here, D), bf16)
    sems = pltpu.SemaphoreType.DMA((CHUNKS,))
    pair = pltpu.SemaphoreType.DMA((2,))
    partial = shape((NXY, PAIR, WROWS, LANES), bf16)
    work = 6 * D * D * tokens_here
    with jax.named_scope("grams_theirs"):
        other, spare, kept, keep, ahead = call(
            theirs_kernel,
            (
                partial,
                shape((NXY, PAIR, ROWS + ROWS // 2, LANES), bf16),
                shape((tokens_here, D), bf16),
                shape((tokens_here, LANES), bf16),
                shape((tokens_here, D), bf16),
            ),
            [SMEM] + [HBM] * 5,
            [buf, buf, mask_buf, mask_buf, sems, sems, pair, sems],
            flops=work,
            moved=4 * MB,
        )(core[None], *masks, frames, keys, vals)
    received = lax.ppermute(other, "dp", SWAP)
    with jax.named_scope("grams_mine"):
        mine = call(
            mine_kernel,
            shape((NXY, PAIR, F0 + ROWS // 2, LANES), bf16),
            [VMEM] * 3,
            flops=work,
            moved=4 * MB,
        )(keep, kept, ahead)
    with jax.named_scope("chip_sum"):
        chip = call(
            add_kernel,
            pltpu.HBM(partial.shape, bf16),
            [VMEM] * 3,
            [pltpu.VMEM(partial.shape, bf16), pltpu.SemaphoreType.DMA((PIECES,))],
        )(mine, spare, received).reshape(WIDE, WROWS, LANES)
    with jax.named_scope("wide_sum"):
        parts = exchange(chip, WIDE_GROUPS)

    lam_shape = shape((2, D), f32)
    with jax.named_scope("lam"):
        keep_lam, send_lam, basis_in_t, mirror = call(
            functools.partial(lam_kernel, share),
            (lam_shape, lam_shape, shape((D, D), bf16), shape((2 * PAIR * LANES, D), bf16)),
            [SMEM, SMEM, HBM, VMEM, HBM, HBM, HBM, VMEM],
            [buf] * 3 + [sems] * 3,
            flops=work,
            moved=4 * MB,
        )(*here[1:], in_hbm(chip), keep, frames, keys, vals, bases)
    old_lam = []
    my_rows = lax.dynamic_slice_in_dim(bases, 2 * index, 2, 1).astype(f32)
    for f in range(3):
        old_image = jnp.dot(old_factors[:, f, :], bases[f].astype(f32), precision=lax.Precision.HIGHEST)
        old_lam.append(decay * jnp.sum(my_rows[f] * old_image, axis=0))
    keep_lam = keep_lam + jnp.stack([old_lam[0], jnp.where(first, old_lam[1], old_lam[2])])
    send_lam = send_lam + jnp.stack([old_lam[0], jnp.where(first, old_lam[2], old_lam[1])])
    sent_lam = lax.ppermute(send_lam, "dp", SWAP)

    with jax.named_scope("pack"):
        packed = call(pack_kernel, shape((DEEP, DEEP_ROWS, LANES), bf16), [VMEM] * 3)(parts, keep_lam, sent_lam)
    with jax.named_scope("deep_sum"):
        got = exchange(packed, DEEP_GROUPS)
    basis_out = lax.dynamic_index_in_dim(bases, 1 + core, 0, keepdims=False)
    lines = shape((16, D), f32)
    with jax.named_scope("rotate"):
        spread = call(rotate_kernel, shape((WIDE, GATHER_ROWS, LANES), bf16), [VMEM] * 2)(got, basis_out)
    with jax.named_scope("gather"):
        gathered = exchange(spread, WIDE_GROUPS)
    with jax.named_scope("rows"):
        rows = call(rows_kernel, lines, [SMEM] * 3 + [VMEM])(*here, got)
    rows_in = lax.dynamic_slice_in_dim(bases[0], (index // NC) * FR, FR, 0)
    rows_in = jnp.where(first, rows_in, jnp.roll(rows_in, 2, axis=0))
    rows_in = jnp.pad(rows_in, ((0, 16 - FR), (0, 0)))
    with jax.named_scope("solve"):
        own, their = call(solve_kernel, (lines, lines), [SMEM] * 2 + [VMEM] * 6, [pltpu.VMEM((D, D), bf16)])(
            *here[1:], gathered, basis_in_t, basis_out, rows_in, mirror, rows
        )
    theirs = lax.ppermute(their, "dp", SWAP)
    with jax.named_scope("finish"):
        new_factors, gradients, updates = call(
            functools.partial(finish_kernel, share),
            (shape((3, 2, D), f32), shape((2, 2, D), f32), shape((2, 2, D), bf16)),
            [SMEM] + [VMEM] * 3,
        )(core[None], own, theirs, jnp.transpose(old_factors, (1, 0, 2)))
    return (jnp.transpose(new_factors, (1, 0, 2)), gradients, updates)


def solution(mesh):
    in_specs = (
        P("dp", None),
        P("dp", None),
        P("dp", None),
        P("dp", None),
        P("dp", None),
        P(),
        P("dp", None, None),
    )
    out_specs = (P("dp", None, None), P("dp", None, None), P(None, "dp", None))
    return jax.shard_map(body, mesh=mesh, in_specs=in_specs, out_specs=out_specs, check_vma=False)
```

```python
import functools

import jax
import jax.numpy as jnp
from jax import lax
from jax.experimental import pallas as pl
from jax.experimental.pallas import tpu as pltpu
from jax.sharding import PartitionSpec as P

LEN = 128
NX, NY, NZ, NC = 4, 4, 8, 2
NXY = NX * NY
D = 512
HALF = D // 2
PAIR = 2
WIDE = NXY * PAIR
DEEP = NZ // PAIR
ROWS = D // WIDE
LANES = 128
FR = ROWS // DEEP
GT = D // LANES
BLK = D // NXY
FA, F0, FL = GT * ROWS, (GT + 2) * ROWS, (GT + 3) * ROWS
WROWS = FL + ROWS // 2
MB = 1 << 20

decay = 0.8
damping = 0.001
kl_clip = 0.001
learn_rate = 7e-05

f32, bf16 = jnp.float32, jnp.bfloat16


def device(xy, z, c):
    return (xy * NZ + z) * NC + c


SWAP = [(d, d ^ 1) for d in range(NXY * NZ * NC)]
WIDE_GROUPS = [
    [device(i, k * PAIR + l, c) for i in range(NXY) for l in range(PAIR)]
    for k in range(DEEP)
    for c in range(NC)
]
DEEP_GROUPS = [
    [device(i, k * PAIR + l, c) for k in range(DEEP)] for i in range(NXY) for l in range(PAIR) for c in range(NC)
]
VMEM = pl.BlockSpec(memory_space=pltpu.VMEM)
SMEM = pl.BlockSpec(memory_space=pltpu.SMEM)
HBM = pl.BlockSpec(memory_space=pltpu.HBM)
CHUNKS = 2


def call(kernel, outs, in_specs, scratch=(), limit=16, flops=0, moved=0):
    return pl.pallas_call(
        kernel,
        out_shape=outs,
        in_specs=in_specs,
        out_specs=jax.tree.map(lambda out: HBM if isinstance(out, pl.MemoryRef) else VMEM, outs),
        scratch_shapes=list(scratch),
        compiler_params=pltpu.CompilerParams(vmem_limit_bytes=limit * MB),
        cost_estimate=pl.CostEstimate(flops=flops, bytes_accessed=moved, transcendentals=0),
    )


def shape(dims, dtype):
    return jax.ShapeDtypeStruct(dims, dtype)


def dot(a, b):
    return jnp.dot(a, b, preferred_element_type=f32)


def arrange(value):
    size = value.shape[1]
    pairs = value.reshape(value.shape[0] // 16, 2, 8, size)
    even, odd = pairs[:, 0], pairs[:, 1]
    upper = lax.broadcasted_iota(jnp.int32, even.shape, 1) < FR
    low = jnp.where(upper, even, pltpu.roll(odd, FR, 1))
    high = jnp.where(upper, pltpu.roll(even, FR, 1), odd)
    blocks = (value.shape[0] // (PAIR * ROWS), ROWS, size)
    return low.reshape(blocks), high.reshape(blocks)


def build_keep(start, width, keep):
    position = lax.broadcasted_iota(jnp.int32, (LEN, LANES), 0)
    for u in range(start.shape[1]):
        outside = None
        for m in range(start.shape[0]):
            first = start[m, u]
            here = (position < first) | (position >= first + width[m, u])
            outside = here if outside is None else outside & here
        keep[pl.ds(u * LEN, LEN), :] = jnp.where(outside, 1.0, 0.0).astype(bf16)


def apply_mask(source, target, keep, q):
    rows = pl.ds(q * (source.shape[0] // CHUNKS), source.shape[0] // CHUNKS)
    for j in range(GT):
        view = (rows, pl.ds(j * LANES, LANES))
        target[view] = source[view] * keep[rows, :]


def fetch(source, target, sems):
    rows = source.shape[0] // CHUNKS
    return [
        pltpu.make_async_copy(source.at[pl.ds(q * rows, rows)], target.at[pl.ds(q * rows, rows)], sems.at[q])
        for q in range(CHUNKS)
    ]


def fetch_picked(pick, xk, xv, target, sems):
    @pl.when(pick == 0)
    def _():
        for copy in fetch(xk, target, sems):
            copy.start()

    @pl.when(pick != 0)
    def _():
        for copy in fetch(xv, target, sems):
            copy.start()

    return fetch(xk, target, sems)


BLOCK = 256


def put(out, r, value, begin):
    places = pl.ds(r * (BLOCK // BLK), BLOCK // BLK)
    for half, rows in enumerate(arrange(value)):
        for j in range(value.shape[1] // LANES):
            out[places, half, pl.ds(begin + j * ROWS, ROWS), :] = rows[:, :, j * LANES : (j + 1) * LANES].astype(bf16)


def put_folded(out, r, value, begin):
    places = pl.ds(r * (BLOCK // BLK), BLOCK // BLK)
    for half, rows in enumerate(arrange(value)):
        upper, lower = rows[:, : ROWS // 2], pltpu.roll(rows[:, ROWS // 2 :], LANES // 2, 2)
        lane = lax.broadcasted_iota(jnp.int32, upper.shape, 2)
        out[places, half, pl.ds(begin, ROWS // 2), :] = jnp.where(lane < LANES // 2, upper, lower).astype(bf16)


def end_lanes(value):
    lane = lax.broadcasted_iota(jnp.int32, value.shape, 1)
    return jnp.where(lane < BLK, value, 0.0)


def circulate(value, r):
    rows = []
    for b in range(BLOCK // BLK):
        shift = (D - BLK * (r * (BLOCK // BLK) + b)) % D
        piece = value[b * BLK : (b + 1) * BLK]
        rows.append(pltpu.roll(piece, shift, 1) if shift else piece)
    return [jnp.concatenate([p[:, t * LANES : (t + 1) * LANES] for p in rows], axis=0) for t in range(3)]


def zero_grams(pick, x0, out, spare):
    lefts, rests = [], []
    for r in range(D // BLOCK):
        lefts.append(x0[:, pl.ds(r * BLOCK, BLOCK)].T)
        tiles = circulate(dot(lefts[r], x0[...]), r)
        put(out, r, jnp.where(pick == 0, tiles[0], tiles[1]), F0)
        put(spare, r, jnp.where(pick == 0, tiles[1], tiles[0]), 0)
        last = pltpu.roll(end_lanes(tiles[2]), BLK, 1)
        rests.append(jnp.where(pick == 0, 0.0, last))
        put_folded(spare, r, jnp.where(pick == 0, last, 0.0), ROWS)
    return lefts, rests


def picked_grams(lefts, x1, keep, rests, out, end):
    for r in range(D // BLOCK):
        put(out, r, dot(lefts[r], x1[...]), 0)
    wide = jnp.concatenate([keep[...]] * (BLOCK // LANES), axis=1)
    for r in range(D // BLOCK):
        left = (x1[:, pl.ds(r * BLOCK, BLOCK)] * wide).T
        tiles = circulate(dot(left, x1[...]), r)
        put(out, r, jnp.concatenate(tiles[:2], axis=1), FA)
        last = end_lanes(tiles[2])
        put_folded(out, r, last if rests is None else last + rests[r], end)


def theirs_kernel(
    core, start, width, x0, xk, xv, out, spare, kept, keep, ahead, buf0, buf1, starts, widths, sem0, sem1, sem2, sem3
):
    pick = 1 - core[0]
    small = [pltpu.make_async_copy(v, w, sem2.at[i]) for i, (v, w) in enumerate(((start, starts), (width, widths)))]
    copies0 = fetch(x0, buf0, sem0)
    for copy in small + copies0:
        copy.start()
    for copy in small:
        copy.wait()
    build_keep(starts, widths, keep)
    for q in range(CHUNKS):
        copies0[q].wait()
        if q == 0:
            copies1 = fetch_picked(pick, xk, xv, buf1, sem1)
        apply_mask(buf0, kept, keep, q)
    lefts, rests = zero_grams(pick, kept, out, spare)
    for copy in copies1:
        copy.wait()
    copies2 = fetch_picked(core[0], xk, xv, ahead, sem3)
    picked_grams(lefts, buf1, keep, rests, out, FL)
    for copy in copies2:
        copy.wait()


def mine_kernel(keep, x0, x1, out):
    lefts = [x0[:, pl.ds(r * BLOCK, BLOCK)].T for r in range(D // BLOCK)]
    picked_grams(lefts, x1, keep, None, out, F0)


PIECES = 4


def add_kernel(mine, spare, received, out, buf, sems):
    size = NXY // PIECES
    copies = []
    main, zero, last = slice(0, F0), slice(F0, FL), slice(FL, WROWS)
    for q in range(PIECES):
        for i in range(q * size, (q + 1) * size):
            for j in range(PAIR):
                buf[i, j, main] = mine[i, j, main] + received[i, j, main]
                buf[i, j, zero] = spare[i, j, :ROWS] + received[i, j, zero]
                ends = mine[i, j, F0:] + spare[i, j, ROWS:]
                buf[i, j, last] = ends + received[i, j, last]
        part = pl.ds(q * size, size)
        copies.append(pltpu.make_async_copy(buf.at[part], out.at[part], sems.at[q]))
        copies[q].start()
    for copy in copies:
        copy.wait()


def lam_kernel(
    share, core, block, chip, _, keep, x0, xk, xv, bases, keep_lam, send_lam, basis_in_t, mirror, basis_out, rows_in, b0, b1, b2, sem0, sem1, sem2
):
    c = core[0]
    bufs = (b0, b1, b2)
    copies = [fetch(x, buf, sem) for x, buf, sem in zip((x0, xk, xv), bufs, (sem0, sem1, sem2))]
    for group in copies:
        for copy in group:
            copy.start()
    low, high = arrange(bases[0].astype(f32))
    basis_in_t[...] = jnp.concatenate([low, high], axis=1).reshape(D, D).T.astype(bf16)
    lane = lax.broadcasted_iota(jnp.int32, (LANES, D), 0)
    column = lax.broadcasted_iota(jnp.int32, (LANES, D), 1)
    for half in range(PAIR):
        home = 8 * ((lane >> 2) & 3) + FR * half + (lane & 3) + 2 * D
        for kind in range(2):
            distance = (lane >> 4) + (4 * c if kind else 0)
            there = (home + BLK * (block[0] - distance)) & (D - 1)
            one = jnp.where(column == there, 1.0, 0.0).astype(bf16)
            mirror[pl.ds((2 * half + kind) * LANES, LANES), :] = one
    basis_out[...] = bases[1 + c]
    row = lax.broadcasted_iota(jnp.int32, (16, D), 0)
    column = lax.broadcasted_iota(jnp.int32, (16, D), 1)
    wanted = (row < FR) & (column == FR * chip[0] + ((row + 2 * c) & (FR - 1)))
    rows_in[...] = dot(jnp.where(wanted, 1.0, 0.0).astype(bf16), bases[0]).astype(bf16)
    lam = []
    for f in range(3):
        total = jnp.zeros((8, D), f32)
        for q in range(CHUNKS):
            copies[f][q].wait()
            apply_mask(bufs[f], bufs[f], keep, q)
        for q in range(bufs[f].shape[0] // BLOCK):
            product = dot(bufs[f][pl.ds(q * BLOCK, BLOCK), :], bases[f])
            total = total + jnp.sum((product * product).reshape(BLOCK // 8, 8, D), axis=0)
        lam.append(jnp.sum(total, axis=0, keepdims=True) * share)
    keep_lam[0:1, :] = lam[0]
    send_lam[0:1, :] = lam[0]
    keep_lam[1:2, :] = jnp.where(c == 0, lam[1], lam[2])
    send_lam[1:2, :] = jnp.where(c == 0, lam[2], lam[1])


def split(value):
    high = value.astype(bf16)
    return high.astype(f32), value - high.astype(f32)


def lam_rows(lam):
    return jnp.concatenate(split(jnp.concatenate([lam[:, j * LANES : (j + 1) * LANES] for j in range(GT)], axis=0)), axis=0)


def add_lam(rows):
    return rows[: 2 * GT] + rows[2 * GT :]


def lam_row(total, index):
    return jnp.concatenate([total[2 * j + index : 2 * j + index + 1] for j in range(GT)], axis=1)


LAMR = 4 * GT
DIRECT = GT * ROWS
TURNED = DIRECT + 4 * FR
DEEP_LAM = TURNED + 16
DEEP_ROWS = DEEP_LAM + LAMR
GATHER_LAM = GT * ROWS
GATHER_TURNED = GATHER_LAM + 2 * GT
GATHER_ROWS = GATHER_TURNED + 8


def pack_kernel(parts, keep_lam, send_lam, out):
    total = parts[0].astype(f32)
    for i in range(1, WIDE):
        total = total + parts[i].astype(f32)
    lam = lam_rows(keep_lam[...] + send_lam[...]).astype(bf16)
    for j in range(GT):
        tile = total[j * ROWS : (j + 1) * ROWS].astype(bf16)
        for k in range(DEEP):
            out[k, pl.ds(j * ROWS, ROWS), :] = tile
    near, mid, zero = total[FA : FA + ROWS], total[FA + ROWS : F0], total[F0:FL]
    last = total[FL:]
    last = jnp.concatenate([last, pltpu.roll(last, LANES // 2, 1)], axis=0)
    empty = jnp.zeros((LANES - ROWS, LANES), f32)
    turned = [jnp.concatenate([v, empty], axis=0).T for v in (near, mid, zero)]
    for k in range(DEEP):
        rows = slice(k * FR, (k + 1) * FR)
        direct = jnp.concatenate([v[rows] for v in (near, mid, zero, last)], axis=0)
        out[k, pl.ds(DIRECT, 4 * FR), :] = direct.astype(bf16)

        def pieces(sources):
            result = None
            for n in range(4 * len(sources)):
                piece = sources[n // 4][(n % 4) * BLK + 8 * k : (n % 4) * BLK + 8 * k + 8]
                piece = pltpu.roll(piece, ROWS * n, 1) if n else piece
                result = piece if result is None else result + piece
            return result

        mirrored = jnp.concatenate([pieces(turned[:2]), pieces(turned[2:])], axis=0)
        out[k, pl.ds(TURNED, 16), :] = mirrored.astype(bf16)
        out[k, pl.ds(DEEP_LAM, LAMR), :] = lam


def deep_total(got):
    total = got[0].astype(f32)
    for i in range(1, DEEP):
        total = total + got[i].astype(f32)
    return total, jnp.concatenate([total[j * ROWS : (j + 1) * ROWS] for j in range(GT)], axis=1)


def rotate_kernel(got, basis, out):
    total, grad = deep_total(got)
    rot = dot(grad.astype(bf16), basis[...]).astype(bf16)
    lam = add_lam(total[DEEP_LAM:])
    picked, zero = total[TURNED : TURNED + 8], total[TURNED + 8 : TURNED + 16]
    for half in range(PAIR):
        rows = slice(half * FR, (half + 1) * FR)
        tail = jnp.concatenate([lam, picked[rows], zero[rows]], axis=0).astype(bf16)
        for i in range(half, WIDE, PAIR):
            out[i, pl.ds(GATHER_LAM, ROWS), :] = tail
    for j in range(GT):
        tile = rot[:, j * LANES : (j + 1) * LANES]
        for i in range(WIDE):
            out[i, pl.ds(j * ROWS, ROWS), :] = tile


def direct_rows(k, c, block, got):
    total, grad = deep_total(got)
    rows = grad[0:FR]
    for other in range(1, DEEP):
        rows = jnp.where(k == other, grad[other * FR : (other + 1) * FR], rows)
    near, mid, zero, last = [total[DIRECT + t * FR : DIRECT + (t + 1) * FR] for t in range(4)]
    lane = lax.broadcasted_iota(jnp.int32, last.shape, 1)
    none = jnp.zeros_like(last)
    end = jnp.where(lane < BLK, last, none)
    end0 = jnp.where(lane < BLK, pltpu.roll(last, LANES - BLK, 1), none)
    picked = jnp.concatenate([near, mid, end, none], axis=1)
    zero = jnp.where(
        c == 0,
        jnp.concatenate([zero, none, none, none], axis=1),
        jnp.concatenate([none, zero, end0, none], axis=1),
    )
    return rows, pltpu.roll(jnp.concatenate([picked, zero], axis=0), BLK * block, 1)


def mirrored_rows(c, block, tails, mirror):
    row = lax.broadcasted_iota(jnp.int32, (8, LANES), 0)
    group = (lax.broadcasted_iota(jnp.int32, (8, LANES), 1) >> 4) + jnp.where(row >= FR, 4 * c, 0)
    parts = []
    for half in range(PAIR):
        own = jnp.zeros((8, LANES), f32)
        for i in range(NXY):
            distance = (block - i) & (NXY - 1)
            wanted = jnp.where((distance >= 1) & (distance < 8), distance, -1)
            own = jnp.where(group == wanted, tails[PAIR * i + half][8:], own)
        parts += [jnp.where(row < FR, own, 0.0), jnp.where(row < FR, 0.0, own)]
    return dot(jnp.concatenate(parts, axis=1).astype(bf16), mirror[...])


def solve_kernel(deep, core, block, got, packed, basis_in_t, basis_out, rows_in, mirror, own, their, scaled):
    tails = [got[i, pl.ds(GATHER_LAM, ROWS), :].astype(f32) for i in range(WIDE)]
    lam = tails[0][:8]
    for tail in tails[1:]:
        lam = lam + tail[:8]
    column = jnp.broadcast_to(lam_row(lam, 0), (8, D)).T[:, 0:1]
    column = jnp.broadcast_to(column, (D, LANES))
    curve = jnp.zeros((8, LANES), f32)
    for j in range(GT):
        rot = got[:, pl.ds(j * ROWS, ROWS), :].reshape(D, LANES)
        rotated = dot(basis_in_t[...], rot)
        low = (rotated / (column * lam[2 * j + 1 : 2 * j + 2] + damping)).astype(bf16)
        scaled[:, pl.ds(j * LANES, LANES)] = low
        curve = curve + jnp.sum((low.astype(f32) * rotated).reshape(D // 8, 8, LANES), axis=0)
    curve = jnp.sum(jnp.sum(curve, axis=1, keepdims=True), axis=0, keepdims=True)
    back = dot(rows_in[...], scaled[...]).astype(bf16)
    prec = lax.dot_general(back, basis_out[...], (((1,), (1,)), ((), ())), preferred_element_type=f32)
    prec = prec.astype(bf16).astype(f32)
    curve = jnp.broadcast_to(curve, (2, D))
    rows, factors = direct_rows(deep[0], core[0], block[0], packed)
    factors = factors + mirrored_rows(core[0], block[0], tails, mirror)
    low = jnp.concatenate([rows[0:2], factors[0:2], factors[4:6]], axis=0)
    high = jnp.concatenate([rows[2:4], factors[2:4], factors[6:8]], axis=0)
    first = core[0] == 0
    pad = jnp.zeros((6, D), f32)
    own[...] = jnp.concatenate([prec[0:2], curve, jnp.where(first, low, high), pad], axis=0)
    their[...] = jnp.concatenate([prec[2:4], curve, jnp.where(first, high, low), pad], axis=0)


def finish_kernel(scale, core, own, got, old, new_factors, gradients, updates):
    first = core[0] == 0
    curve = own[2:3, :] + got[2:3, :]
    factor = jnp.sqrt(kl_clip / (learn_rate * learn_rate * curve))
    side0 = jnp.where(first, own[...], got[...])
    side1 = jnp.where(first, got[...], own[...])
    updates[0] = (side0[0:2] * factor).astype(bf16)
    updates[1] = (side1[0:2] * factor).astype(bf16)
    gradients[:, 0, :] = side0[4:6]
    gradients[:, 1, :] = side1[4:6]
    batch = (side0[8:10] + side1[8:10], side0[6:8], side1[6:8])
    for f in range(3):
        new_factors[f] = decay * old[f] + scale * batch[f]


def exchange(value, groups):
    return lax.all_to_all(value, "dp", 0, 0, axis_index_groups=groups, tiled=True)


def body(activations, grad_key, grad_value, time_start, time_width, bases, old_factors):
    index = lax.axis_index("dp").astype(jnp.int32)
    core = index & (NC - 1)
    first = core == 0
    chip_here = index >> 1
    z = chip_here & (NZ - 1)
    here = ((z >> 1)[None], core[None], (chip_here >> 3)[None])
    chip_index = chip_here[None]
    tokens_here = activations.shape[0]
    share = (1.0 - decay) / (tokens_here * lax.axis_size("dp"))

    def in_hbm(value):
        return pltpu.with_memory_space_constraint(value, pltpu.HBM)

    masks = (in_hbm(time_start.T), in_hbm(time_width.T))
    frames, keys, vals = in_hbm(activations), in_hbm(grad_key), in_hbm(grad_value)
    mask_buf = pltpu.SMEM(time_start.shape[::-1], jnp.int32)
    buf = pltpu.VMEM((tokens_here, D), bf16)
    sems = pltpu.SemaphoreType.DMA((CHUNKS,))
    pair = pltpu.SemaphoreType.DMA((2,))
    partial = shape((NXY, PAIR, WROWS, LANES), bf16)
    work = 6 * D * D * tokens_here
    with jax.named_scope("grams_theirs"):
        other, spare, kept, keep, ahead = call(
            theirs_kernel,
            (
                partial,
                shape((NXY, PAIR, ROWS + ROWS // 2, LANES), bf16),
                shape((tokens_here, D), bf16),
                shape((tokens_here, LANES), bf16),
                shape((tokens_here, D), bf16),
            ),
            [SMEM] + [HBM] * 5,
            [buf, buf, mask_buf, mask_buf, sems, sems, pair, sems],
            flops=work,
            moved=4 * MB,
        )(core[None], *masks, frames, keys, vals)
    received = lax.ppermute(other, "dp", SWAP)
    with jax.named_scope("grams_mine"):
        mine = call(
            mine_kernel,
            shape((NXY, PAIR, F0 + ROWS // 2, LANES), bf16),
            [VMEM] * 3,
            flops=work,
            moved=4 * MB,
        )(keep, kept, ahead)
    with jax.named_scope("chip_sum"):
        chip = call(
            add_kernel,
            pltpu.HBM(partial.shape, bf16),
            [VMEM] * 3,
            [pltpu.VMEM(partial.shape, bf16), pltpu.SemaphoreType.DMA((PIECES,))],
        )(mine, spare, received).reshape(WIDE, WROWS, LANES)
    with jax.named_scope("wide_sum"):
        parts = exchange(chip, WIDE_GROUPS)

    lam_shape, square = shape((2, D), f32), shape((D, D), bf16)
    with jax.named_scope("lam"):
        keep_lam, send_lam, basis_in_t, mirror, basis_out, rows_in = call(
            functools.partial(lam_kernel, share),
            (lam_shape, lam_shape, square, square, square, shape((16, D), bf16)),
            [SMEM, SMEM, SMEM, HBM, VMEM, HBM, HBM, HBM, VMEM],
            [buf] * 3 + [sems] * 3,
            flops=work,
            moved=4 * MB,
        )(*here[1:], chip_index, in_hbm(chip), keep, frames, keys, vals, bases)
    old_lam = []
    my_rows = lax.dynamic_slice_in_dim(bases, 2 * index, 2, 1).astype(f32)
    for f in range(3):
        old_image = jnp.dot(old_factors[:, f, :], bases[f].astype(f32), precision=lax.Precision.HIGHEST)
        old_lam.append(decay * jnp.sum(my_rows[f] * old_image, axis=0))
    keep_lam = keep_lam + jnp.stack([old_lam[0], jnp.where(first, old_lam[1], old_lam[2])])
    send_lam = send_lam + jnp.stack([old_lam[0], jnp.where(first, old_lam[2], old_lam[1])])
    sent_lam = lax.ppermute(send_lam, "dp", SWAP)

    with jax.named_scope("pack"):
        packed = call(pack_kernel, shape((DEEP, DEEP_ROWS, LANES), bf16), [VMEM] * 3)(parts, keep_lam, sent_lam)
    with jax.named_scope("deep_sum"):
        got = exchange(packed, DEEP_GROUPS)
    lines = shape((16, D), f32)
    with jax.named_scope("rotate"):
        spread = call(rotate_kernel, shape((WIDE, GATHER_ROWS, LANES), bf16), [VMEM] * 2)(got, basis_out)
    with jax.named_scope("gather"):
        gathered = exchange(spread, WIDE_GROUPS)
    with jax.named_scope("solve"):
        own, their = call(solve_kernel, (lines, lines), [SMEM] * 3 + [VMEM] * 6, [pltpu.VMEM((D, D), bf16)])(
            *here, gathered, got, basis_in_t, basis_out, rows_in, mirror
        )
    theirs = lax.ppermute(their, "dp", SWAP)
    with jax.named_scope("finish"):
        new_factors, gradients, updates = call(
            functools.partial(finish_kernel, share),
            (shape((3, 2, D), f32), shape((2, 2, D), f32), shape((2, 2, D), bf16)),
            [SMEM] + [VMEM] * 3,
        )(core[None], own, theirs, jnp.transpose(old_factors, (1, 0, 2)))
    return (jnp.transpose(new_factors, (1, 0, 2)), gradients, updates)


def solution(mesh):
    in_specs = (
        P("dp", None),
        P("dp", None),
        P("dp", None),
        P("dp", None),
        P("dp", None),
        P(),
        P("dp", None, None),
    )
    out_specs = (P("dp", None, None), P("dp", None, None), P(None, "dp", None))
    return jax.shard_map(body, mesh=mesh, in_specs=in_specs, out_specs=out_specs, check_vma=False)
```

```python
import functools

import jax
import jax.numpy as jnp
from jax import lax
from jax.experimental import pallas as pl
from jax.experimental.pallas import tpu as pltpu
from jax.sharding import PartitionSpec as P

LEN = 128
NX, NY, NZ, NC = 4, 4, 8, 2
NXY = NX * NY
D = 512
HALF = D // 2
PAIR = 2
WIDE = NXY * PAIR
DEEP = NZ // PAIR
ROWS = D // WIDE
LANES = 128
FR = ROWS // DEEP
GT = D // LANES
BLK = D // NXY
FA, F0, FL = GT * ROWS, (GT + 2) * ROWS, (GT + 3) * ROWS
WROWS = FL + ROWS // 2
MB = 1 << 20

decay = 0.8
damping = 0.001
kl_clip = 0.001
learn_rate = 7e-05

f32, bf16 = jnp.float32, jnp.bfloat16


def device(xy, z, c):
    return (xy * NZ + z) * NC + c


SWAP = [(d, d ^ 1) for d in range(NXY * NZ * NC)]
WIDE_GROUPS = [
    [device(i, k * PAIR + l, c) for i in range(NXY) for l in range(PAIR)]
    for k in range(DEEP)
    for c in range(NC)
]
DEEP_GROUPS = [
    [device(i, k * PAIR + l, c) for k in range(DEEP)] for i in range(NXY) for l in range(PAIR) for c in range(NC)
]
VMEM = pl.BlockSpec(memory_space=pltpu.VMEM)
SMEM = pl.BlockSpec(memory_space=pltpu.SMEM)
HBM = pl.BlockSpec(memory_space=pltpu.HBM)
CHUNKS = 2


def call(kernel, outs, in_specs, scratch=(), limit=16, flops=0, moved=0):
    return pl.pallas_call(
        kernel,
        out_shape=outs,
        in_specs=in_specs,
        out_specs=jax.tree.map(lambda out: HBM if isinstance(out, pl.MemoryRef) else VMEM, outs),
        scratch_shapes=list(scratch),
        compiler_params=pltpu.CompilerParams(vmem_limit_bytes=limit * MB),
        cost_estimate=pl.CostEstimate(flops=flops, bytes_accessed=moved, transcendentals=0),
    )


def shape(dims, dtype):
    return jax.ShapeDtypeStruct(dims, dtype)


def dot(a, b):
    return jnp.dot(a, b, preferred_element_type=f32)


def arrange(value):
    size = value.shape[1]
    pairs = value.reshape(value.shape[0] // 16, 2, 8, size)
    even, odd = pairs[:, 0], pairs[:, 1]
    upper = lax.broadcasted_iota(jnp.int32, even.shape, 1) < FR
    low = jnp.where(upper, even, pltpu.roll(odd, FR, 1))
    high = jnp.where(upper, pltpu.roll(even, FR, 1), odd)
    blocks = (value.shape[0] // (PAIR * ROWS), ROWS, size)
    return low.reshape(blocks), high.reshape(blocks)


def build_keep(start, width, keep):
    position = lax.broadcasted_iota(jnp.int32, (LEN, LANES), 0)
    for u in range(start.shape[1]):
        outside = None
        for m in range(start.shape[0]):
            first = start[m, u]
            here = (position < first) | (position >= first + width[m, u])
            outside = here if outside is None else outside & here
        keep[pl.ds(u * LEN, LEN), :] = jnp.where(outside, 1.0, 0.0).astype(bf16)


def apply_mask(source, target, keep, q):
    rows = pl.ds(q * (source.shape[0] // CHUNKS), source.shape[0] // CHUNKS)
    for j in range(GT):
        view = (rows, pl.ds(j * LANES, LANES))
        target[view] = source[view] * keep[rows, :]


def fetch(source, target, sems):
    rows = source.shape[0] // CHUNKS
    return [
        pltpu.make_async_copy(source.at[pl.ds(q * rows, rows)], target.at[pl.ds(q * rows, rows)], sems.at[q])
        for q in range(CHUNKS)
    ]


def fetch_picked(pick, xk, xv, target, sems):
    @pl.when(pick == 0)
    def _():
        for copy in fetch(xk, target, sems):
            copy.start()

    @pl.when(pick != 0)
    def _():
        for copy in fetch(xv, target, sems):
            copy.start()

    return fetch(xk, target, sems)


BLOCK = 256


def put(out, r, value, begin):
    places = pl.ds(r * (BLOCK // BLK), BLOCK // BLK)
    for half, rows in enumerate(arrange(value)):
        for j in range(value.shape[1] // LANES):
            out[places, half, pl.ds(begin + j * ROWS, ROWS), :] = rows[:, :, j * LANES : (j + 1) * LANES].astype(bf16)


def put_folded(out, r, value, begin):
    places = pl.ds(r * (BLOCK // BLK), BLOCK // BLK)
    for half, rows in enumerate(arrange(value)):
        upper, lower = rows[:, : ROWS // 2], pltpu.roll(rows[:, ROWS // 2 :], LANES // 2, 2)
        lane = lax.broadcasted_iota(jnp.int32, upper.shape, 2)
        out[places, half, pl.ds(begin, ROWS // 2), :] = jnp.where(lane < LANES // 2, upper, lower).astype(bf16)


def end_lanes(value):
    lane = lax.broadcasted_iota(jnp.int32, value.shape, 1)
    return jnp.where(lane < BLK, value, 0.0)


def circulate(value, r):
    rows = []
    for b in range(BLOCK // BLK):
        shift = (D - BLK * (r * (BLOCK // BLK) + b)) % D
        piece = value[b * BLK : (b + 1) * BLK]
        rows.append(pltpu.roll(piece, shift, 1) if shift else piece)
    return [jnp.concatenate([p[:, t * LANES : (t + 1) * LANES] for p in rows], axis=0) for t in range(3)]


def zero_grams(pick, x0, out, spare):
    lefts, rests = [], []
    for r in range(D // BLOCK):
        lefts.append(x0[:, pl.ds(r * BLOCK, BLOCK)].T)
        tiles = circulate(dot(lefts[r], x0[...]), r)
        put(out, r, jnp.where(pick == 0, tiles[0], tiles[1]), F0)
        put(spare, r, jnp.where(pick == 0, tiles[1], tiles[0]), 0)
        last = pltpu.roll(end_lanes(tiles[2]), BLK, 1)
        rests.append(jnp.where(pick == 0, 0.0, last))
        put_folded(spare, r, jnp.where(pick == 0, last, 0.0), ROWS)
    return lefts, rests


def picked_grams(lefts, x1, keep, rests, out, end):
    for r in range(D // BLOCK):
        put(out, r, dot(lefts[r], x1[...]), 0)
    wide = jnp.concatenate([keep[...]] * (BLOCK // LANES), axis=1)
    for r in range(D // BLOCK):
        left = (x1[:, pl.ds(r * BLOCK, BLOCK)] * wide).T
        tiles = circulate(dot(left, x1[...]), r)
        put(out, r, jnp.concatenate(tiles[:2], axis=1), FA)
        last = end_lanes(tiles[2])
        put_folded(out, r, last if rests is None else last + rests[r], end)


def theirs_kernel(
    core, start, width, x0, xk, xv, out, spare, kept, keep, ahead, buf0, buf1, starts, widths, sem0, sem1, sem2, sem3
):
    pick = 1 - core[0]
    small = [pltpu.make_async_copy(v, w, sem2.at[i]) for i, (v, w) in enumerate(((start, starts), (width, widths)))]
    copies0 = fetch(x0, buf0, sem0)
    for copy in small + copies0:
        copy.start()
    for copy in small:
        copy.wait()
    build_keep(starts, widths, keep)
    for q in range(CHUNKS):
        copies0[q].wait()
        if q == 0:
            copies1 = fetch_picked(pick, xk, xv, buf1, sem1)
        apply_mask(buf0, kept, keep, q)
    lefts, rests = zero_grams(pick, kept, out, spare)
    for copy in copies1:
        copy.wait()
    copies2 = fetch_picked(core[0], xk, xv, ahead, sem3)
    picked_grams(lefts, buf1, keep, rests, out, FL)
    for copy in copies2:
        copy.wait()


def mine_kernel(keep, x0, x1, out):
    lefts = [x0[:, pl.ds(r * BLOCK, BLOCK)].T for r in range(D // BLOCK)]
    picked_grams(lefts, x1, keep, None, out, F0)


PIECES = 4


def add_kernel(mine, spare, received, out, buf, sems):
    size = NXY // PIECES
    copies = []
    main, zero, last = slice(0, F0), slice(F0, FL), slice(FL, WROWS)
    for q in range(PIECES):
        for i in range(q * size, (q + 1) * size):
            for j in range(PAIR):
                buf[i, j, main] = mine[i, j, main] + received[i, j, main]
                buf[i, j, zero] = spare[i, j, :ROWS] + received[i, j, zero]
                ends = mine[i, j, F0:] + spare[i, j, ROWS:]
                buf[i, j, last] = ends + received[i, j, last]
        part = pl.ds(q * size, size)
        copies.append(pltpu.make_async_copy(buf.at[part], out.at[part], sems.at[q]))
        copies[q].start()
    for copy in copies:
        copy.wait()


def lam_kernel(
    share, core, chip, _, keep, x0, xk, xv, bases, keep_lam, send_lam, basis_in_t, mirror, basis_out, rows_in, b0, b1, b2, sem0, sem1, sem2
):
    c = core[0]
    bufs = (b0, b1, b2)
    copies = [fetch(x, buf, sem) for x, buf, sem in zip((x0, xk, xv), bufs, (sem0, sem1, sem2))]
    for group in copies:
        for copy in group:
            copy.start()
    low, high = arrange(bases[0].astype(f32))
    basis_in_t[...] = jnp.concatenate([low, high], axis=1).reshape(D, D).T.astype(bf16)
    lane = lax.broadcasted_iota(jnp.int32, (LANES, D), 0)
    column = lax.broadcasted_iota(jnp.int32, (LANES, D), 1)
    for half in range(PAIR):
        home = 8 * ((lane >> 2) & 3) + FR * half + (lane & 3) + 2 * D
        for kind in range(2):
            distance = (lane >> 4) + (4 * c if kind else 0)
            there = (home + BLK * ((chip[0] >> 3) - distance)) & (D - 1)
            one = jnp.where(column == there, 1.0, 0.0).astype(bf16)
            mirror[pl.ds((2 * half + kind) * LANES, LANES), :] = one
    basis_out[...] = bases[1 + c]
    row = lax.broadcasted_iota(jnp.int32, (16, D), 0)
    column = lax.broadcasted_iota(jnp.int32, (16, D), 1)
    wanted = (row < FR) & (column == FR * chip[0] + ((row + 2 * c) & (FR - 1)))
    rows_in[...] = dot(jnp.where(wanted, 1.0, 0.0).astype(bf16), bases[0]).astype(bf16)
    lam = []
    for f in range(3):
        total = jnp.zeros((8, D), f32)
        for q in range(CHUNKS):
            copies[f][q].wait()
            apply_mask(bufs[f], bufs[f], keep, q)
        for q in range(bufs[f].shape[0] // BLOCK):
            product = dot(bufs[f][pl.ds(q * BLOCK, BLOCK), :], bases[f])
            total = total + jnp.sum((product * product).reshape(BLOCK // 8, 8, D), axis=0)
        lam.append(jnp.sum(total, axis=0, keepdims=True) * share)
    keep_lam[0:1, :] = lam[0]
    send_lam[0:1, :] = lam[0]
    keep_lam[1:2, :] = jnp.where(c == 0, lam[1], lam[2])
    send_lam[1:2, :] = jnp.where(c == 0, lam[2], lam[1])


def split(value):
    high = value.astype(bf16)
    return high.astype(f32), value - high.astype(f32)


def lam_rows(lam):
    return jnp.concatenate(split(jnp.concatenate([lam[:, j * LANES : (j + 1) * LANES] for j in range(GT)], axis=0)), axis=0)


def add_lam(rows):
    return rows[: 2 * GT] + rows[2 * GT :]


def lam_row(total, index):
    return jnp.concatenate([total[2 * j + index : 2 * j + index + 1] for j in range(GT)], axis=1)


LAMR = 4 * GT
DIRECT = GT * ROWS
TURNED = DIRECT + 4 * FR
DEEP_LAM = TURNED + 16
DEEP_ROWS = DEEP_LAM + LAMR
GATHER_LAM = GT * ROWS
GATHER_TURNED = GATHER_LAM + 2 * GT
GATHER_ROWS = GATHER_TURNED + 8


def pack_kernel(parts, keep_lam, send_lam, out):
    total = parts[0].astype(f32)
    for i in range(1, WIDE):
        total = total + parts[i].astype(f32)
    lam = lam_rows(keep_lam[...] + send_lam[...]).astype(bf16)
    for j in range(GT):
        tile = total[j * ROWS : (j + 1) * ROWS].astype(bf16)
        for k in range(DEEP):
            out[k, pl.ds(j * ROWS, ROWS), :] = tile
    near, mid, zero = total[FA : FA + ROWS], total[FA + ROWS : F0], total[F0:FL]
    last = total[FL:]
    last = jnp.concatenate([last, pltpu.roll(last, LANES // 2, 1)], axis=0)
    empty = jnp.zeros((LANES - ROWS, LANES), f32)
    turned = [jnp.concatenate([v, empty], axis=0).T for v in (near, mid, zero)]
    for k in range(DEEP):
        rows = slice(k * FR, (k + 1) * FR)
        direct = jnp.concatenate([v[rows] for v in (near, mid, zero, last)], axis=0)
        out[k, pl.ds(DIRECT, 4 * FR), :] = direct.astype(bf16)

        def pieces(sources):
            result = None
            for n in range(4 * len(sources)):
                piece = sources[n // 4][(n % 4) * BLK + 8 * k : (n % 4) * BLK + 8 * k + 8]
                piece = pltpu.roll(piece, ROWS * n, 1) if n else piece
                result = piece if result is None else result + piece
            return result

        mirrored = jnp.concatenate([pieces(turned[:2]), pieces(turned[2:])], axis=0)
        out[k, pl.ds(TURNED, 16), :] = mirrored.astype(bf16)
        out[k, pl.ds(DEEP_LAM, LAMR), :] = lam


def deep_total(got):
    total = got[0].astype(f32)
    for i in range(1, DEEP):
        total = total + got[i].astype(f32)
    return total, jnp.concatenate([total[j * ROWS : (j + 1) * ROWS] for j in range(GT)], axis=1)


def rotate_kernel(got, basis, out):
    total, grad = deep_total(got)
    rot = dot(grad.astype(bf16), basis[...]).astype(bf16)
    lam = add_lam(total[DEEP_LAM:])
    picked, zero = total[TURNED : TURNED + 8], total[TURNED + 8 : TURNED + 16]
    for half in range(PAIR):
        rows = slice(half * FR, (half + 1) * FR)
        tail = jnp.concatenate([lam, picked[rows], zero[rows]], axis=0).astype(bf16)
        for i in range(half, WIDE, PAIR):
            out[i, pl.ds(GATHER_LAM, ROWS), :] = tail
    for j in range(GT):
        tile = rot[:, j * LANES : (j + 1) * LANES]
        for i in range(WIDE):
            out[i, pl.ds(j * ROWS, ROWS), :] = tile


def direct_rows(k, c, block, got):
    total, grad = deep_total(got)
    rows = grad[0:FR]
    for other in range(1, DEEP):
        rows = jnp.where(k == other, grad[other * FR : (other + 1) * FR], rows)
    near, mid, zero, last = [total[DIRECT + t * FR : DIRECT + (t + 1) * FR] for t in range(4)]
    lane = lax.broadcasted_iota(jnp.int32, last.shape, 1)
    none = jnp.zeros_like(last)
    end = jnp.where(lane < BLK, last, none)
    end0 = jnp.where(lane < BLK, pltpu.roll(last, LANES - BLK, 1), none)
    picked = jnp.concatenate([near, mid, end, none], axis=1)
    zero = jnp.where(
        c == 0,
        jnp.concatenate([zero, none, none, none], axis=1),
        jnp.concatenate([none, zero, end0, none], axis=1),
    )
    return rows, pltpu.roll(jnp.concatenate([picked, zero], axis=0), BLK * block, 1)


def mirrored_rows(c, block, tails, mirror):
    row = lax.broadcasted_iota(jnp.int32, (8, LANES), 0)
    group = (lax.broadcasted_iota(jnp.int32, (8, LANES), 1) >> 4) + jnp.where(row >= FR, 4 * c, 0)
    parts = []
    for half in range(PAIR):
        own = jnp.zeros((8, LANES), f32)
        for i in range(NXY):
            distance = (block - i) & (NXY - 1)
            wanted = jnp.where((distance >= 1) & (distance < 8), distance, -1)
            own = jnp.where(group == wanted, tails[PAIR * i + half][8:], own)
        parts += [jnp.where(row < FR, own, 0.0), jnp.where(row < FR, 0.0, own)]
    return dot(jnp.concatenate(parts, axis=1).astype(bf16), mirror[...])


def solve_kernel(core, chip, got, packed, basis_in_t, basis_out, rows_in, mirror, own, their, scaled):
    tails = [got[i, pl.ds(GATHER_LAM, ROWS), :].astype(f32) for i in range(WIDE)]
    lam = tails[0][:8]
    for tail in tails[1:]:
        lam = lam + tail[:8]
    column = jnp.broadcast_to(lam_row(lam, 0), (8, D)).T[:, 0:1]
    column = jnp.broadcast_to(column, (D, LANES))
    curve = jnp.zeros((8, LANES), f32)
    for j in range(GT):
        rot = got[:, pl.ds(j * ROWS, ROWS), :].reshape(D, LANES)
        rotated = dot(basis_in_t[...], rot)
        low = (rotated / (column * lam[2 * j + 1 : 2 * j + 2] + damping)).astype(bf16)
        scaled[:, pl.ds(j * LANES, LANES)] = low
        curve = curve + jnp.sum((low.astype(f32) * rotated).reshape(D // 8, 8, LANES), axis=0)
    curve = jnp.sum(jnp.sum(curve, axis=1, keepdims=True), axis=0, keepdims=True)
    back = dot(rows_in[...], scaled[...]).astype(bf16)
    prec = lax.dot_general(back, basis_out[...], (((1,), (1,)), ((), ())), preferred_element_type=f32)
    prec = prec.astype(bf16).astype(f32)
    curve = jnp.broadcast_to(curve, (2, D))
    rows, factors = direct_rows((chip[0] & (NZ - 1)) >> 1, core[0], chip[0] >> 3, packed)
    factors = factors + mirrored_rows(core[0], chip[0] >> 3, tails, mirror)
    low = jnp.concatenate([rows[0:2], factors[0:2], factors[4:6]], axis=0)
    high = jnp.concatenate([rows[2:4], factors[2:4], factors[6:8]], axis=0)
    first = core[0] == 0
    pad = jnp.zeros((6, D), f32)
    own[...] = jnp.concatenate([prec[0:2], curve, jnp.where(first, low, high), pad], axis=0)
    their[...] = jnp.concatenate([prec[2:4], curve, jnp.where(first, high, low), pad], axis=0)


def finish_kernel(scale, core, own, got, old, new_factors, gradients, updates):
    first = core[0] == 0
    curve = own[2:3, :] + got[2:3, :]
    factor = jnp.sqrt(kl_clip / (learn_rate * learn_rate * curve))
    side0 = jnp.where(first, own[...], got[...])
    side1 = jnp.where(first, got[...], own[...])
    updates[0] = (side0[0:2] * factor).astype(bf16)
    updates[1] = (side1[0:2] * factor).astype(bf16)
    gradients[:, 0, :] = side0[4:6]
    gradients[:, 1, :] = side1[4:6]
    batch = (side0[8:10] + side1[8:10], side0[6:8], side1[6:8])
    for f in range(3):
        new_factors[f] = decay * old[f] + scale * batch[f]


def exchange(value, groups):
    return lax.all_to_all(value, "dp", 0, 0, axis_index_groups=groups, tiled=True)


def body(activations, grad_key, grad_value, time_start, time_width, bases, old_factors):
    index = lax.axis_index("dp").astype(jnp.int32)
    core = index & (NC - 1)
    first = core == 0
    here = (core[None], (index >> 1)[None])
    tokens_here = activations.shape[0]
    share = (1.0 - decay) / (tokens_here * lax.axis_size("dp"))

    def in_hbm(value):
        return pltpu.with_memory_space_constraint(value, pltpu.HBM)

    masks = (in_hbm(time_start.T), in_hbm(time_width.T))
    frames, keys, vals = in_hbm(activations), in_hbm(grad_key), in_hbm(grad_value)
    mask_buf = pltpu.SMEM(time_start.shape[::-1], jnp.int32)
    buf = pltpu.VMEM((tokens_here, D), bf16)
    sems = pltpu.SemaphoreType.DMA((CHUNKS,))
    pair = pltpu.SemaphoreType.DMA((2,))
    partial = shape((NXY, PAIR, WROWS, LANES), bf16)
    work = 6 * D * D * tokens_here
    with jax.named_scope("grams_theirs"):
        other, spare, kept, keep, ahead = call(
            theirs_kernel,
            (
                partial,
                shape((NXY, PAIR, ROWS + ROWS // 2, LANES), bf16),
                shape((tokens_here, D), bf16),
                shape((tokens_here, LANES), bf16),
                shape((tokens_here, D), bf16),
            ),
            [SMEM] + [HBM] * 5,
            [buf, buf, mask_buf, mask_buf, sems, sems, pair, sems],
            flops=work,
            moved=4 * MB,
        )(core[None], *masks, frames, keys, vals)
    received = lax.ppermute(other, "dp", SWAP)
    with jax.named_scope("grams_mine"):
        mine = call(
            mine_kernel,
            shape((NXY, PAIR, F0 + ROWS // 2, LANES), bf16),
            [VMEM] * 3,
            flops=work,
            moved=4 * MB,
        )(keep, kept, ahead)
    with jax.named_scope("chip_sum"):
        chip = call(
            add_kernel,
            pltpu.HBM(partial.shape, bf16),
            [VMEM] * 3,
            [pltpu.VMEM(partial.shape, bf16), pltpu.SemaphoreType.DMA((PIECES,))],
        )(mine, spare, received).reshape(WIDE, WROWS, LANES)
    with jax.named_scope("wide_sum"):
        parts = exchange(chip, WIDE_GROUPS)

    lam_shape, square = shape((2, D), f32), shape((D, D), bf16)
    with jax.named_scope("lam"):
        keep_lam, send_lam, basis_in_t, mirror, basis_out, rows_in = call(
            functools.partial(lam_kernel, share),
            (lam_shape, lam_shape, square, square, square, shape((16, D), bf16)),
            [SMEM, SMEM, HBM, VMEM, HBM, HBM, HBM, VMEM],
            [buf] * 3 + [sems] * 3,
            flops=work,
            moved=4 * MB,
        )(*here, in_hbm(chip), keep, frames, keys, vals, bases)
    old_lam = []
    my_rows = lax.dynamic_slice_in_dim(bases, 2 * index, 2, 1).astype(f32)
    for f in range(3):
        old_image = jnp.dot(old_factors[:, f, :], bases[f].astype(f32), precision=lax.Precision.HIGHEST)
        old_lam.append(decay * jnp.sum(my_rows[f] * old_image, axis=0))
    keep_lam = keep_lam + jnp.stack([old_lam[0], jnp.where(first, old_lam[1], old_lam[2])])
    send_lam = send_lam + jnp.stack([old_lam[0], jnp.where(first, old_lam[2], old_lam[1])])
    sent_lam = lax.ppermute(send_lam, "dp", SWAP)

    with jax.named_scope("pack"):
        packed = call(pack_kernel, shape((DEEP, DEEP_ROWS, LANES), bf16), [VMEM] * 3)(parts, keep_lam, sent_lam)
    with jax.named_scope("deep_sum"):
        got = exchange(packed, DEEP_GROUPS)
    lines = shape((16, D), f32)
    with jax.named_scope("rotate"):
        spread = call(rotate_kernel, shape((WIDE, GATHER_ROWS, LANES), bf16), [VMEM] * 2)(got, basis_out)
    with jax.named_scope("gather"):
        gathered = exchange(spread, WIDE_GROUPS)
    with jax.named_scope("solve"):
        own, their = call(solve_kernel, (lines, lines), [SMEM] * 2 + [VMEM] * 6, [pltpu.VMEM((D, D), bf16)])(
            *here, gathered, got, basis_in_t, basis_out, rows_in, mirror
        )
    theirs = lax.ppermute(their, "dp", SWAP)
    with jax.named_scope("finish"):
        new_factors, gradients, updates = call(
            functools.partial(finish_kernel, share),
            (shape((3, 2, D), f32), shape((2, 2, D), f32), shape((2, 2, D), bf16)),
            [SMEM] + [VMEM] * 3,
        )(core[None], own, theirs, jnp.transpose(old_factors, (1, 0, 2)))
    return (jnp.transpose(new_factors, (1, 0, 2)), gradients, updates)


def solution(mesh):
    in_specs = (
        P("dp", None),
        P("dp", None),
        P("dp", None),
        P("dp", None),
        P("dp", None),
        P(),
        P("dp", None, None),
    )
    out_specs = (P("dp", None, None), P("dp", None, None), P(None, "dp", None))
    return jax.shard_map(body, mesh=mesh, in_specs=in_specs, out_specs=out_specs, check_vma=False)
```

```python
import functools

import jax
import jax.numpy as jnp
from jax import lax
from jax.experimental import pallas as pl
from jax.experimental.pallas import tpu as pltpu
from jax.sharding import PartitionSpec as P

LEN = 128
NX, NY, NZ, NC = 4, 4, 8, 2
NXY = NX * NY
D = 512
HALF = D // 2
PAIR = 2
WIDE = NXY * PAIR
DEEP = NZ // PAIR
ROWS = D // WIDE
LANES = 128
FR = ROWS // DEEP
GT = D // LANES
BLK = D // NXY
FA, F0, FL = GT * ROWS, (GT + 2) * ROWS, (GT + 3) * ROWS
WROWS = FL + ROWS // 2
MB = 1 << 20

decay = 0.8
damping = 0.001
kl_clip = 0.001
learn_rate = 7e-05

f32, bf16 = jnp.float32, jnp.bfloat16


def device(xy, z, c):
    return (xy * NZ + z) * NC + c


SWAP = [(d, d ^ 1) for d in range(NXY * NZ * NC)]
WIDE_GROUPS = [
    [device(i, k * PAIR + l, c) for i in range(NXY) for l in range(PAIR)]
    for k in range(DEEP)
    for c in range(NC)
]
DEEP_GROUPS = [
    [device(i, k * PAIR + l, c) for k in range(DEEP)] for i in range(NXY) for l in range(PAIR) for c in range(NC)
]
VMEM = pl.BlockSpec(memory_space=pltpu.VMEM)
SMEM = pl.BlockSpec(memory_space=pltpu.SMEM)
HBM = pl.BlockSpec(memory_space=pltpu.HBM)
CHUNKS = 2


def call(kernel, outs, in_specs, scratch=(), limit=16, flops=0, moved=0):
    return pl.pallas_call(
        kernel,
        out_shape=outs,
        in_specs=in_specs,
        out_specs=jax.tree.map(lambda out: HBM if isinstance(out, pl.MemoryRef) else VMEM, outs),
        scratch_shapes=list(scratch),
        compiler_params=pltpu.CompilerParams(vmem_limit_bytes=limit * MB),
        cost_estimate=pl.CostEstimate(flops=flops, bytes_accessed=moved, transcendentals=0),
    )


def shape(dims, dtype):
    return jax.ShapeDtypeStruct(dims, dtype)


def dot(a, b):
    return jnp.dot(a, b, preferred_element_type=f32)


def arrange(value):
    size = value.shape[1]
    pairs = value.reshape(value.shape[0] // 16, 2, 8, size)
    even, odd = pairs[:, 0], pairs[:, 1]
    upper = lax.broadcasted_iota(jnp.int32, even.shape, 1) < FR
    low = jnp.where(upper, even, pltpu.roll(odd, FR, 1))
    high = jnp.where(upper, pltpu.roll(even, FR, 1), odd)
    blocks = (value.shape[0] // (PAIR * ROWS), ROWS, size)
    return low.reshape(blocks), high.reshape(blocks)


def build_keep(start, width, keep):
    position = lax.broadcasted_iota(jnp.int32, (LEN, LANES), 0)
    for u in range(start.shape[1]):
        outside = None
        for m in range(start.shape[0]):
            first = start[m, u]
            here = (position < first) | (position >= first + width[m, u])
            outside = here if outside is None else outside & here
        keep[pl.ds(u * LEN, LEN), :] = jnp.where(outside, 1.0, 0.0).astype(bf16)


def apply_mask(source, target, keep, q):
    rows = pl.ds(q * (source.shape[0] // CHUNKS), source.shape[0] // CHUNKS)
    for j in range(GT):
        view = (rows, pl.ds(j * LANES, LANES))
        target[view] = source[view] * keep[rows, :]


def fetch(source, target, sems):
    rows = source.shape[0] // CHUNKS
    return [
        pltpu.make_async_copy(source.at[pl.ds(q * rows, rows)], target.at[pl.ds(q * rows, rows)], sems.at[q])
        for q in range(CHUNKS)
    ]


def fetch_picked(pick, xk, xv, target, sems):
    @pl.when(pick == 0)
    def _():
        for copy in fetch(xk, target, sems):
            copy.start()

    @pl.when(pick != 0)
    def _():
        for copy in fetch(xv, target, sems):
            copy.start()

    return fetch(xk, target, sems)


BLOCK = 256


def put(out, r, value, begin):
    places = pl.ds(r * (BLOCK // BLK), BLOCK // BLK)
    for half, rows in enumerate(arrange(value)):
        for j in range(value.shape[1] // LANES):
            out[places, half, pl.ds(begin + j * ROWS, ROWS), :] = rows[:, :, j * LANES : (j + 1) * LANES].astype(bf16)


def put_folded(out, r, value, begin):
    places = pl.ds(r * (BLOCK // BLK), BLOCK // BLK)
    for half, rows in enumerate(arrange(value)):
        upper, lower = rows[:, : ROWS // 2], pltpu.roll(rows[:, ROWS // 2 :], LANES // 2, 2)
        lane = lax.broadcasted_iota(jnp.int32, upper.shape, 2)
        out[places, half, pl.ds(begin, ROWS // 2), :] = jnp.where(lane < LANES // 2, upper, lower).astype(bf16)


def end_lanes(value):
    lane = lax.broadcasted_iota(jnp.int32, value.shape, 1)
    return jnp.where(lane < BLK, value, 0.0)


def circulate(value, r):
    rows = []
    for b in range(BLOCK // BLK):
        shift = (D - BLK * (r * (BLOCK // BLK) + b)) % D
        piece = value[b * BLK : (b + 1) * BLK]
        rows.append(pltpu.roll(piece, shift, 1) if shift else piece)
    return [jnp.concatenate([p[:, t * LANES : (t + 1) * LANES] for p in rows], axis=0) for t in range(3)]


def zero_grams(pick, x0, out, spare, full):
    lefts, rests = [], []
    for r in range(D // BLOCK):
        lefts.append(x0[:, pl.ds(r * BLOCK, BLOCK)].T)
        value = dot(lefts[r], x0[...])
        full[pl.ds(r * BLOCK, BLOCK), :] = value.astype(bf16)
        tiles = circulate(value, r)
        put(out, r, jnp.where(pick == 0, tiles[0], tiles[1]), F0)
        put(spare, r, jnp.where(pick == 0, tiles[1], tiles[0]), 0)
        last = pltpu.roll(end_lanes(tiles[2]), BLK, 1)
        rests.append(jnp.where(pick == 0, 0.0, last))
        put_folded(spare, r, jnp.where(pick == 0, last, 0.0), ROWS)
    return lefts, rests


def picked_grams(lefts, x1, keep, rests, out, end, full):
    for r in range(D // BLOCK):
        put(out, r, dot(lefts[r], x1[...]), 0)
    wide = jnp.concatenate([keep[...]] * (BLOCK // LANES), axis=1)
    for r in range(D // BLOCK):
        left = (x1[:, pl.ds(r * BLOCK, BLOCK)] * wide).T
        value = dot(left, x1[...])
        full[pl.ds(r * BLOCK, BLOCK), :] = value.astype(bf16)
        tiles = circulate(value, r)
        put(out, r, jnp.concatenate(tiles[:2], axis=1), FA)
        last = end_lanes(tiles[2])
        put_folded(out, r, last if rests is None else last + rests[r], end)


def make_mirror(c, chip, mirror):
    lane = lax.broadcasted_iota(jnp.int32, (LANES, D), 0)
    column = lax.broadcasted_iota(jnp.int32, (LANES, D), 1)
    for half in range(PAIR):
        home = 8 * ((lane >> 2) & 3) + FR * half + (lane & 3) + 2 * D
        for kind in range(2):
            distance = (lane >> 4) + (4 * c if kind else 0)
            there = (home + BLK * ((chip >> 3) - distance)) & (D - 1)
            one = jnp.where(column == there, 1.0, 0.0).astype(bf16)
            mirror[pl.ds((2 * half + kind) * LANES, LANES), :] = one


def theirs_kernel(
    core, chip, start, width, x0, xk, xv, bases, out, spare, kept, keep, ahead, full0, full1, mirror, bases_here,
    buf0, buf1, starts, widths, sem0, sem1, sem2, sem3, sem4
):
    pick = 1 - core[0]
    small = [pltpu.make_async_copy(v, w, sem2.at[i]) for i, (v, w) in enumerate(((start, starts), (width, widths)))]
    copies0 = fetch(x0, buf0, sem0)
    for copy in small + copies0:
        copy.start()
    make_mirror(core[0], chip[0], mirror)
    for copy in small:
        copy.wait()
    build_keep(starts, widths, keep)
    for q in range(CHUNKS):
        copies0[q].wait()
        if q == 0:
            copies1 = fetch_picked(pick, xk, xv, buf1, sem1)
        apply_mask(buf0, kept, keep, q)
    lefts, rests = zero_grams(pick, kept, out, spare, full0)
    for copy in copies1:
        copy.wait()
    copies2 = fetch_picked(core[0], xk, xv, ahead, sem3)
    fetched = pltpu.make_async_copy(bases, bases_here, sem4)
    fetched.start()
    picked_grams(lefts, buf1, keep, rests, out, FL, full1)
    for copy in copies2:
        copy.wait()
    fetched.wait()


def basis_values(share, full, basis, old, picked):
    high = old.astype(bf16).astype(f32)
    mid = (old - high).astype(bf16).astype(f32)
    row = lax.broadcasted_iota(jnp.int32, (8, D), 0)
    column = lax.broadcasted_iota(jnp.int32, (8, D), 1)
    chosen = jnp.zeros((8, D), f32)
    for r, index in enumerate(picked):
        chosen = jnp.where((row == r) & (column == index), 1.0, chosen)
    extra = jnp.concatenate([high, mid, old - high - mid, jnp.zeros((2, D), f32), chosen], axis=0).astype(bf16)
    image = dot(full[...], basis)
    more = dot(extra, basis)
    batch = jnp.sum(basis.astype(f32) * image, axis=0, keepdims=True)
    old_image = more[0:2] + more[2:4] + more[4:6]
    return batch * share + decay * jnp.sum(more[8:10] * old_image, axis=0, keepdims=True), more[8:]


def mine_kernel(
    share, core, chip, keep, x0, x1, full0, full1, bases, old, out, keep_lam, send_lam, basis_in_t, rows_in, full
):
    c, first_row = core[0], FR * chip[0]
    lefts = [x0[:, pl.ds(r * BLOCK, BLOCK)].T for r in range(D // BLOCK)]
    picked_grams(lefts, x1, keep, None, out, F0, full)
    low, high = arrange(bases[0].astype(f32))
    basis_in_t[...] = jnp.concatenate([low, high], axis=1).reshape(D, D).T.astype(bf16)
    own = [first_row + 2 * c, first_row + 2 * c + 1]
    rest = [first_row + 2 * (1 - c), first_row + 2 * (1 - c) + 1]
    lam0, rows = basis_values(share, full0, bases[0], old[0], own + rest)
    rows_in[...] = jnp.concatenate([rows, jnp.zeros((8, D), f32)], axis=0).astype(bf16)
    keep_lam[0:1, :] = lam0
    send_lam[0:1, :] = lam0
    keep_lam[1:2, :] = basis_values(share, full, bases[1 + c], old[1 + c], own)[0]
    send_lam[1:2, :] = basis_values(share, full1, bases[2 - c], old[2 - c], own)[0]


def add_kernel(mine, spare, received, out):
    main, zero, last = slice(0, F0), slice(F0, FL), slice(FL, WROWS)
    for i in range(NXY):
        for j in range(PAIR):
            out[i, j, main] = mine[i, j, main] + received[i, j, main]
            out[i, j, zero] = spare[i, j, :ROWS] + received[i, j, zero]
            out[i, j, last] = mine[i, j, F0:] + spare[i, j, ROWS:] + received[i, j, last]


def split(value):
    high = value.astype(bf16)
    return high.astype(f32), value - high.astype(f32)


def lam_rows(lam):
    return jnp.concatenate(split(jnp.concatenate([lam[:, j * LANES : (j + 1) * LANES] for j in range(GT)], axis=0)), axis=0)


def add_lam(rows):
    return rows[: 2 * GT] + rows[2 * GT :]


def lam_row(total, index):
    return jnp.concatenate([total[2 * j + index : 2 * j + index + 1] for j in range(GT)], axis=1)


LAMR = 4 * GT
DIRECT = GT * ROWS
TURNED = DIRECT + 4 * FR
DEEP_LAM = TURNED + 16
DEEP_ROWS = DEEP_LAM + LAMR
GATHER_LAM = GT * ROWS
GATHER_TURNED = GATHER_LAM + 2 * GT
GATHER_ROWS = GATHER_TURNED + 8


def pack_kernel(parts, keep_lam, send_lam, out):
    total = parts[0].astype(f32)
    for i in range(1, WIDE):
        total = total + parts[i].astype(f32)
    lam = lam_rows(keep_lam[...] + send_lam[...]).astype(bf16)
    for j in range(GT):
        tile = total[j * ROWS : (j + 1) * ROWS].astype(bf16)
        for k in range(DEEP):
            out[k, pl.ds(j * ROWS, ROWS), :] = tile
    near, mid, zero = total[FA : FA + ROWS], total[FA + ROWS : F0], total[F0:FL]
    last = total[FL:]
    last = jnp.concatenate([last, pltpu.roll(last, LANES // 2, 1)], axis=0)
    empty = jnp.zeros((LANES - ROWS, LANES), f32)
    turned = [jnp.concatenate([v, empty], axis=0).T for v in (near, mid, zero)]
    for k in range(DEEP):
        rows = slice(k * FR, (k + 1) * FR)
        direct = jnp.concatenate([v[rows] for v in (near, mid, zero, last)], axis=0)
        out[k, pl.ds(DIRECT, 4 * FR), :] = direct.astype(bf16)

        def pieces(sources):
            result = None
            for n in range(4 * len(sources)):
                piece = sources[n // 4][(n % 4) * BLK + 8 * k : (n % 4) * BLK + 8 * k + 8]
                piece = pltpu.roll(piece, ROWS * n, 1) if n else piece
                result = piece if result is None else result + piece
            return result

        mirrored = jnp.concatenate([pieces(turned[:2]), pieces(turned[2:])], axis=0)
        out[k, pl.ds(TURNED, 16), :] = mirrored.astype(bf16)
        out[k, pl.ds(DEEP_LAM, LAMR), :] = lam


def deep_total(got):
    total = got[0].astype(f32)
    for i in range(1, DEEP):
        total = total + got[i].astype(f32)
    return total, jnp.concatenate([total[j * ROWS : (j + 1) * ROWS] for j in range(GT)], axis=1)


def rotate_kernel(core, got, bases, out):
    total, grad = deep_total(got)
    rot = dot(grad.astype(bf16), bases[1 + core[0]]).astype(bf16)
    lam = add_lam(total[DEEP_LAM:])
    picked, zero = total[TURNED : TURNED + 8], total[TURNED + 8 : TURNED + 16]
    for half in range(PAIR):
        rows = slice(half * FR, (half + 1) * FR)
        tail = jnp.concatenate([lam, picked[rows], zero[rows]], axis=0).astype(bf16)
        for i in range(half, WIDE, PAIR):
            out[i, pl.ds(GATHER_LAM, ROWS), :] = tail
    for j in range(GT):
        tile = rot[:, j * LANES : (j + 1) * LANES]
        for i in range(WIDE):
            out[i, pl.ds(j * ROWS, ROWS), :] = tile


def direct_rows(k, c, block, got):
    total, grad = deep_total(got)
    rows = grad[0:FR]
    for other in range(1, DEEP):
        rows = jnp.where(k == other, grad[other * FR : (other + 1) * FR], rows)
    near, mid, zero, last = [total[DIRECT + t * FR : DIRECT + (t + 1) * FR] for t in range(4)]
    lane = lax.broadcasted_iota(jnp.int32, last.shape, 1)
    none = jnp.zeros_like(last)
    end = jnp.where(lane < BLK, last, none)
    end0 = jnp.where(lane < BLK, pltpu.roll(last, LANES - BLK, 1), none)
    picked = jnp.concatenate([near, mid, end, none], axis=1)
    zero = jnp.where(
        c == 0,
        jnp.concatenate([zero, none, none, none], axis=1),
        jnp.concatenate([none, zero, end0, none], axis=1),
    )
    return rows, pltpu.roll(jnp.concatenate([picked, zero], axis=0), BLK * block, 1)


def mirrored_rows(c, block, tails, mirror):
    row = lax.broadcasted_iota(jnp.int32, (8, LANES), 0)
    group = (lax.broadcasted_iota(jnp.int32, (8, LANES), 1) >> 4) + jnp.where(row >= FR, 4 * c, 0)
    parts = []
    for half in range(PAIR):
        own = jnp.zeros((8, LANES), f32)
        for i in range(NXY):
            distance = (block - i) & (NXY - 1)
            wanted = jnp.where((distance >= 1) & (distance < 8), distance, -1)
            own = jnp.where(group == wanted, tails[PAIR * i + half][8:], own)
        parts += [jnp.where(row < FR, own, 0.0), jnp.where(row < FR, 0.0, own)]
    return dot(jnp.concatenate(parts, axis=1).astype(bf16), mirror[...])


def solve_kernel(core, chip, got, packed, basis_in_t, bases, rows_in, mirror, own, their, scaled):
    tails = [got[i, pl.ds(GATHER_LAM, ROWS), :].astype(f32) for i in range(WIDE)]
    lam = tails[0][:8]
    for tail in tails[1:]:
        lam = lam + tail[:8]
    column = jnp.broadcast_to(lam_row(lam, 0), (8, D)).T[:, 0:1]
    column = jnp.broadcast_to(column, (D, LANES))
    curve = jnp.zeros((8, LANES), f32)
    for j in range(GT):
        rot = got[:, pl.ds(j * ROWS, ROWS), :].reshape(D, LANES)
        rotated = dot(basis_in_t[...], rot)
        low = (rotated / (column * lam[2 * j + 1 : 2 * j + 2] + damping)).astype(bf16)
        scaled[:, pl.ds(j * LANES, LANES)] = low
        curve = curve + jnp.sum((low.astype(f32) * rotated).reshape(D // 8, 8, LANES), axis=0)
    curve = jnp.sum(jnp.sum(curve, axis=1, keepdims=True), axis=0, keepdims=True)
    back = dot(rows_in[...], scaled[...]).astype(bf16)
    prec = lax.dot_general(back, bases[1 + core[0]], (((1,), (1,)), ((), ())), preferred_element_type=f32)
    prec = prec.astype(bf16).astype(f32)
    curve = jnp.broadcast_to(curve, (2, D))
    rows, factors = direct_rows((chip[0] & (NZ - 1)) >> 1, core[0], chip[0] >> 3, packed)
    factors = factors + mirrored_rows(core[0], chip[0] >> 3, tails, mirror)
    low = jnp.concatenate([rows[0:2], factors[0:2], factors[4:6]], axis=0)
    high = jnp.concatenate([rows[2:4], factors[2:4], factors[6:8]], axis=0)
    first = core[0] == 0
    pad = jnp.zeros((6, D), f32)
    own[...] = jnp.concatenate([prec[0:2], curve, jnp.where(first, low, high), pad], axis=0)
    their[...] = jnp.concatenate([prec[2:4], curve, jnp.where(first, high, low), pad], axis=0)


def finish_kernel(scale, core, own, got, old, new_factors, gradients, updates):
    first = core[0] == 0
    curve = own[2:3, :] + got[2:3, :]
    factor = jnp.sqrt(kl_clip / (learn_rate * learn_rate * curve))
    side0 = jnp.where(first, own[...], got[...])
    side1 = jnp.where(first, got[...], own[...])
    updates[0] = (side0[0:2] * factor).astype(bf16)
    updates[1] = (side1[0:2] * factor).astype(bf16)
    gradients[:, 0, :] = side0[4:6]
    gradients[:, 1, :] = side1[4:6]
    batch = (side0[8:10] + side1[8:10], side0[6:8], side1[6:8])
    for f in range(3):
        new_factors[f] = decay * old[f] + scale * batch[f]


def exchange(value, groups):
    return lax.all_to_all(value, "dp", 0, 0, axis_index_groups=groups, tiled=True)


def body(activations, grad_key, grad_value, time_start, time_width, bases, old_factors):
    index = lax.axis_index("dp").astype(jnp.int32)
    core = index & (NC - 1)
    here = (core[None], (index >> 1)[None])
    tokens_here = activations.shape[0]
    share = (1.0 - decay) / (tokens_here * lax.axis_size("dp"))

    def in_hbm(value):
        return pltpu.with_memory_space_constraint(value, pltpu.HBM)

    masks = (in_hbm(time_start.T), in_hbm(time_width.T))
    frames, keys, vals = in_hbm(activations), in_hbm(grad_key), in_hbm(grad_value)
    mask_buf = pltpu.SMEM(time_start.shape[::-1], jnp.int32)
    buf = pltpu.VMEM((tokens_here, D), bf16)
    sems = pltpu.SemaphoreType.DMA((CHUNKS,))
    pair = pltpu.SemaphoreType.DMA((2,))
    partial = shape((NXY, PAIR, WROWS, LANES), bf16)
    work = 6 * D * D * tokens_here
    square, lam_shape = shape((D, D), bf16), shape((2, D), f32)
    frames_shape = shape((tokens_here, D), bf16)
    old = jnp.transpose(old_factors, (1, 0, 2))
    with jax.named_scope("grams_theirs"):
        other, spare, kept, keep, ahead, full0, full1, mirror, bases_here = call(
            theirs_kernel,
            (
                partial,
                shape((NXY, PAIR, ROWS + ROWS // 2, LANES), bf16),
                frames_shape,
                shape((tokens_here, LANES), bf16),
                frames_shape,
                square,
                square,
                square,
                shape(bases.shape, bf16),
            ),
            [SMEM] * 2 + [HBM] * 6,
            [buf, buf, mask_buf, mask_buf, sems, sems, pair, sems, pltpu.SemaphoreType.DMA],
            limit=20,
            flops=work,
            moved=5 * MB,
        )(*here, *masks, frames, keys, vals, in_hbm(bases))
    received = lax.ppermute(other, "dp", SWAP)
    with jax.named_scope("grams_mine"):
        mine, keep_lam, send_lam, basis_in_t, rows_in = call(
            functools.partial(mine_kernel, share),
            (
                shape((NXY, PAIR, F0 + ROWS // 2, LANES), bf16),
                lam_shape,
                lam_shape,
                square,
                shape((16, D), bf16),
            ),
            [SMEM] * 2 + [VMEM] * 7,
            [pltpu.VMEM((D, D), bf16)],
            limit=20,
            flops=work,
            moved=4 * MB,
        )(*here, keep, kept, ahead, full0, full1, bases_here, old)
    sent_lam = lax.ppermute(send_lam, "dp", SWAP)
    with jax.named_scope("chip_sum"):
        chip = call(add_kernel, partial, [VMEM] * 3)(mine, spare, received).reshape(WIDE, WROWS, LANES)
    with jax.named_scope("wide_sum"):
        parts = exchange(chip, WIDE_GROUPS)
    with jax.named_scope("pack"):
        packed = call(pack_kernel, shape((DEEP, DEEP_ROWS, LANES), bf16), [VMEM] * 3)(parts, keep_lam, sent_lam)
    with jax.named_scope("deep_sum"):
        got = exchange(packed, DEEP_GROUPS)
    lines = shape((16, D), f32)
    with jax.named_scope("rotate"):
        spread = call(rotate_kernel, shape((WIDE, GATHER_ROWS, LANES), bf16), [SMEM] + [VMEM] * 2)(
            here[0], got, bases_here
        )
    with jax.named_scope("gather"):
        gathered = exchange(spread, WIDE_GROUPS)
    with jax.named_scope("solve"):
        own, their = call(solve_kernel, (lines, lines), [SMEM] * 2 + [VMEM] * 6, [pltpu.VMEM((D, D), bf16)])(
            *here, gathered, got, basis_in_t, bases_here, rows_in, mirror
        )
    theirs = lax.ppermute(their, "dp", SWAP)
    with jax.named_scope("finish"):
        new_factors, gradients, updates = call(
            functools.partial(finish_kernel, share),
            (shape((3, 2, D), f32), shape((2, 2, D), f32), shape((2, 2, D), bf16)),
            [SMEM] + [VMEM] * 3,
        )(core[None], own, theirs, old)
    return (jnp.transpose(new_factors, (1, 0, 2)), gradients, updates)


def solution(mesh):
    in_specs = (
        P("dp", None),
        P("dp", None),
        P("dp", None),
        P("dp", None),
        P("dp", None),
        P(),
        P("dp", None, None),
    )
    out_specs = (P("dp", None, None), P("dp", None, None), P(None, "dp", None))
    return jax.shard_map(body, mesh=mesh, in_specs=in_specs, out_specs=out_specs, check_vma=False)
```

```python
import functools

import jax
import jax.numpy as jnp
from jax import lax
from jax.experimental import pallas as pl
from jax.experimental.pallas import tpu as pltpu
from jax.sharding import PartitionSpec as P

LEN = 128
NX, NY, NZ, NC = 4, 4, 8, 2
NXY = NX * NY
D = 512
HALF = D // 2
PAIR = 2
WIDE = NXY * PAIR
DEEP = NZ // PAIR
ROWS = D // WIDE
LANES = 128
FR = ROWS // DEEP
GT = D // LANES
BLK = D // NXY
FA, F0, FL = GT * ROWS, (GT + 2) * ROWS, (GT + 3) * ROWS
WROWS = FL + ROWS // 2
MB = 1 << 20

decay = 0.8
damping = 0.001
kl_clip = 0.001
learn_rate = 7e-05

f32, bf16 = jnp.float32, jnp.bfloat16


def device(xy, z, c):
    return (xy * NZ + z) * NC + c


SWAP = [(d, d ^ 1) for d in range(NXY * NZ * NC)]
WIDE_GROUPS = [
    [device(i, k * PAIR + l, c) for i in range(NXY) for l in range(PAIR)]
    for k in range(DEEP)
    for c in range(NC)
]
DEEP_GROUPS = [
    [device(i, k * PAIR + l, c) for k in range(DEEP)] for i in range(NXY) for l in range(PAIR) for c in range(NC)
]
VMEM = pl.BlockSpec(memory_space=pltpu.VMEM)
SMEM = pl.BlockSpec(memory_space=pltpu.SMEM)
HBM = pl.BlockSpec(memory_space=pltpu.HBM)
CHUNKS = 2


def call(kernel, outs, in_specs, scratch=(), limit=16, flops=0, moved=0):
    return pl.pallas_call(
        kernel,
        out_shape=outs,
        in_specs=in_specs,
        out_specs=jax.tree.map(lambda out: HBM if isinstance(out, pl.MemoryRef) else VMEM, outs),
        scratch_shapes=list(scratch),
        compiler_params=pltpu.CompilerParams(vmem_limit_bytes=limit * MB),
        cost_estimate=pl.CostEstimate(flops=flops, bytes_accessed=moved, transcendentals=0),
    )


def shape(dims, dtype):
    return jax.ShapeDtypeStruct(dims, dtype)


def dot(a, b):
    return jnp.dot(a, b, preferred_element_type=f32)


def arrange(value):
    size = value.shape[1]
    pairs = value.reshape(value.shape[0] // 16, 2, 8, size)
    even, odd = pairs[:, 0], pairs[:, 1]
    upper = lax.broadcasted_iota(jnp.int32, even.shape, 1) < FR
    low = jnp.where(upper, even, pltpu.roll(odd, FR, 1))
    high = jnp.where(upper, pltpu.roll(even, FR, 1), odd)
    blocks = (value.shape[0] // (PAIR * ROWS), ROWS, size)
    return low.reshape(blocks), high.reshape(blocks)


def build_keep(start, width, keep):
    position = lax.broadcasted_iota(jnp.int32, (LEN, LANES), 0)
    for u in range(start.shape[1]):
        outside = None
        for m in range(start.shape[0]):
            first = start[m, u]
            here = (position < first) | (position >= first + width[m, u])
            outside = here if outside is None else outside & here
        keep[pl.ds(u * LEN, LEN), :] = jnp.where(outside, 1.0, 0.0).astype(bf16)


def apply_mask(source, target, keep, q):
    rows = pl.ds(q * (source.shape[0] // CHUNKS), source.shape[0] // CHUNKS)
    for j in range(GT):
        view = (rows, pl.ds(j * LANES, LANES))
        target[view] = source[view] * keep[rows, :]


def fetch(source, target, sems):
    rows = source.shape[0] // CHUNKS
    return [
        pltpu.make_async_copy(source.at[pl.ds(q * rows, rows)], target.at[pl.ds(q * rows, rows)], sems.at[q])
        for q in range(CHUNKS)
    ]


def fetch_picked(pick, xk, xv, target, sems):
    @pl.when(pick == 0)
    def _():
        for copy in fetch(xk, target, sems):
            copy.start()

    @pl.when(pick != 0)
    def _():
        for copy in fetch(xv, target, sems):
            copy.start()

    return fetch(xk, target, sems)


BLOCK = 256


def put(out, r, value, begin):
    places = pl.ds(r * (BLOCK // BLK), BLOCK // BLK)
    for half, rows in enumerate(arrange(value)):
        for j in range(value.shape[1] // LANES):
            out[places, half, pl.ds(begin + j * ROWS, ROWS), :] = rows[:, :, j * LANES : (j + 1) * LANES].astype(bf16)


def put_folded(out, r, value, begin):
    places = pl.ds(r * (BLOCK // BLK), BLOCK // BLK)
    for half, rows in enumerate(arrange(value)):
        upper, lower = rows[:, : ROWS // 2], pltpu.roll(rows[:, ROWS // 2 :], LANES // 2, 2)
        lane = lax.broadcasted_iota(jnp.int32, upper.shape, 2)
        out[places, half, pl.ds(begin, ROWS // 2), :] = jnp.where(lane < LANES // 2, upper, lower).astype(bf16)


def end_lanes(value):
    lane = lax.broadcasted_iota(jnp.int32, value.shape, 1)
    return jnp.where(lane < BLK, value, 0.0)


def circulate(value, r):
    rows = []
    for b in range(BLOCK // BLK):
        shift = (D - BLK * (r * (BLOCK // BLK) + b)) % D
        piece = value[b * BLK : (b + 1) * BLK]
        rows.append(pltpu.roll(piece, shift, 1) if shift else piece)
    return [jnp.concatenate([p[:, t * LANES : (t + 1) * LANES] for p in rows], axis=0) for t in range(3)]


def zero_grams(pick, x0, out, spare, full):
    lefts, rests = [], []
    for r in range(D // BLOCK):
        lefts.append(x0[:, pl.ds(r * BLOCK, BLOCK)].T)
        value = dot(lefts[r], x0[...])
        full[pl.ds(r * BLOCK, BLOCK), :] = value.astype(bf16)
        tiles = circulate(value, r)
        put(out, r, jnp.where(pick == 0, tiles[0], tiles[1]), F0)
        put(spare, r, jnp.where(pick == 0, tiles[1], tiles[0]), 0)
        last = pltpu.roll(end_lanes(tiles[2]), BLK, 1)
        rests.append(jnp.where(pick == 0, 0.0, last))
        put_folded(spare, r, jnp.where(pick == 0, last, 0.0), ROWS)
    return lefts, rests


def gradient_grams(lefts, x1, out):
    for r in range(D // BLOCK):
        put(out, r, dot(lefts[r], x1[...]), 0)


def picked_grams(x1, keep, rests, out, begin, end, full):
    wide = jnp.concatenate([keep[...]] * (BLOCK // LANES), axis=1)
    for r in range(D // BLOCK):
        left = (x1[:, pl.ds(r * BLOCK, BLOCK)] * wide).T
        value = dot(left, x1[...])
        full[pl.ds(r * BLOCK, BLOCK), :] = value.astype(bf16)
        tiles = circulate(value, r)
        put(out, r, jnp.concatenate(tiles[:2], axis=1), begin)
        last = end_lanes(tiles[2])
        put_folded(out, r, last if rests is None else last + rests[r], end)


def make_mirror(c, chip, mirror):
    lane = lax.broadcasted_iota(jnp.int32, (LANES, D), 0)
    column = lax.broadcasted_iota(jnp.int32, (LANES, D), 1)
    for half in range(PAIR):
        home = 8 * ((lane >> 2) & 3) + FR * half + (lane & 3) + 2 * D
        for kind in range(2):
            distance = (lane >> 4) + (4 * c if kind else 0)
            there = (home + BLK * ((chip >> 3) - distance)) & (D - 1)
            one = jnp.where(column == there, 1.0, 0.0).astype(bf16)
            mirror[pl.ds((2 * half + kind) * LANES, LANES), :] = one


def theirs_kernel(
    core, chip, start, width, x0, xk, xv, out, spare, kept, keep, ahead, full0, full1, mirror,
    buf0, buf1, starts, widths, sem0, sem1, sem2, sem3
):
    pick = 1 - core[0]
    small = [pltpu.make_async_copy(v, w, sem2.at[i]) for i, (v, w) in enumerate(((start, starts), (width, widths)))]
    copies0 = fetch(x0, buf0, sem0)
    for copy in small + copies0:
        copy.start()
    make_mirror(core[0], chip[0], mirror)
    for copy in small:
        copy.wait()
    build_keep(starts, widths, keep)
    for q in range(CHUNKS):
        copies0[q].wait()
        if q == 0:
            copies1 = fetch_picked(pick, xk, xv, buf1, sem1)
        apply_mask(buf0, kept, keep, q)
    lefts, rests = zero_grams(pick, kept, out, spare, full0)
    for copy in copies1:
        copy.wait()
    copies2 = fetch_picked(core[0], xk, xv, ahead, sem3)
    gradient_grams(lefts, buf1, out)
    picked_grams(buf1, keep, rests, out, FA, FL, full1)
    for copy in copies2:
        copy.wait()


def basis_values(share, full, basis, old, picked):
    high = old.astype(bf16).astype(f32)
    mid = (old - high).astype(bf16).astype(f32)
    row = lax.broadcasted_iota(jnp.int32, (8, D), 0)
    column = lax.broadcasted_iota(jnp.int32, (8, D), 1)
    chosen = jnp.zeros((8, D), f32)
    for r, index in enumerate(picked):
        chosen = jnp.where((row == r) & (column == index), 1.0, chosen)
    extra = jnp.concatenate([high, mid, old - high - mid, jnp.zeros((2, D), f32), chosen], axis=0).astype(bf16)
    image = dot(full[...], basis)
    more = dot(extra, basis)
    batch = jnp.sum(basis.astype(f32) * image, axis=0, keepdims=True)
    old_image = more[0:2] + more[2:4] + more[4:6]
    return batch * share + decay * jnp.sum(more[8:10] * old_image, axis=0, keepdims=True), more[8:]


def mine_kernel(
    share, core, chip, keep, x1, full0, full1, old, bases_far, out, keep_lam, send_lam, basis_in_t, rows_in, bases, full, sem
):
    fetched = pltpu.make_async_copy(bases_far, bases, sem)
    fetched.start()
    c, first_row = core[0], FR * chip[0]
    picked_grams(x1, keep, None, out, 0, F0 - FA, full)
    fetched.wait()
    low, high = arrange(bases[0].astype(f32))
    basis_in_t[...] = jnp.concatenate([low, high], axis=1).reshape(D, D).T.astype(bf16)
    own = [first_row + 2 * c, first_row + 2 * c + 1]
    rest = [first_row + 2 * (1 - c), first_row + 2 * (1 - c) + 1]
    lam0, rows = basis_values(share, full0, bases[0], old[0], own + rest)
    rows_in[...] = jnp.concatenate([rows, jnp.zeros((8, D), f32)], axis=0).astype(bf16)
    keep_lam[0:1, :] = lam0
    send_lam[0:1, :] = lam0
    keep_lam[1:2, :] = basis_values(share, full, bases[1 + c], old[1 + c], own)[0]
    send_lam[1:2, :] = basis_values(share, full1, bases[2 - c], old[2 - c], own)[0]


def gradient_kernel(x0, x1, out):
    gradient_grams([x0[:, pl.ds(r * BLOCK, BLOCK)].T for r in range(D // BLOCK)], x1, out)


def add_kernel(gradient, picked, spare, received, keep_lam, sent_lam, out, lam):
    first, second, zero, last = slice(0, FA), slice(FA, F0), slice(F0, FL), slice(FL, WROWS)
    for i in range(NXY):
        for j in range(PAIR):
            out[i, j, first] = gradient[i, j] + received[i, j, first]
            out[i, j, second] = picked[i, j, : F0 - FA] + received[i, j, second]
            out[i, j, zero] = spare[i, j, :ROWS] + received[i, j, zero]
            out[i, j, last] = picked[i, j, F0 - FA :] + spare[i, j, ROWS:] + received[i, j, last]
    lam[...] = keep_lam[...] + sent_lam[...]


def split(value):
    high = value.astype(bf16)
    return high.astype(f32), value - high.astype(f32)


def lam_rows(lam):
    return jnp.concatenate(split(jnp.concatenate([lam[:, j * LANES : (j + 1) * LANES] for j in range(GT)], axis=0)), axis=0)


def add_lam(rows):
    return rows[: 2 * GT] + rows[2 * GT :]


def lam_row(total, index):
    return jnp.concatenate([total[2 * j + index : 2 * j + index + 1] for j in range(GT)], axis=1)


LAMR = 4 * GT
DIRECT = GT * ROWS
TURNED = DIRECT + 4 * FR
DEEP_LAM = TURNED + 16
DEEP_ROWS = DEEP_LAM + LAMR
GATHER_LAM = GT * ROWS
GATHER_TURNED = GATHER_LAM + 2 * GT
GATHER_ROWS = GATHER_TURNED + 8


def pack_kernel(parts, lam, out):
    total = parts[0].astype(f32)
    for i in range(1, WIDE):
        total = total + parts[i].astype(f32)
    lam = lam_rows(lam[...]).astype(bf16)
    for j in range(GT):
        tile = total[j * ROWS : (j + 1) * ROWS].astype(bf16)
        for k in range(DEEP):
            out[k, pl.ds(j * ROWS, ROWS), :] = tile
    near, mid, zero = total[FA : FA + ROWS], total[FA + ROWS : F0], total[F0:FL]
    last = total[FL:]
    last = jnp.concatenate([last, pltpu.roll(last, LANES // 2, 1)], axis=0)
    empty = jnp.zeros((LANES - ROWS, LANES), f32)
    turned = [jnp.concatenate([v, empty], axis=0).T for v in (near, mid, zero)]
    for k in range(DEEP):
        rows = slice(k * FR, (k + 1) * FR)
        direct = jnp.concatenate([v[rows] for v in (near, mid, zero, last)], axis=0)
        out[k, pl.ds(DIRECT, 4 * FR), :] = direct.astype(bf16)

        def pieces(sources):
            result = None
            for n in range(4 * len(sources)):
                piece = sources[n // 4][(n % 4) * BLK + 8 * k : (n % 4) * BLK + 8 * k + 8]
                piece = pltpu.roll(piece, ROWS * n, 1) if n else piece
                result = piece if result is None else result + piece
            return result

        mirrored = jnp.concatenate([pieces(turned[:2]), pieces(turned[2:])], axis=0)
        out[k, pl.ds(TURNED, 16), :] = mirrored.astype(bf16)
        out[k, pl.ds(DEEP_LAM, LAMR), :] = lam


def deep_total(got):
    total = got[0].astype(f32)
    for i in range(1, DEEP):
        total = total + got[i].astype(f32)
    return total, jnp.concatenate([total[j * ROWS : (j + 1) * ROWS] for j in range(GT)], axis=1)


def rotate_kernel(core, got, bases, out):
    total, grad = deep_total(got)
    rot = dot(grad.astype(bf16), bases[1 + core[0]]).astype(bf16)
    lam = add_lam(total[DEEP_LAM:])
    picked, zero = total[TURNED : TURNED + 8], total[TURNED + 8 : TURNED + 16]
    for half in range(PAIR):
        rows = slice(half * FR, (half + 1) * FR)
        tail = jnp.concatenate([lam, picked[rows], zero[rows]], axis=0).astype(bf16)
        for i in range(half, WIDE, PAIR):
            out[i, pl.ds(GATHER_LAM, ROWS), :] = tail
    for j in range(GT):
        tile = rot[:, j * LANES : (j + 1) * LANES]
        for i in range(WIDE):
            out[i, pl.ds(j * ROWS, ROWS), :] = tile


def direct_rows(k, c, block, got):
    total, grad = deep_total(got)
    rows = grad[0:FR]
    for other in range(1, DEEP):
        rows = jnp.where(k == other, grad[other * FR : (other + 1) * FR], rows)
    near, mid, zero, last = [total[DIRECT + t * FR : DIRECT + (t + 1) * FR] for t in range(4)]
    lane = lax.broadcasted_iota(jnp.int32, last.shape, 1)
    none = jnp.zeros_like(last)
    end = jnp.where(lane < BLK, last, none)
    end0 = jnp.where(lane < BLK, pltpu.roll(last, LANES - BLK, 1), none)
    picked = jnp.concatenate([near, mid, end, none], axis=1)
    zero = jnp.where(
        c == 0,
        jnp.concatenate([zero, none, none, none], axis=1),
        jnp.concatenate([none, zero, end0, none], axis=1),
    )
    return rows, pltpu.roll(jnp.concatenate([picked, zero], axis=0), BLK * block, 1)


def mirrored_rows(c, block, tails, mirror):
    row = lax.broadcasted_iota(jnp.int32, (8, LANES), 0)
    group = (lax.broadcasted_iota(jnp.int32, (8, LANES), 1) >> 4) + jnp.where(row >= FR, 4 * c, 0)
    parts = []
    for half in range(PAIR):
        own = jnp.zeros((8, LANES), f32)
        for i in range(NXY):
            distance = (block - i) & (NXY - 1)
            wanted = jnp.where((distance >= 1) & (distance < 8), distance, -1)
            own = jnp.where(group == wanted, tails[PAIR * i + half][8:], own)
        parts += [jnp.where(row < FR, own, 0.0), jnp.where(row < FR, 0.0, own)]
    return dot(jnp.concatenate(parts, axis=1).astype(bf16), mirror[...])


def solve_kernel(core, chip, got, packed, basis_in_t, bases, rows_in, mirror, own, their, scaled):
    tails = [got[i, pl.ds(GATHER_LAM, ROWS), :].astype(f32) for i in range(WIDE)]
    lam = tails[0][:8]
    for tail in tails[1:]:
        lam = lam + tail[:8]
    column = jnp.broadcast_to(lam_row(lam, 0), (8, D)).T[:, 0:1]
    column = jnp.broadcast_to(column, (D, LANES))
    curve = jnp.zeros((8, LANES), f32)
    for j in range(GT):
        rot = got[:, pl.ds(j * ROWS, ROWS), :].reshape(D, LANES)
        rotated = dot(basis_in_t[...], rot)
        low = (rotated / (column * lam[2 * j + 1 : 2 * j + 2] + damping)).astype(bf16)
        scaled[:, pl.ds(j * LANES, LANES)] = low
        curve = curve + jnp.sum((low.astype(f32) * rotated).reshape(D // 8, 8, LANES), axis=0)
    curve = jnp.sum(jnp.sum(curve, axis=1, keepdims=True), axis=0, keepdims=True)
    back = dot(rows_in[...], scaled[...]).astype(bf16)
    prec = lax.dot_general(back, bases[1 + core[0]], (((1,), (1,)), ((), ())), preferred_element_type=f32)
    prec = prec.astype(bf16).astype(f32)
    curve = jnp.broadcast_to(curve, (2, D))
    rows, factors = direct_rows((chip[0] & (NZ - 1)) >> 1, core[0], chip[0] >> 3, packed)
    factors = factors + mirrored_rows(core[0], chip[0] >> 3, tails, mirror)
    low = jnp.concatenate([rows[0:2], factors[0:2], factors[4:6]], axis=0)
    high = jnp.concatenate([rows[2:4], factors[2:4], factors[6:8]], axis=0)
    first = core[0] == 0
    pad = jnp.zeros((6, D), f32)
    own[...] = jnp.concatenate([prec[0:2], curve, jnp.where(first, low, high), pad], axis=0)
    their[...] = jnp.concatenate([prec[2:4], curve, jnp.where(first, high, low), pad], axis=0)


def finish_kernel(scale, core, own, got, old, new_factors, gradients, updates):
    first = core[0] == 0
    curve = own[2:3, :] + got[2:3, :]
    factor = jnp.sqrt(kl_clip / (learn_rate * learn_rate * curve))
    side0 = jnp.where(first, own[...], got[...])
    side1 = jnp.where(first, got[...], own[...])
    updates[0] = (side0[0:2] * factor).astype(bf16)
    updates[1] = (side1[0:2] * factor).astype(bf16)
    gradients[:, 0, :] = side0[4:6]
    gradients[:, 1, :] = side1[4:6]
    batch = (side0[8:10] + side1[8:10], side0[6:8], side1[6:8])
    for f in range(3):
        new_factors[f] = decay * old[f] + scale * batch[f]


def exchange(value, groups):
    return lax.all_to_all(value, "dp", 0, 0, axis_index_groups=groups, tiled=True)


def body(activations, grad_key, grad_value, time_start, time_width, bases, old_factors):
    index = lax.axis_index("dp").astype(jnp.int32)
    core = index & (NC - 1)
    here = (core[None], (index >> 1)[None])
    tokens_here = activations.shape[0]
    share = (1.0 - decay) / (tokens_here * lax.axis_size("dp"))

    def in_hbm(value):
        return pltpu.with_memory_space_constraint(value, pltpu.HBM)

    masks = (in_hbm(time_start.T), in_hbm(time_width.T))
    frames, keys, vals = in_hbm(activations), in_hbm(grad_key), in_hbm(grad_value)
    mask_buf = pltpu.SMEM(time_start.shape[::-1], jnp.int32)
    buf = pltpu.VMEM((tokens_here, D), bf16)
    sems = pltpu.SemaphoreType.DMA((CHUNKS,))
    pair = pltpu.SemaphoreType.DMA((2,))
    partial = shape((NXY, PAIR, WROWS, LANES), bf16)
    work = 6 * D * D * tokens_here
    square, lam_shape = shape((D, D), bf16), shape((2, D), f32)
    frames_shape = shape((tokens_here, D), bf16)
    old = jnp.transpose(old_factors, (1, 0, 2))
    with jax.named_scope("grams_theirs"):
        other, spare, kept, keep, ahead, full0, full1, mirror = call(
            theirs_kernel,
            (
                partial,
                shape((NXY, PAIR, ROWS + ROWS // 2, LANES), bf16),
                frames_shape,
                shape((tokens_here, LANES), bf16),
                frames_shape,
                square,
                square,
                square,
            ),
            [SMEM] * 2 + [HBM] * 5,
            [buf, buf, mask_buf, mask_buf, sems, sems, pair, sems],
            limit=20,
            flops=work,
            moved=5 * MB,
        )(*here, *masks, frames, keys, vals)
    received = lax.ppermute(other, "dp", SWAP)
    with jax.named_scope("factors_mine"):
        picked, keep_lam, send_lam, basis_in_t, rows_in, bases_here = call(
            functools.partial(mine_kernel, share),
            (
                shape((NXY, PAIR, F0 - FA + ROWS // 2, LANES), bf16),
                lam_shape,
                lam_shape,
                square,
                shape((16, D), bf16),
                shape(bases.shape, bf16),
            ),
            [SMEM] * 2 + [VMEM] * 5 + [HBM],
            [pltpu.VMEM((D, D), bf16), pltpu.SemaphoreType.DMA],
            limit=20,
            flops=work,
            moved=4 * MB,
        )(*here, keep, ahead, full0, full1, old, in_hbm(bases))
    sent_lam = lax.ppermute(send_lam, "dp", SWAP)
    with jax.named_scope("gradient_mine"):
        gradient = call(
            gradient_kernel,
            shape((NXY, PAIR, FA, LANES), bf16),
            [VMEM] * 2,
            flops=work // 3,
            moved=4 * MB,
        )(kept, ahead)
    with jax.named_scope("chip_sum"):
        chip, lam = call(add_kernel, (partial, lam_shape), [VMEM] * 6)(
            gradient, picked, spare, received, keep_lam, sent_lam
        )
        chip = chip.reshape(WIDE, WROWS, LANES)
    with jax.named_scope("wide_sum"):
        parts = exchange(chip, WIDE_GROUPS)
    with jax.named_scope("pack"):
        packed = call(pack_kernel, shape((DEEP, DEEP_ROWS, LANES), bf16), [VMEM] * 2)(parts, lam)
    with jax.named_scope("deep_sum"):
        got = exchange(packed, DEEP_GROUPS)
    lines = shape((16, D), f32)
    with jax.named_scope("rotate"):
        spread = call(rotate_kernel, shape((WIDE, GATHER_ROWS, LANES), bf16), [SMEM] + [VMEM] * 2)(
            here[0], got, bases_here
        )
    with jax.named_scope("gather"):
        gathered = exchange(spread, WIDE_GROUPS)
    with jax.named_scope("solve"):
        own, their = call(solve_kernel, (lines, lines), [SMEM] * 2 + [VMEM] * 6, [pltpu.VMEM((D, D), bf16)])(
            *here, gathered, got, basis_in_t, bases_here, rows_in, mirror
        )
    theirs = lax.ppermute(their, "dp", SWAP)
    with jax.named_scope("finish"):
        new_factors, gradients, updates = call(
            functools.partial(finish_kernel, share),
            (shape((3, 2, D), f32), shape((2, 2, D), f32), shape((2, 2, D), bf16)),
            [SMEM] + [VMEM] * 3,
        )(core[None], own, theirs, old)
    return (jnp.transpose(new_factors, (1, 0, 2)), gradients, updates)


def solution(mesh):
    in_specs = (
        P("dp", None),
        P("dp", None),
        P("dp", None),
        P("dp", None),
        P("dp", None),
        P(),
        P("dp", None, None),
    )
    out_specs = (P("dp", None, None), P("dp", None, None), P(None, "dp", None))
    return jax.shard_map(body, mesh=mesh, in_specs=in_specs, out_specs=out_specs, check_vma=False)
```

```python
import functools

import jax
import jax.numpy as jnp
from jax import lax
from jax.experimental import pallas as pl
from jax.experimental.pallas import tpu as pltpu
from jax.sharding import PartitionSpec as P

LEN = 128
NX, NY, NZ, NC = 4, 4, 8, 2
NXY = NX * NY
D = 512
HALF = D // 2
PAIR = 2
WIDE = NXY * PAIR
DEEP = NZ // PAIR
ROWS = D // WIDE
LANES = 128
FR = ROWS // DEEP
GT = D // LANES
BLK = D // NXY
FA, F0, FL = GT * ROWS, (GT + 2) * ROWS, (GT + 3) * ROWS
WROWS = FL + ROWS // 2
MB = 1 << 20

decay = 0.8
damping = 0.001
kl_clip = 0.001
learn_rate = 7e-05

f32, bf16 = jnp.float32, jnp.bfloat16


def device(xy, z, c):
    return (xy * NZ + z) * NC + c


SWAP = [(d, d ^ 1) for d in range(NXY * NZ * NC)]
WIDE_GROUPS = [
    [device(i, k * PAIR + l, c) for i in range(NXY) for l in range(PAIR)]
    for k in range(DEEP)
    for c in range(NC)
]
DEEP_GROUPS = [
    [device(i, k * PAIR + l, c) for k in range(DEEP)] for i in range(NXY) for l in range(PAIR) for c in range(NC)
]
VMEM = pl.BlockSpec(memory_space=pltpu.VMEM)
SMEM = pl.BlockSpec(memory_space=pltpu.SMEM)
HBM = pl.BlockSpec(memory_space=pltpu.HBM)
CHUNKS = 2


def call(kernel, outs, in_specs, scratch=(), limit=16, flops=0, moved=0, aliases=None):
    return pl.pallas_call(
        kernel,
        out_shape=outs,
        in_specs=in_specs,
        out_specs=jax.tree.map(lambda out: HBM if isinstance(out, pl.MemoryRef) else VMEM, outs),
        scratch_shapes=list(scratch),
        input_output_aliases=aliases or {},
        compiler_params=pltpu.CompilerParams(vmem_limit_bytes=limit * MB),
        cost_estimate=pl.CostEstimate(flops=flops, bytes_accessed=moved, transcendentals=0),
    )


def shape(dims, dtype):
    return jax.ShapeDtypeStruct(dims, dtype)


def dot(a, b):
    return jnp.dot(a, b, preferred_element_type=f32)


def arrange(value):
    size = value.shape[1]
    pairs = value.reshape(value.shape[0] // 16, 2, 8, size)
    even, odd = pairs[:, 0], pairs[:, 1]
    upper = lax.broadcasted_iota(jnp.int32, even.shape, 1) < FR
    low = jnp.where(upper, even, pltpu.roll(odd, FR, 1))
    high = jnp.where(upper, pltpu.roll(even, FR, 1), odd)
    blocks = (value.shape[0] // (PAIR * ROWS), ROWS, size)
    return low.reshape(blocks), high.reshape(blocks)


def build_keep(start, width, keep):
    position = lax.broadcasted_iota(jnp.int32, (LEN, LANES), 0)
    for u in range(start.shape[1]):
        outside = None
        for m in range(start.shape[0]):
            first = start[m, u]
            here = (position < first) | (position >= first + width[m, u])
            outside = here if outside is None else outside & here
        keep[pl.ds(u * LEN, LEN), :] = jnp.where(outside, 1.0, 0.0).astype(bf16)


def apply_mask(source, target, keep, q):
    rows = pl.ds(q * (source.shape[0] // CHUNKS), source.shape[0] // CHUNKS)
    for j in range(GT):
        view = (rows, pl.ds(j * LANES, LANES))
        target[view] = source[view] * keep[rows, :]


def fetch(source, target, sems):
    rows = source.shape[0] // CHUNKS
    return [
        pltpu.make_async_copy(source.at[pl.ds(q * rows, rows)], target.at[pl.ds(q * rows, rows)], sems.at[q])
        for q in range(CHUNKS)
    ]


def fetch_picked(pick, xk, xv, target, sems):
    @pl.when(pick == 0)
    def _():
        for copy in fetch(xk, target, sems):
            copy.start()

    @pl.when(pick != 0)
    def _():
        for copy in fetch(xv, target, sems):
            copy.start()

    return fetch(xk, target, sems)


BLOCK = 256


def put(out, r, value, begin):
    for half, rows in enumerate(arrange(value)):
        for j in range(value.shape[1] // LANES):
            out[r][:, half, pl.ds(begin + j * ROWS, ROWS), :] = rows[:, :, j * LANES : (j + 1) * LANES].astype(bf16)


def put_folded(out, r, value, begin):
    for half, rows in enumerate(arrange(value)):
        upper, lower = rows[:, : ROWS // 2], pltpu.roll(rows[:, ROWS // 2 :], LANES // 2, 2)
        lane = lax.broadcasted_iota(jnp.int32, upper.shape, 2)
        out[r][:, half, pl.ds(begin, ROWS // 2), :] = jnp.where(lane < LANES // 2, upper, lower).astype(bf16)


def end_lanes(value):
    lane = lax.broadcasted_iota(jnp.int32, value.shape, 1)
    return jnp.where(lane < BLK, value, 0.0)


def circulate(value, r):
    rows = []
    for b in range(BLOCK // BLK):
        shift = (D - BLK * (r * (BLOCK // BLK) + b)) % D
        piece = value[b * BLK : (b + 1) * BLK]
        rows.append(pltpu.roll(piece, shift, 1) if shift else piece)
    return [jnp.concatenate([p[:, t * LANES : (t + 1) * LANES] for p in rows], axis=0) for t in range(3)]


def zero_grams(pick, x0, out, spare):
    lefts, rests = [], []
    for r in range(D // BLOCK):
        lefts.append(x0[:, pl.ds(r * BLOCK, BLOCK)].T)
        tiles = circulate(dot(lefts[r], x0[...]), r)
        put(out, r, jnp.where(pick == 0, tiles[0], tiles[1]), F0)
        put(spare, r, jnp.where(pick == 0, tiles[1], tiles[0]), 0)
        last = pltpu.roll(end_lanes(tiles[2]), BLK, 1)
        rests.append(jnp.where(pick == 0, 0.0, last))
        put_folded(spare, r, jnp.where(pick == 0, last, 0.0), ROWS)
    return lefts, rests


def picked_grams(lefts, x1, keep, rests, out, end):
    for r in range(D // BLOCK):
        put(out, r, dot(lefts[r], x1[...]), 0)
    wide = jnp.concatenate([keep[...]] * (BLOCK // LANES), axis=1)
    for r in range(D // BLOCK):
        left = (x1[:, pl.ds(r * BLOCK, BLOCK)] * wide).T
        tiles = circulate(dot(left, x1[...]), r)
        put(out, r, jnp.concatenate(tiles[:2], axis=1), FA)
        last = end_lanes(tiles[2])
        put_folded(out, r, last if rests is None else last + rests[r], end)


def theirs_kernel(
    core, start, width, x0, xk, xv, out0, out1, spare0, spare1, kept, keep, ahead, buf0, buf1, starts, widths, sem0, sem1, sem2, sem3
):
    pick = 1 - core[0]
    small = [pltpu.make_async_copy(v, w, sem2.at[i]) for i, (v, w) in enumerate(((start, starts), (width, widths)))]
    copies0 = fetch(x0, buf0, sem0)
    for copy in small + copies0:
        copy.start()
    for copy in small:
        copy.wait()
    build_keep(starts, widths, keep)
    for q in range(CHUNKS):
        copies0[q].wait()
        if q == 0:
            copies1 = fetch_picked(pick, xk, xv, buf1, sem1)
        apply_mask(buf0, kept, keep, q)
    out, spare = (out0, out1), (spare0, spare1)
    lefts, rests = zero_grams(pick, kept, out, spare)
    for copy in copies1:
        copy.wait()
    copies2 = fetch_picked(core[0], xk, xv, ahead, sem3)
    picked_grams(lefts, buf1, keep, rests, out, FL)
    for copy in copies2:
        copy.wait()


def mine_kernel(keep, x0, x1, out0, out1):
    lefts = [x0[:, pl.ds(r * BLOCK, BLOCK)].T for r in range(D // BLOCK)]
    picked_grams(lefts, x1, keep, None, (out0, out1), F0)


SIDES = D // BLOCK
PIECES = 2


def add_kernel(side, mine, spare, received, *rest):
    out, buf, sems = rest[-3:]
    size = NXY // SIDES // PIECES
    copies = []
    main, zero, last = slice(0, F0), slice(F0, FL), slice(FL, WROWS)
    for q in range(PIECES):
        for i in range(q * size, (q + 1) * size):
            for j in range(PAIR):
                buf[i, j, main] = mine[i, j, main] + received[i, j, main]
                buf[i, j, zero] = spare[i, j, :ROWS] + received[i, j, zero]
                ends = mine[i, j, F0:] + spare[i, j, ROWS:]
                buf[i, j, last] = ends + received[i, j, last]
        target = out.at[pl.ds(side * (NXY // SIDES) + q * size, size)]
        copies.append(pltpu.make_async_copy(buf.at[pl.ds(q * size, size)], target, sems.at[q]))
        copies[q].start()
    for copy in copies:
        copy.wait()


def lam_kernel(
    share, core, chip, _, keep, x0, xk, xv, bases, keep_lam, send_lam, basis_in_t, mirror, basis_out, rows_in, b0, b1, b2, sem0, sem1, sem2
):
    c = core[0]
    bufs = (b0, b1, b2)
    copies = [fetch(x, buf, sem) for x, buf, sem in zip((x0, xk, xv), bufs, (sem0, sem1, sem2))]
    for group in copies:
        for copy in group:
            copy.start()
    low, high = arrange(bases[0].astype(f32))
    basis_in_t[...] = jnp.concatenate([low, high], axis=1).reshape(D, D).T.astype(bf16)
    lane = lax.broadcasted_iota(jnp.int32, (LANES, D), 0)
    column = lax.broadcasted_iota(jnp.int32, (LANES, D), 1)
    for half in range(PAIR):
        home = 8 * ((lane >> 2) & 3) + FR * half + (lane & 3) + 2 * D
        for kind in range(2):
            distance = (lane >> 4) + (4 * c if kind else 0)
            there = (home + BLK * ((chip[0] >> 3) - distance)) & (D - 1)
            one = jnp.where(column == there, 1.0, 0.0).astype(bf16)
            mirror[pl.ds((2 * half + kind) * LANES, LANES), :] = one
    basis_out[...] = bases[1 + c]
    row = lax.broadcasted_iota(jnp.int32, (16, D), 0)
    column = lax.broadcasted_iota(jnp.int32, (16, D), 1)
    wanted = (row < FR) & (column == FR * chip[0] + ((row + 2 * c) & (FR - 1)))
    rows_in[...] = dot(jnp.where(wanted, 1.0, 0.0).astype(bf16), bases[0]).astype(bf16)
    lam = []
    for f in range(3):
        total = jnp.zeros((8, D), f32)
        for q in range(CHUNKS):
            copies[f][q].wait()
            apply_mask(bufs[f], bufs[f], keep, q)
        for q in range(bufs[f].shape[0] // BLOCK):
            product = dot(bufs[f][pl.ds(q * BLOCK, BLOCK), :], bases[f])
            total = total + jnp.sum((product * product).reshape(BLOCK // 8, 8, D), axis=0)
        lam.append(jnp.sum(total, axis=0, keepdims=True) * share)
    keep_lam[0:1, :] = lam[0]
    send_lam[0:1, :] = lam[0]
    keep_lam[1:2, :] = jnp.where(c == 0, lam[1], lam[2])
    send_lam[1:2, :] = jnp.where(c == 0, lam[2], lam[1])


def split(value):
    high = value.astype(bf16)
    return high.astype(f32), value - high.astype(f32)


def lam_rows(lam):
    return jnp.concatenate(split(jnp.concatenate([lam[:, j * LANES : (j + 1) * LANES] for j in range(GT)], axis=0)), axis=0)


def add_lam(rows):
    return rows[: 2 * GT] + rows[2 * GT :]


def lam_row(total, index):
    return jnp.concatenate([total[2 * j + index : 2 * j + index + 1] for j in range(GT)], axis=1)


LAMR = 4 * GT
DIRECT = GT * ROWS
TURNED = DIRECT + 4 * FR
DEEP_LAM = TURNED + 16
DEEP_ROWS = DEEP_LAM + LAMR
GATHER_LAM = GT * ROWS
GATHER_TURNED = GATHER_LAM + 2 * GT
GATHER_ROWS = GATHER_TURNED + 8


def pack_kernel(parts, keep_lam, send_lam, out):
    total = parts[0].astype(f32)
    for i in range(1, WIDE):
        total = total + parts[i].astype(f32)
    lam = lam_rows(keep_lam[...] + send_lam[...]).astype(bf16)
    for j in range(GT):
        tile = total[j * ROWS : (j + 1) * ROWS].astype(bf16)
        for k in range(DEEP):
            out[k, pl.ds(j * ROWS, ROWS), :] = tile
    near, mid, zero = total[FA : FA + ROWS], total[FA + ROWS : F0], total[F0:FL]
    last = total[FL:]
    last = jnp.concatenate([last, pltpu.roll(last, LANES // 2, 1)], axis=0)
    empty = jnp.zeros((LANES - ROWS, LANES), f32)
    turned = [jnp.concatenate([v, empty], axis=0).T for v in (near, mid, zero)]
    for k in range(DEEP):
        rows = slice(k * FR, (k + 1) * FR)
        direct = jnp.concatenate([v[rows] for v in (near, mid, zero, last)], axis=0)
        out[k, pl.ds(DIRECT, 4 * FR), :] = direct.astype(bf16)

        def pieces(sources):
            result = None
            for n in range(4 * len(sources)):
                piece = sources[n // 4][(n % 4) * BLK + 8 * k : (n % 4) * BLK + 8 * k + 8]
                piece = pltpu.roll(piece, ROWS * n, 1) if n else piece
                result = piece if result is None else result + piece
            return result

        mirrored = jnp.concatenate([pieces(turned[:2]), pieces(turned[2:])], axis=0)
        out[k, pl.ds(TURNED, 16), :] = mirrored.astype(bf16)
        out[k, pl.ds(DEEP_LAM, LAMR), :] = lam


def deep_total(got):
    total = got[0].astype(f32)
    for i in range(1, DEEP):
        total = total + got[i].astype(f32)
    return total, jnp.concatenate([total[j * ROWS : (j + 1) * ROWS] for j in range(GT)], axis=1)


def rotate_kernel(got, basis, out):
    total, grad = deep_total(got)
    rot = dot(grad.astype(bf16), basis[...]).astype(bf16)
    lam = add_lam(total[DEEP_LAM:])
    picked, zero = total[TURNED : TURNED + 8], total[TURNED + 8 : TURNED + 16]
    for half in range(PAIR):
        rows = slice(half * FR, (half + 1) * FR)
        tail = jnp.concatenate([lam, picked[rows], zero[rows]], axis=0).astype(bf16)
        for i in range(half, WIDE, PAIR):
            out[i, pl.ds(GATHER_LAM, ROWS), :] = tail
    for j in range(GT):
        tile = rot[:, j * LANES : (j + 1) * LANES]
        for i in range(WIDE):
            out[i, pl.ds(j * ROWS, ROWS), :] = tile


def direct_rows(k, c, block, got):
    total, grad = deep_total(got)
    rows = grad[0:FR]
    for other in range(1, DEEP):
        rows = jnp.where(k == other, grad[other * FR : (other + 1) * FR], rows)
    near, mid, zero, last = [total[DIRECT + t * FR : DIRECT + (t + 1) * FR] for t in range(4)]
    lane = lax.broadcasted_iota(jnp.int32, last.shape, 1)
    none = jnp.zeros_like(last)
    end = jnp.where(lane < BLK, last, none)
    end0 = jnp.where(lane < BLK, pltpu.roll(last, LANES - BLK, 1), none)
    picked = jnp.concatenate([near, mid, end, none], axis=1)
    zero = jnp.where(
        c == 0,
        jnp.concatenate([zero, none, none, none], axis=1),
        jnp.concatenate([none, zero, end0, none], axis=1),
    )
    return rows, pltpu.roll(jnp.concatenate([picked, zero], axis=0), BLK * block, 1)


def mirrored_rows(c, block, tails, mirror):
    row = lax.broadcasted_iota(jnp.int32, (8, LANES), 0)
    group = (lax.broadcasted_iota(jnp.int32, (8, LANES), 1) >> 4) + jnp.where(row >= FR, 4 * c, 0)
    parts = []
    for half in range(PAIR):
        own = jnp.zeros((8, LANES), f32)
        for i in range(NXY):
            distance = (block - i) & (NXY - 1)
            wanted = jnp.where((distance >= 1) & (distance < 8), distance, -1)
            own = jnp.where(group == wanted, tails[PAIR * i + half][8:], own)
        parts += [jnp.where(row < FR, own, 0.0), jnp.where(row < FR, 0.0, own)]
    return dot(jnp.concatenate(parts, axis=1).astype(bf16), mirror[...])


def solve_kernel(core, chip, got, packed, basis_in_t, basis_out, rows_in, mirror, own, their, scaled):
    tails = [got[i, pl.ds(GATHER_LAM, ROWS), :].astype(f32) for i in range(WIDE)]
    lam = tails[0][:8]
    for tail in tails[1:]:
        lam = lam + tail[:8]
    column = jnp.broadcast_to(lam_row(lam, 0), (8, D)).T[:, 0:1]
    column = jnp.broadcast_to(column, (D, LANES))
    curve = jnp.zeros((8, LANES), f32)
    for j in range(GT):
        rot = got[:, pl.ds(j * ROWS, ROWS), :].reshape(D, LANES)
        rotated = dot(basis_in_t[...], rot)
        low = (rotated / (column * lam[2 * j + 1 : 2 * j + 2] + damping)).astype(bf16)
        scaled[:, pl.ds(j * LANES, LANES)] = low
        curve = curve + jnp.sum((low.astype(f32) * rotated).reshape(D // 8, 8, LANES), axis=0)
    curve = jnp.sum(jnp.sum(curve, axis=1, keepdims=True), axis=0, keepdims=True)
    back = dot(rows_in[...], scaled[...]).astype(bf16)
    prec = lax.dot_general(back, basis_out[...], (((1,), (1,)), ((), ())), preferred_element_type=f32)
    prec = prec.astype(bf16).astype(f32)
    curve = jnp.broadcast_to(curve, (2, D))
    rows, factors = direct_rows((chip[0] & (NZ - 1)) >> 1, core[0], chip[0] >> 3, packed)
    factors = factors + mirrored_rows(core[0], chip[0] >> 3, tails, mirror)
    low = jnp.concatenate([rows[0:2], factors[0:2], factors[4:6]], axis=0)
    high = jnp.concatenate([rows[2:4], factors[2:4], factors[6:8]], axis=0)
    first = core[0] == 0
    pad = jnp.zeros((6, D), f32)
    own[...] = jnp.concatenate([prec[0:2], curve, jnp.where(first, low, high), pad], axis=0)
    their[...] = jnp.concatenate([prec[2:4], curve, jnp.where(first, high, low), pad], axis=0)


def finish_kernel(scale, core, own, got, old, new_factors, gradients, updates):
    first = core[0] == 0
    curve = own[2:3, :] + got[2:3, :]
    factor = jnp.sqrt(kl_clip / (learn_rate * learn_rate * curve))
    side0 = jnp.where(first, own[...], got[...])
    side1 = jnp.where(first, got[...], own[...])
    updates[0] = (side0[0:2] * factor).astype(bf16)
    updates[1] = (side1[0:2] * factor).astype(bf16)
    gradients[:, 0, :] = side0[4:6]
    gradients[:, 1, :] = side1[4:6]
    batch = (side0[8:10] + side1[8:10], side0[6:8], side1[6:8])
    for f in range(3):
        new_factors[f] = decay * old[f] + scale * batch[f]


def exchange(value, groups):
    return lax.all_to_all(value, "dp", 0, 0, axis_index_groups=groups, tiled=True)


def body(activations, grad_key, grad_value, time_start, time_width, bases, old_factors):
    index = lax.axis_index("dp").astype(jnp.int32)
    core = index & (NC - 1)
    first = core == 0
    here = (core[None], (index >> 1)[None])
    tokens_here = activations.shape[0]
    share = (1.0 - decay) / (tokens_here * lax.axis_size("dp"))

    def in_hbm(value):
        return pltpu.with_memory_space_constraint(value, pltpu.HBM)

    masks = (in_hbm(time_start.T), in_hbm(time_width.T))
    frames, keys, vals = in_hbm(activations), in_hbm(grad_key), in_hbm(grad_value)
    mask_buf = pltpu.SMEM(time_start.shape[::-1], jnp.int32)
    buf = pltpu.VMEM((tokens_here, D), bf16)
    sems = pltpu.SemaphoreType.DMA((CHUNKS,))
    pair = pltpu.SemaphoreType.DMA((2,))
    side_rows = NXY // SIDES
    partial = shape((side_rows, PAIR, WROWS, LANES), bf16)
    spare_shape = shape((side_rows, PAIR, ROWS + ROWS // 2, LANES), bf16)
    mine_shape = shape((side_rows, PAIR, F0 + ROWS // 2, LANES), bf16)
    work = 6 * D * D * tokens_here
    with jax.named_scope("grams_theirs"):
        *sent, spare0, spare1, kept, keep, ahead = call(
            theirs_kernel,
            (
                partial,
                partial,
                spare_shape,
                spare_shape,
                shape((tokens_here, D), bf16),
                shape((tokens_here, LANES), bf16),
                shape((tokens_here, D), bf16),
            ),
            [SMEM] + [HBM] * 5,
            [buf, buf, mask_buf, mask_buf, sems, sems, pair, sems],
            flops=work,
            moved=4 * MB,
        )(core[None], *masks, frames, keys, vals)
    received = [lax.ppermute(part, "dp", SWAP) for part in sent]
    with jax.named_scope("grams_mine"):
        mine = call(
            mine_kernel,
            (mine_shape, mine_shape),
            [VMEM] * 3,
            flops=work,
            moved=4 * MB,
        )(keep, kept, ahead)
    whole = pltpu.HBM((NXY, PAIR, WROWS, LANES), bf16)
    room = [pltpu.VMEM(partial.shape, bf16), pltpu.SemaphoreType.DMA((PIECES,))]
    with jax.named_scope("chip_sum0"):
        chip = call(functools.partial(add_kernel, 0), whole, [VMEM] * 3, room, moved=MB)(mine[0], spare0, received[0])
    with jax.named_scope("chip_sum1"):
        chip = call(
            functools.partial(add_kernel, 1), whole, [VMEM] * 3 + [HBM], room, moved=MB, aliases={3: 0}
        )(mine[1], spare1, received[1], chip)
        chip = chip.reshape(WIDE, WROWS, LANES)
    with jax.named_scope("wide_sum"):
        parts = exchange(chip, WIDE_GROUPS)

    lam_shape, square = shape((2, D), f32), shape((D, D), bf16)
    with jax.named_scope("lam"):
        keep_lam, send_lam, basis_in_t, mirror, basis_out, rows_in = call(
            functools.partial(lam_kernel, share),
            (lam_shape, lam_shape, square, square, square, shape((16, D), bf16)),
            [SMEM, SMEM, HBM, VMEM, HBM, HBM, HBM, VMEM],
            [buf] * 3 + [sems] * 3,
            flops=work,
            moved=4 * MB,
        )(*here, in_hbm(chip), keep, frames, keys, vals, bases)
    old_lam = []
    my_rows = lax.dynamic_slice_in_dim(bases, 2 * index, 2, 1).astype(f32)
    for f in range(3):
        old_image = jnp.dot(old_factors[:, f, :], bases[f].astype(f32), precision=lax.Precision.HIGHEST)
        old_lam.append(decay * jnp.sum(my_rows[f] * old_image, axis=0))
    keep_lam = keep_lam + jnp.stack([old_lam[0], jnp.where(first, old_lam[1], old_lam[2])])
    send_lam = send_lam + jnp.stack([old_lam[0], jnp.where(first, old_lam[2], old_lam[1])])
    sent_lam = lax.ppermute(send_lam, "dp", SWAP)

    with jax.named_scope("pack"):
        packed = call(pack_kernel, shape((DEEP, DEEP_ROWS, LANES), bf16), [VMEM] * 3)(parts, keep_lam, sent_lam)
    with jax.named_scope("deep_sum"):
        got = exchange(packed, DEEP_GROUPS)
    lines = shape((16, D), f32)
    with jax.named_scope("rotate"):
        spread = call(rotate_kernel, shape((WIDE, GATHER_ROWS, LANES), bf16), [VMEM] * 2)(got, basis_out)
    with jax.named_scope("gather"):
        gathered = exchange(spread, WIDE_GROUPS)
    with jax.named_scope("solve"):
        own, their = call(solve_kernel, (lines, lines), [SMEM] * 2 + [VMEM] * 6, [pltpu.VMEM((D, D), bf16)])(
            *here, gathered, got, basis_in_t, basis_out, rows_in, mirror
        )
    theirs = lax.ppermute(their, "dp", SWAP)
    with jax.named_scope("finish"):
        new_factors, gradients, updates = call(
            functools.partial(finish_kernel, share),
            (shape((3, 2, D), f32), shape((2, 2, D), f32), shape((2, 2, D), bf16)),
            [SMEM] + [VMEM] * 3,
        )(core[None], own, theirs, jnp.transpose(old_factors, (1, 0, 2)))
    return (jnp.transpose(new_factors, (1, 0, 2)), gradients, updates)


def solution(mesh):
    in_specs = (
        P("dp", None),
        P("dp", None),
        P("dp", None),
        P("dp", None),
        P("dp", None),
        P(),
        P("dp", None, None),
    )
    out_specs = (P("dp", None, None), P("dp", None, None), P(None, "dp", None))
    return jax.shard_map(body, mesh=mesh, in_specs=in_specs, out_specs=out_specs, check_vma=False)
```

```python
import functools

import jax
import jax.numpy as jnp
from jax import lax
from jax.experimental import pallas as pl
from jax.experimental.pallas import tpu as pltpu
from jax.sharding import PartitionSpec as P

LEN = 128
NX, NY, NZ, NC = 4, 4, 8, 2
NXY = NX * NY
D = 512
HALF = D // 2
PAIR = 2
WIDE = NXY * PAIR
DEEP = NZ // PAIR
ROWS = D // WIDE
LANES = 128
FR = ROWS // DEEP
GT = D // LANES
BLK = D // NXY
FA, F0, FL = GT * ROWS, (GT + 2) * ROWS, (GT + 3) * ROWS
WROWS = FL + ROWS // 2
MB = 1 << 20

decay = 0.8
damping = 0.001
kl_clip = 0.001
learn_rate = 7e-05

f32, bf16 = jnp.float32, jnp.bfloat16


def device(xy, z, c):
    return (xy * NZ + z) * NC + c


SWAP = [(d, d ^ 1) for d in range(NXY * NZ * NC)]
WIDE_GROUPS = [
    [device(i, k * PAIR + l, c) for i in range(NXY) for l in range(PAIR)]
    for k in range(DEEP)
    for c in range(NC)
]
DEEP_GROUPS = [
    [device(i, k * PAIR + l, c) for k in range(DEEP)] for i in range(NXY) for l in range(PAIR) for c in range(NC)
]
VMEM = pl.BlockSpec(memory_space=pltpu.VMEM)
SMEM = pl.BlockSpec(memory_space=pltpu.SMEM)
HBM = pl.BlockSpec(memory_space=pltpu.HBM)
CHUNKS = 2


def call(kernel, outs, in_specs, scratch=(), limit=16, flops=0, moved=0):
    return pl.pallas_call(
        kernel,
        out_shape=outs,
        in_specs=in_specs,
        out_specs=jax.tree.map(lambda out: HBM if isinstance(out, pl.MemoryRef) else VMEM, outs),
        scratch_shapes=list(scratch),
        compiler_params=pltpu.CompilerParams(vmem_limit_bytes=limit * MB),
        cost_estimate=pl.CostEstimate(flops=flops, bytes_accessed=moved, transcendentals=0),
    )


def shape(dims, dtype):
    return jax.ShapeDtypeStruct(dims, dtype)


def dot(a, b):
    return jnp.dot(a, b, preferred_element_type=f32)


def arrange(value):
    size = value.shape[1]
    pairs = value.reshape(value.shape[0] // 16, 2, 8, size)
    even, odd = pairs[:, 0], pairs[:, 1]
    upper = lax.broadcasted_iota(jnp.int32, even.shape, 1) < FR
    low = jnp.where(upper, even, pltpu.roll(odd, FR, 1))
    high = jnp.where(upper, pltpu.roll(even, FR, 1), odd)
    blocks = (value.shape[0] // (PAIR * ROWS), ROWS, size)
    return low.reshape(blocks), high.reshape(blocks)


def build_keep(start, width, keep):
    position = lax.broadcasted_iota(jnp.int32, (LEN, LANES), 0)
    for u in range(start.shape[1]):
        outside = None
        for m in range(start.shape[0]):
            first = start[m, u]
            here = (position < first) | (position >= first + width[m, u])
            outside = here if outside is None else outside & here
        keep[pl.ds(u * LEN, LEN), :] = jnp.where(outside, 1.0, 0.0).astype(bf16)


def apply_mask(source, target, keep, q):
    rows = pl.ds(q * (source.shape[0] // CHUNKS), source.shape[0] // CHUNKS)
    for j in range(GT):
        view = (rows, pl.ds(j * LANES, LANES))
        target[view] = source[view] * keep[rows, :]


def fetch(source, target, sems):
    rows = source.shape[0] // CHUNKS
    return [
        pltpu.make_async_copy(source.at[pl.ds(q * rows, rows)], target.at[pl.ds(q * rows, rows)], sems.at[q])
        for q in range(CHUNKS)
    ]


def fetch_picked(pick, xk, xv, target, sems):
    @pl.when(pick == 0)
    def _():
        for copy in fetch(xk, target, sems):
            copy.start()

    @pl.when(pick != 0)
    def _():
        for copy in fetch(xv, target, sems):
            copy.start()

    return fetch(xk, target, sems)


BLOCK = 256


def put(out, r, value, begin):
    for half, rows in enumerate(arrange(value)):
        for j in range(value.shape[1] // LANES):
            out[r][:, half, pl.ds(begin + j * ROWS, ROWS), :] = rows[:, :, j * LANES : (j + 1) * LANES].astype(bf16)


def put_folded(out, r, value, begin):
    for half, rows in enumerate(arrange(value)):
        upper, lower = rows[:, : ROWS // 2], pltpu.roll(rows[:, ROWS // 2 :], LANES // 2, 2)
        lane = lax.broadcasted_iota(jnp.int32, upper.shape, 2)
        out[r][:, half, pl.ds(begin, ROWS // 2), :] = jnp.where(lane < LANES // 2, upper, lower).astype(bf16)


def end_lanes(value):
    lane = lax.broadcasted_iota(jnp.int32, value.shape, 1)
    return jnp.where(lane < BLK, value, 0.0)


def circulate(value, r):
    rows = []
    for b in range(BLOCK // BLK):
        shift = (D - BLK * (r * (BLOCK // BLK) + b)) % D
        piece = value[b * BLK : (b + 1) * BLK]
        rows.append(pltpu.roll(piece, shift, 1) if shift else piece)
    return [jnp.concatenate([p[:, t * LANES : (t + 1) * LANES] for p in rows], axis=0) for t in range(3)]


def zero_grams(pick, x0, out, spare):
    lefts, rests = [], []
    for r in range(D // BLOCK):
        lefts.append(x0[:, pl.ds(r * BLOCK, BLOCK)].T)
        tiles = circulate(dot(lefts[r], x0[...]), r)
        put(out, r, jnp.where(pick == 0, tiles[0], tiles[1]), F0)
        put(spare, r, jnp.where(pick == 0, tiles[1], tiles[0]), 0)
        last = pltpu.roll(end_lanes(tiles[2]), BLK, 1)
        rests.append(jnp.where(pick == 0, 0.0, last))
        put_folded(spare, r, jnp.where(pick == 0, last, 0.0), ROWS)
    return lefts, rests


def picked_grams(lefts, x1, keep, rests, out, end):
    for r in range(D // BLOCK):
        put(out, r, dot(lefts[r], x1[...]), 0)
    wide = jnp.concatenate([keep[...]] * (BLOCK // LANES), axis=1)
    for r in range(D // BLOCK):
        left = (x1[:, pl.ds(r * BLOCK, BLOCK)] * wide).T
        tiles = circulate(dot(left, x1[...]), r)
        put(out, r, jnp.concatenate(tiles[:2], axis=1), FA)
        last = end_lanes(tiles[2])
        put_folded(out, r, last if rests is None else last + rests[r], end)


def theirs_kernel(
    core, start, width, x0, xk, xv, out0, out1, spare0, spare1, kept, keep, ahead, buf0, buf1, starts, widths, sem0, sem1, sem2, sem3
):
    pick = 1 - core[0]
    small = [pltpu.make_async_copy(v, w, sem2.at[i]) for i, (v, w) in enumerate(((start, starts), (width, widths)))]
    copies0 = fetch(x0, buf0, sem0)
    for copy in small + copies0:
        copy.start()
    for copy in small:
        copy.wait()
    build_keep(starts, widths, keep)
    for q in range(CHUNKS):
        copies0[q].wait()
        if q == 0:
            copies1 = fetch_picked(pick, xk, xv, buf1, sem1)
        apply_mask(buf0, kept, keep, q)
    out, spare = (out0, out1), (spare0, spare1)
    lefts, rests = zero_grams(pick, kept, out, spare)
    for copy in copies1:
        copy.wait()
    copies2 = fetch_picked(core[0], xk, xv, ahead, sem3)
    picked_grams(lefts, buf1, keep, rests, out, FL)
    for copy in copies2:
        copy.wait()


def mine_kernel(keep, x0, x1, out0, out1):
    lefts = [x0[:, pl.ds(r * BLOCK, BLOCK)].T for r in range(D // BLOCK)]
    picked_grams(lefts, x1, keep, None, (out0, out1), F0)


SIDES = D // BLOCK
PIECES = 2


def add_rows(mine, spare, received, out, blocks):
    main, zero, last = slice(0, F0), slice(F0, FL), slice(FL, WROWS)
    for i in blocks:
        for j in range(PAIR):
            out[i, j, main] = mine[i, j, main] + received[i, j, main]
            out[i, j, zero] = spare[i, j, :ROWS] + received[i, j, zero]
            ends = mine[i, j, F0:] + spare[i, j, ROWS:]
            out[i, j, last] = ends + received[i, j, last]


def add_first_kernel(mine, spare, received, out):
    add_rows(mine, spare, received, out, range(NXY // SIDES))


def add_second_kernel(first, mine, spare, received, out, buf, sems):
    count = NXY // SIDES
    size = count // PIECES
    copies = [pltpu.make_async_copy(first, out.at[pl.ds(0, count)], sems.at[PIECES])]
    copies[0].start()
    for q in range(PIECES):
        add_rows(mine, spare, received, buf, range(q * size, (q + 1) * size))
        target = out.at[pl.ds(count + q * size, size)]
        copies.append(pltpu.make_async_copy(buf.at[pl.ds(q * size, size)], target, sems.at[q]))
        copies[-1].start()
    for copy in copies:
        copy.wait()


def lam_kernel(
    share, core, chip, _, keep, x0, xk, xv, bases, keep_lam, send_lam, basis_in_t, mirror, basis_out, rows_in, b0, b1, b2, sem0, sem1, sem2
):
    c = core[0]
    bufs = (b0, b1, b2)
    copies = [fetch(x, buf, sem) for x, buf, sem in zip((x0, xk, xv), bufs, (sem0, sem1, sem2))]
    for group in copies:
        for copy in group:
            copy.start()
    low, high = arrange(bases[0].astype(f32))
    basis_in_t[...] = jnp.concatenate([low, high], axis=1).reshape(D, D).T.astype(bf16)
    lane = lax.broadcasted_iota(jnp.int32, (LANES, D), 0)
    column = lax.broadcasted_iota(jnp.int32, (LANES, D), 1)
    for half in range(PAIR):
        home = 8 * ((lane >> 2) & 3) + FR * half + (lane & 3) + 2 * D
        for kind in range(2):
            distance = (lane >> 4) + (4 * c if kind else 0)
            there = (home + BLK * ((chip[0] >> 3) - distance)) & (D - 1)
            one = jnp.where(column == there, 1.0, 0.0).astype(bf16)
            mirror[pl.ds((2 * half + kind) * LANES, LANES), :] = one
    basis_out[...] = bases[1 + c]
    row = lax.broadcasted_iota(jnp.int32, (16, D), 0)
    column = lax.broadcasted_iota(jnp.int32, (16, D), 1)
    wanted = (row < FR) & (column == FR * chip[0] + ((row + 2 * c) & (FR - 1)))
    rows_in[...] = dot(jnp.where(wanted, 1.0, 0.0).astype(bf16), bases[0]).astype(bf16)
    lam = []
    for f in range(3):
        total = jnp.zeros((8, D), f32)
        for q in range(CHUNKS):
            copies[f][q].wait()
            apply_mask(bufs[f], bufs[f], keep, q)
        for q in range(bufs[f].shape[0] // BLOCK):
            product = dot(bufs[f][pl.ds(q * BLOCK, BLOCK), :], bases[f])
            total = total + jnp.sum((product * product).reshape(BLOCK // 8, 8, D), axis=0)
        lam.append(jnp.sum(total, axis=0, keepdims=True) * share)
    keep_lam[0:1, :] = lam[0]
    send_lam[0:1, :] = lam[0]
    keep_lam[1:2, :] = jnp.where(c == 0, lam[1], lam[2])
    send_lam[1:2, :] = jnp.where(c == 0, lam[2], lam[1])


def split(value):
    high = value.astype(bf16)
    return high.astype(f32), value - high.astype(f32)


def lam_rows(lam):
    return jnp.concatenate(split(jnp.concatenate([lam[:, j * LANES : (j + 1) * LANES] for j in range(GT)], axis=0)), axis=0)


def add_lam(rows):
    return rows[: 2 * GT] + rows[2 * GT :]


def lam_row(total, index):
    return jnp.concatenate([total[2 * j + index : 2 * j + index + 1] for j in range(GT)], axis=1)


LAMR = 4 * GT
DIRECT = GT * ROWS
TURNED = DIRECT + 4 * FR
DEEP_LAM = TURNED + 16
DEEP_ROWS = DEEP_LAM + LAMR
GATHER_LAM = GT * ROWS
GATHER_TURNED = GATHER_LAM + 2 * GT
GATHER_ROWS = GATHER_TURNED + 8


def pack_kernel(parts, keep_lam, send_lam, out):
    total = parts[0].astype(f32)
    for i in range(1, WIDE):
        total = total + parts[i].astype(f32)
    lam = lam_rows(keep_lam[...] + send_lam[...]).astype(bf16)
    for j in range(GT):
        tile = total[j * ROWS : (j + 1) * ROWS].astype(bf16)
        for k in range(DEEP):
            out[k, pl.ds(j * ROWS, ROWS), :] = tile
    near, mid, zero = total[FA : FA + ROWS], total[FA + ROWS : F0], total[F0:FL]
    last = total[FL:]
    last = jnp.concatenate([last, pltpu.roll(last, LANES // 2, 1)], axis=0)
    empty = jnp.zeros((LANES - ROWS, LANES), f32)
    turned = [jnp.concatenate([v, empty], axis=0).T for v in (near, mid, zero)]
    for k in range(DEEP):
        rows = slice(k * FR, (k + 1) * FR)
        direct = jnp.concatenate([v[rows] for v in (near, mid, zero, last)], axis=0)
        out[k, pl.ds(DIRECT, 4 * FR), :] = direct.astype(bf16)

        def pieces(sources):
            result = None
            for n in range(4 * len(sources)):
                piece = sources[n // 4][(n % 4) * BLK + 8 * k : (n % 4) * BLK + 8 * k + 8]
                piece = pltpu.roll(piece, ROWS * n, 1) if n else piece
                result = piece if result is None else result + piece
            return result

        mirrored = jnp.concatenate([pieces(turned[:2]), pieces(turned[2:])], axis=0)
        out[k, pl.ds(TURNED, 16), :] = mirrored.astype(bf16)
        out[k, pl.ds(DEEP_LAM, LAMR), :] = lam


def deep_total(got):
    total = got[0].astype(f32)
    for i in range(1, DEEP):
        total = total + got[i].astype(f32)
    return total, jnp.concatenate([total[j * ROWS : (j + 1) * ROWS] for j in range(GT)], axis=1)


def rotate_kernel(got, basis, out):
    total, grad = deep_total(got)
    rot = dot(grad.astype(bf16), basis[...]).astype(bf16)
    lam = add_lam(total[DEEP_LAM:])
    picked, zero = total[TURNED : TURNED + 8], total[TURNED + 8 : TURNED + 16]
    for half in range(PAIR):
        rows = slice(half * FR, (half + 1) * FR)
        tail = jnp.concatenate([lam, picked[rows], zero[rows]], axis=0).astype(bf16)
        for i in range(half, WIDE, PAIR):
            out[i, pl.ds(GATHER_LAM, ROWS), :] = tail
    for j in range(GT):
        tile = rot[:, j * LANES : (j + 1) * LANES]
        for i in range(WIDE):
            out[i, pl.ds(j * ROWS, ROWS), :] = tile


def direct_rows(k, c, block, got):
    total, grad = deep_total(got)
    rows = grad[0:FR]
    for other in range(1, DEEP):
        rows = jnp.where(k == other, grad[other * FR : (other + 1) * FR], rows)
    near, mid, zero, last = [total[DIRECT + t * FR : DIRECT + (t + 1) * FR] for t in range(4)]
    lane = lax.broadcasted_iota(jnp.int32, last.shape, 1)
    none = jnp.zeros_like(last)
    end = jnp.where(lane < BLK, last, none)
    end0 = jnp.where(lane < BLK, pltpu.roll(last, LANES - BLK, 1), none)
    picked = jnp.concatenate([near, mid, end, none], axis=1)
    zero = jnp.where(
        c == 0,
        jnp.concatenate([zero, none, none, none], axis=1),
        jnp.concatenate([none, zero, end0, none], axis=1),
    )
    return rows, pltpu.roll(jnp.concatenate([picked, zero], axis=0), BLK * block, 1)


def mirrored_rows(c, block, tails, mirror):
    row = lax.broadcasted_iota(jnp.int32, (8, LANES), 0)
    group = (lax.broadcasted_iota(jnp.int32, (8, LANES), 1) >> 4) + jnp.where(row >= FR, 4 * c, 0)
    parts = []
    for half in range(PAIR):
        own = jnp.zeros((8, LANES), f32)
        for i in range(NXY):
            distance = (block - i) & (NXY - 1)
            wanted = jnp.where((distance >= 1) & (distance < 8), distance, -1)
            own = jnp.where(group == wanted, tails[PAIR * i + half][8:], own)
        parts += [jnp.where(row < FR, own, 0.0), jnp.where(row < FR, 0.0, own)]
    return dot(jnp.concatenate(parts, axis=1).astype(bf16), mirror[...])


def solve_kernel(core, chip, got, packed, basis_in_t, basis_out, rows_in, mirror, own, their, scaled):
    tails = [got[i, pl.ds(GATHER_LAM, ROWS), :].astype(f32) for i in range(WIDE)]
    lam = tails[0][:8]
    for tail in tails[1:]:
        lam = lam + tail[:8]
    column = jnp.broadcast_to(lam_row(lam, 0), (8, D)).T[:, 0:1]
    column = jnp.broadcast_to(column, (D, LANES))
    curve = jnp.zeros((8, LANES), f32)
    for j in range(GT):
        rot = got[:, pl.ds(j * ROWS, ROWS), :].reshape(D, LANES)
        rotated = dot(basis_in_t[...], rot)
        low = (rotated / (column * lam[2 * j + 1 : 2 * j + 2] + damping)).astype(bf16)
        scaled[:, pl.ds(j * LANES, LANES)] = low
        curve = curve + jnp.sum((low.astype(f32) * rotated).reshape(D // 8, 8, LANES), axis=0)
    curve = jnp.sum(jnp.sum(curve, axis=1, keepdims=True), axis=0, keepdims=True)
    back = dot(rows_in[...], scaled[...]).astype(bf16)
    prec = lax.dot_general(back, basis_out[...], (((1,), (1,)), ((), ())), preferred_element_type=f32)
    prec = prec.astype(bf16).astype(f32)
    curve = jnp.broadcast_to(curve, (2, D))
    rows, factors = direct_rows((chip[0] & (NZ - 1)) >> 1, core[0], chip[0] >> 3, packed)
    factors = factors + mirrored_rows(core[0], chip[0] >> 3, tails, mirror)
    low = jnp.concatenate([rows[0:2], factors[0:2], factors[4:6]], axis=0)
    high = jnp.concatenate([rows[2:4], factors[2:4], factors[6:8]], axis=0)
    first = core[0] == 0
    pad = jnp.zeros((6, D), f32)
    own[...] = jnp.concatenate([prec[0:2], curve, jnp.where(first, low, high), pad], axis=0)
    their[...] = jnp.concatenate([prec[2:4], curve, jnp.where(first, high, low), pad], axis=0)


def finish_kernel(scale, core, own, got, old, new_factors, gradients, updates):
    first = core[0] == 0
    curve = own[2:3, :] + got[2:3, :]
    factor = jnp.sqrt(kl_clip / (learn_rate * learn_rate * curve))
    side0 = jnp.where(first, own[...], got[...])
    side1 = jnp.where(first, got[...], own[...])
    updates[0] = (side0[0:2] * factor).astype(bf16)
    updates[1] = (side1[0:2] * factor).astype(bf16)
    gradients[:, 0, :] = side0[4:6]
    gradients[:, 1, :] = side1[4:6]
    batch = (side0[8:10] + side1[8:10], side0[6:8], side1[6:8])
    for f in range(3):
        new_factors[f] = decay * old[f] + scale * batch[f]


def exchange(value, groups):
    return lax.all_to_all(value, "dp", 0, 0, axis_index_groups=groups, tiled=True)


def body(activations, grad_key, grad_value, time_start, time_width, bases, old_factors):
    index = lax.axis_index("dp").astype(jnp.int32)
    core = index & (NC - 1)
    first = core == 0
    here = (core[None], (index >> 1)[None])
    tokens_here = activations.shape[0]
    share = (1.0 - decay) / (tokens_here * lax.axis_size("dp"))

    def in_hbm(value):
        return pltpu.with_memory_space_constraint(value, pltpu.HBM)

    masks = (in_hbm(time_start.T), in_hbm(time_width.T))
    frames, keys, vals = in_hbm(activations), in_hbm(grad_key), in_hbm(grad_value)
    mask_buf = pltpu.SMEM(time_start.shape[::-1], jnp.int32)
    buf = pltpu.VMEM((tokens_here, D), bf16)
    sems = pltpu.SemaphoreType.DMA((CHUNKS,))
    pair = pltpu.SemaphoreType.DMA((2,))
    side_rows = NXY // SIDES
    partial = shape((side_rows, PAIR, WROWS, LANES), bf16)
    spare_shape = shape((side_rows, PAIR, ROWS + ROWS // 2, LANES), bf16)
    mine_shape = shape((side_rows, PAIR, F0 + ROWS // 2, LANES), bf16)
    work = 6 * D * D * tokens_here
    with jax.named_scope("grams_theirs"):
        *sent, spare0, spare1, kept, keep, ahead = call(
            theirs_kernel,
            (
                partial,
                partial,
                spare_shape,
                spare_shape,
                shape((tokens_here, D), bf16),
                shape((tokens_here, LANES), bf16),
                shape((tokens_here, D), bf16),
            ),
            [SMEM] + [HBM] * 5,
            [buf, buf, mask_buf, mask_buf, sems, sems, pair, sems],
            flops=work,
            moved=4 * MB,
        )(core[None], *masks, frames, keys, vals)
    received = [lax.ppermute(part, "dp", SWAP) for part in sent]
    with jax.named_scope("grams_mine"):
        mine = call(
            mine_kernel,
            (mine_shape, mine_shape),
            [VMEM] * 3,
            flops=work,
            moved=4 * MB,
        )(keep, kept, ahead)
    with jax.named_scope("chip_sum0"):
        half = call(add_first_kernel, partial, [VMEM] * 3, moved=MB)(mine[0], spare0, received[0])
    with jax.named_scope("chip_sum1"):
        chip = call(
            add_second_kernel,
            pltpu.HBM((NXY, PAIR, WROWS, LANES), bf16),
            [VMEM] * 4,
            [pltpu.VMEM(partial.shape, bf16), pltpu.SemaphoreType.DMA((PIECES + 1,))],
            moved=MB,
        )(half, mine[1], spare1, received[1])
        chip = chip.reshape(WIDE, WROWS, LANES)
    with jax.named_scope("wide_sum"):
        parts = exchange(chip, WIDE_GROUPS)

    lam_shape, square = shape((2, D), f32), shape((D, D), bf16)
    with jax.named_scope("lam"):
        keep_lam, send_lam, basis_in_t, mirror, basis_out, rows_in = call(
            functools.partial(lam_kernel, share),
            (lam_shape, lam_shape, square, square, square, shape((16, D), bf16)),
            [SMEM, SMEM, HBM, VMEM, HBM, HBM, HBM, VMEM],
            [buf] * 3 + [sems] * 3,
            flops=work,
            moved=4 * MB,
        )(*here, in_hbm(chip), keep, frames, keys, vals, bases)
    old_lam = []
    my_rows = lax.dynamic_slice_in_dim(bases, 2 * index, 2, 1).astype(f32)
    for f in range(3):
        old_image = jnp.dot(old_factors[:, f, :], bases[f].astype(f32), precision=lax.Precision.HIGHEST)
        old_lam.append(decay * jnp.sum(my_rows[f] * old_image, axis=0))
    keep_lam = keep_lam + jnp.stack([old_lam[0], jnp.where(first, old_lam[1], old_lam[2])])
    send_lam = send_lam + jnp.stack([old_lam[0], jnp.where(first, old_lam[2], old_lam[1])])
    sent_lam = lax.ppermute(send_lam, "dp", SWAP)

    with jax.named_scope("pack"):
        packed = call(pack_kernel, shape((DEEP, DEEP_ROWS, LANES), bf16), [VMEM] * 3)(parts, keep_lam, sent_lam)
    with jax.named_scope("deep_sum"):
        got = exchange(packed, DEEP_GROUPS)
    lines = shape((16, D), f32)
    with jax.named_scope("rotate"):
        spread = call(rotate_kernel, shape((WIDE, GATHER_ROWS, LANES), bf16), [VMEM] * 2)(got, basis_out)
    with jax.named_scope("gather"):
        gathered = exchange(spread, WIDE_GROUPS)
    with jax.named_scope("solve"):
        own, their = call(solve_kernel, (lines, lines), [SMEM] * 2 + [VMEM] * 6, [pltpu.VMEM((D, D), bf16)])(
            *here, gathered, got, basis_in_t, basis_out, rows_in, mirror
        )
    theirs = lax.ppermute(their, "dp", SWAP)
    with jax.named_scope("finish"):
        new_factors, gradients, updates = call(
            functools.partial(finish_kernel, share),
            (shape((3, 2, D), f32), shape((2, 2, D), f32), shape((2, 2, D), bf16)),
            [SMEM] + [VMEM] * 3,
        )(core[None], own, theirs, jnp.transpose(old_factors, (1, 0, 2)))
    return (jnp.transpose(new_factors, (1, 0, 2)), gradients, updates)


def solution(mesh):
    in_specs = (
        P("dp", None),
        P("dp", None),
        P("dp", None),
        P("dp", None),
        P("dp", None),
        P(),
        P("dp", None, None),
    )
    out_specs = (P("dp", None, None), P("dp", None, None), P(None, "dp", None))
    return jax.shard_map(body, mesh=mesh, in_specs=in_specs, out_specs=out_specs, check_vma=False)
```

```python
import functools

import jax
import jax.numpy as jnp
from jax import lax
from jax.experimental import pallas as pl
from jax.experimental.pallas import tpu as pltpu
from jax.sharding import PartitionSpec as P

LEN = 128
NX, NY, NZ, NC = 4, 4, 8, 2
NXY = NX * NY
D = 512
HALF = D // 2
PAIR = 2
WIDE = NXY * PAIR
DEEP = NZ // PAIR
ROWS = D // WIDE
LANES = 128
FR = ROWS // DEEP
GT = D // LANES
BLK = D // NXY
FA, F0, FL = GT * ROWS, (GT + 2) * ROWS, (GT + 3) * ROWS
WROWS = FL + ROWS // 2
MB = 1 << 20

decay = 0.8
damping = 0.001
kl_clip = 0.001
learn_rate = 7e-05

f32, bf16 = jnp.float32, jnp.bfloat16


def device(xy, z, c):
    return (xy * NZ + z) * NC + c


SWAP = [(d, d ^ 1) for d in range(NXY * NZ * NC)]
WIDE_GROUPS = [
    [device(i, k * PAIR + l, c) for i in range(NXY) for l in range(PAIR)]
    for k in range(DEEP)
    for c in range(NC)
]
DEEP_GROUPS = [
    [device(i, k * PAIR + l, c) for k in range(DEEP)] for i in range(NXY) for l in range(PAIR) for c in range(NC)
]
VMEM = pl.BlockSpec(memory_space=pltpu.VMEM)
SMEM = pl.BlockSpec(memory_space=pltpu.SMEM)
HBM = pl.BlockSpec(memory_space=pltpu.HBM)
CHUNKS = 2


def call(kernel, outs, in_specs, scratch=(), limit=16, flops=0, moved=0):
    return pl.pallas_call(
        kernel,
        out_shape=outs,
        in_specs=in_specs,
        out_specs=jax.tree.map(lambda out: HBM if isinstance(out, pl.MemoryRef) else VMEM, outs),
        scratch_shapes=list(scratch),
        compiler_params=pltpu.CompilerParams(vmem_limit_bytes=limit * MB),
        cost_estimate=pl.CostEstimate(flops=flops, bytes_accessed=moved, transcendentals=0),
    )


def shape(dims, dtype):
    return jax.ShapeDtypeStruct(dims, dtype)


def dot(a, b):
    return jnp.dot(a, b, preferred_element_type=f32)


def arrange(value):
    size = value.shape[1]
    pairs = value.reshape(value.shape[0] // 16, 2, 8, size)
    even, odd = pairs[:, 0], pairs[:, 1]
    upper = lax.broadcasted_iota(jnp.int32, even.shape, 1) < FR
    low = jnp.where(upper, even, pltpu.roll(odd, FR, 1))
    high = jnp.where(upper, pltpu.roll(even, FR, 1), odd)
    blocks = (value.shape[0] // (PAIR * ROWS), ROWS, size)
    return low.reshape(blocks), high.reshape(blocks)


def build_keep(start, width, keep):
    position = lax.broadcasted_iota(jnp.int32, (LEN, LANES), 0)
    for u in range(start.shape[1]):
        outside = None
        for m in range(start.shape[0]):
            first = start[m, u]
            here = (position < first) | (position >= first + width[m, u])
            outside = here if outside is None else outside & here
        keep[pl.ds(u * LEN, LEN), :] = jnp.where(outside, 1.0, 0.0).astype(bf16)


def apply_mask(source, target, keep, q):
    rows = pl.ds(q * (source.shape[0] // CHUNKS), source.shape[0] // CHUNKS)
    for j in range(GT):
        view = (rows, pl.ds(j * LANES, LANES))
        target[view] = source[view] * keep[rows, :]


def fetch(source, target, sems):
    rows = source.shape[0] // CHUNKS
    return [
        pltpu.make_async_copy(source.at[pl.ds(q * rows, rows)], target.at[pl.ds(q * rows, rows)], sems.at[q])
        for q in range(CHUNKS)
    ]


def fetch_picked(pick, xk, xv, target, sems):
    @pl.when(pick == 0)
    def _():
        for copy in fetch(xk, target, sems):
            copy.start()

    @pl.when(pick != 0)
    def _():
        for copy in fetch(xv, target, sems):
            copy.start()

    return fetch(xk, target, sems)


BLOCK = 256


def put(out, r, value, begin):
    for half, rows in enumerate(arrange(value)):
        for j in range(value.shape[1] // LANES):
            out[r][:, half, pl.ds(begin + j * ROWS, ROWS), :] = rows[:, :, j * LANES : (j + 1) * LANES].astype(bf16)


def put_folded(out, r, value, begin):
    for half, rows in enumerate(arrange(value)):
        upper, lower = rows[:, : ROWS // 2], pltpu.roll(rows[:, ROWS // 2 :], LANES // 2, 2)
        lane = lax.broadcasted_iota(jnp.int32, upper.shape, 2)
        out[r][:, half, pl.ds(begin, ROWS // 2), :] = jnp.where(lane < LANES // 2, upper, lower).astype(bf16)


def end_lanes(value):
    lane = lax.broadcasted_iota(jnp.int32, value.shape, 1)
    return jnp.where(lane < BLK, value, 0.0)


def circulate(value, r):
    rows = []
    for b in range(BLOCK // BLK):
        shift = (D - BLK * (r * (BLOCK // BLK) + b)) % D
        piece = value[b * BLK : (b + 1) * BLK]
        rows.append(pltpu.roll(piece, shift, 1) if shift else piece)
    return [jnp.concatenate([p[:, t * LANES : (t + 1) * LANES] for p in rows], axis=0) for t in range(3)]


def zero_grams(pick, x0, out, spare):
    lefts, rests = [], []
    for r in range(D // BLOCK):
        lefts.append(x0[:, pl.ds(r * BLOCK, BLOCK)].T)
        tiles = circulate(dot(lefts[r], x0[...]), r)
        put(out, r, jnp.where(pick == 0, tiles[0], tiles[1]), F0)
        put(spare, r, jnp.where(pick == 0, tiles[1], tiles[0]), 0)
        last = pltpu.roll(end_lanes(tiles[2]), BLK, 1)
        rests.append(jnp.where(pick == 0, 0.0, last))
        put_folded(spare, r, jnp.where(pick == 0, last, 0.0), ROWS)
    return lefts, rests


def picked_grams(lefts, x1, keep, rests, out, end):
    for r in range(D // BLOCK):
        put(out, r, dot(lefts[r], x1[...]), 0)
    wide = jnp.concatenate([keep[...]] * (BLOCK // LANES), axis=1)
    for r in range(D // BLOCK):
        left = (x1[:, pl.ds(r * BLOCK, BLOCK)] * wide).T
        tiles = circulate(dot(left, x1[...]), r)
        put(out, r, jnp.concatenate(tiles[:2], axis=1), FA)
        last = end_lanes(tiles[2])
        put_folded(out, r, last if rests is None else last + rests[r], end)


def theirs_kernel(
    core, start, width, x0, xk, xv, out0, out1, spare0, spare1, kept, keep, ahead, buf0, buf1, starts, widths, sem0, sem1, sem2, sem3
):
    pick = 1 - core[0]
    small = [pltpu.make_async_copy(v, w, sem2.at[i]) for i, (v, w) in enumerate(((start, starts), (width, widths)))]
    copies0 = fetch(x0, buf0, sem0)
    for copy in small + copies0:
        copy.start()
    for copy in small:
        copy.wait()
    build_keep(starts, widths, keep)
    for q in range(CHUNKS):
        copies0[q].wait()
        if q == 0:
            copies1 = fetch_picked(pick, xk, xv, buf1, sem1)
        apply_mask(buf0, kept, keep, q)
    out, spare = (out0, out1), (spare0, spare1)
    lefts, rests = zero_grams(pick, kept, out, spare)
    for copy in copies1:
        copy.wait()
    copies2 = fetch_picked(core[0], xk, xv, ahead, sem3)
    picked_grams(lefts, buf1, keep, rests, out, FL)
    for copy in copies2:
        copy.wait()


def mine_kernel(keep, x0, x1, out0, out1):
    lefts = [x0[:, pl.ds(r * BLOCK, BLOCK)].T for r in range(D // BLOCK)]
    picked_grams(lefts, x1, keep, None, (out0, out1), F0)


SIDES = D // BLOCK
PIECES = 2


def add_rows(mine, spare, received, out, blocks):
    main, zero, last = slice(0, F0), slice(F0, FL), slice(FL, WROWS)
    for i in blocks:
        for j in range(PAIR):
            out[i, j, main] = mine[i, j, main] + received[i, j, main]
            out[i, j, zero] = spare[i, j, :ROWS] + received[i, j, zero]
            ends = mine[i, j, F0:] + spare[i, j, ROWS:]
            out[i, j, last] = ends + received[i, j, last]


def add_first_kernel(mine, spare, received, out):
    add_rows(mine, spare, received, out, range(NXY // SIDES))


def add_second_kernel(first, mine, spare, received, out, buf, sems):
    count = NXY // SIDES
    size = count // PIECES
    copies = [pltpu.make_async_copy(first, out.at[pl.ds(0, count)], sems.at[PIECES])]
    copies[0].start()
    for q in range(PIECES):
        add_rows(mine, spare, received, buf, range(q * size, (q + 1) * size))
        target = out.at[pl.ds(count + q * size, size)]
        copies.append(pltpu.make_async_copy(buf.at[pl.ds(q * size, size)], target, sems.at[q]))
        copies[-1].start()
    for copy in copies:
        copy.wait()


def lam_kernel(
    share, core, chip, _, keep, x0, xk, xv, bases, keep_lam, send_lam, basis_in_t, mirror, basis_out, rows_in, b0, b1, b2, sem0, sem1, sem2
):
    c = core[0]
    bufs = (b0, b1, b2)
    copies = [fetch(x, buf, sem) for x, buf, sem in zip((x0, xk, xv), bufs, (sem0, sem1, sem2))]
    for group in copies:
        for copy in group:
            copy.start()
    low, high = arrange(bases[0].astype(f32))
    basis_in_t[...] = jnp.concatenate([low, high], axis=1).reshape(D, D).T.astype(bf16)
    lane = lax.broadcasted_iota(jnp.int32, (LANES, D), 0)
    column = lax.broadcasted_iota(jnp.int32, (LANES, D), 1)
    for half in range(PAIR):
        home = 8 * ((lane >> 2) & 3) + FR * half + (lane & 3) + 2 * D
        for kind in range(2):
            distance = (lane >> 4) + (4 * c if kind else 0)
            there = (home + BLK * ((chip[0] >> 3) - distance)) & (D - 1)
            one = jnp.where(column == there, 1.0, 0.0).astype(bf16)
            mirror[pl.ds((2 * half + kind) * LANES, LANES), :] = one
    basis_out[...] = bases[1 + c]
    row = lax.broadcasted_iota(jnp.int32, (16, D), 0)
    column = lax.broadcasted_iota(jnp.int32, (16, D), 1)
    wanted = (row < FR) & (column == FR * chip[0] + ((row + 2 * c) & (FR - 1)))
    rows_in[...] = dot(jnp.where(wanted, 1.0, 0.0).astype(bf16), bases[0]).astype(bf16)
    lam = []
    for f in range(3):
        total = jnp.zeros((8, D), f32)
        for q in range(CHUNKS):
            copies[f][q].wait()
            apply_mask(bufs[f], bufs[f], keep, q)
        for q in range(bufs[f].shape[0] // BLOCK):
            product = dot(bufs[f][pl.ds(q * BLOCK, BLOCK), :], bases[f])
            total = total + jnp.sum((product * product).reshape(BLOCK // 8, 8, D), axis=0)
        lam.append(jnp.sum(total, axis=0, keepdims=True) * share)
    keep_lam[0:1, :] = lam[0]
    send_lam[0:1, :] = lam[0]
    keep_lam[1:2, :] = jnp.where(c == 0, lam[1], lam[2])
    send_lam[1:2, :] = jnp.where(c == 0, lam[2], lam[1])


def split(value):
    high = value.astype(bf16)
    return high.astype(f32), value - high.astype(f32)


def lam_rows(lam):
    return jnp.concatenate(split(jnp.concatenate([lam[:, j * LANES : (j + 1) * LANES] for j in range(GT)], axis=0)), axis=0)


def add_lam(rows):
    return rows[: 2 * GT] + rows[2 * GT :]


def lam_row(total, index):
    return jnp.concatenate([total[2 * j + index : 2 * j + index + 1] for j in range(GT)], axis=1)


LAMR = 4 * GT
DIRECT = GT * ROWS
TURNED = DIRECT + 4 * FR
DEEP_LAM = TURNED + 16
DEEP_ROWS = DEEP_LAM + LAMR
GATHER_LAM = GT * ROWS
GATHER_TURNED = GATHER_LAM + 2 * GT
GATHER_ROWS = GATHER_TURNED + 8


def pack_kernel(parts, keep_lam, send_lam, out):
    total = parts[0].astype(f32)
    for i in range(1, WIDE):
        total = total + parts[i].astype(f32)
    lam = lam_rows(keep_lam[...] + send_lam[...]).astype(bf16)
    for j in range(GT):
        tile = total[j * ROWS : (j + 1) * ROWS].astype(bf16)
        for k in range(DEEP):
            out[k, pl.ds(j * ROWS, ROWS), :] = tile
    near, mid, zero = total[FA : FA + ROWS], total[FA + ROWS : F0], total[F0:FL]
    last = total[FL:]
    last = jnp.concatenate([last, pltpu.roll(last, LANES // 2, 1)], axis=0)
    empty = jnp.zeros((LANES - ROWS, LANES), f32)
    turned = [jnp.concatenate([v, empty], axis=0).T for v in (near, mid, zero)]
    for k in range(DEEP):
        rows = slice(k * FR, (k + 1) * FR)
        direct = jnp.concatenate([v[rows] for v in (near, mid, zero, last)], axis=0)
        out[k, pl.ds(DIRECT, 4 * FR), :] = direct.astype(bf16)

        def pieces(sources):
            result = None
            for n in range(4 * len(sources)):
                piece = sources[n // 4][(n % 4) * BLK + 8 * k : (n % 4) * BLK + 8 * k + 8]
                piece = pltpu.roll(piece, ROWS * n, 1) if n else piece
                result = piece if result is None else result + piece
            return result

        mirrored = jnp.concatenate([pieces(turned[:2]), pieces(turned[2:])], axis=0)
        out[k, pl.ds(TURNED, 16), :] = mirrored.astype(bf16)
        out[k, pl.ds(DEEP_LAM, LAMR), :] = lam


def deep_total(got):
    total = got[0].astype(f32)
    for i in range(1, DEEP):
        total = total + got[i].astype(f32)
    return total, jnp.concatenate([total[j * ROWS : (j + 1) * ROWS] for j in range(GT)], axis=1)


def rotate_kernel(got, basis, out):
    total, grad = deep_total(got)
    rot = dot(grad.astype(bf16), basis[...]).astype(bf16)
    lam = add_lam(total[DEEP_LAM:])
    picked, zero = total[TURNED : TURNED + 8], total[TURNED + 8 : TURNED + 16]
    for half in range(PAIR):
        rows = slice(half * FR, (half + 1) * FR)
        tail = jnp.concatenate([lam, picked[rows], zero[rows]], axis=0).astype(bf16)
        for i in range(half, WIDE, PAIR):
            out[i, pl.ds(GATHER_LAM, ROWS), :] = tail
    for j in range(GT):
        tile = rot[:, j * LANES : (j + 1) * LANES]
        for i in range(WIDE):
            out[i, pl.ds(j * ROWS, ROWS), :] = tile


def direct_rows(k, c, block, got):
    total, grad = deep_total(got)
    rows = grad[0:FR]
    for other in range(1, DEEP):
        rows = jnp.where(k == other, grad[other * FR : (other + 1) * FR], rows)
    near, mid, zero, last = [total[DIRECT + t * FR : DIRECT + (t + 1) * FR] for t in range(4)]
    lane = lax.broadcasted_iota(jnp.int32, last.shape, 1)
    none = jnp.zeros_like(last)
    end = jnp.where(lane < BLK, last, none)
    end0 = jnp.where(lane < BLK, pltpu.roll(last, LANES - BLK, 1), none)
    picked = jnp.concatenate([near, mid, end, none], axis=1)
    zero = jnp.where(
        c == 0,
        jnp.concatenate([zero, none, none, none], axis=1),
        jnp.concatenate([none, zero, end0, none], axis=1),
    )
    return rows, pltpu.roll(jnp.concatenate([picked, zero], axis=0), BLK * block, 1)


def mirrored_rows(c, block, tails, mirror):
    row = lax.broadcasted_iota(jnp.int32, (8, LANES), 0)
    group = (lax.broadcasted_iota(jnp.int32, (8, LANES), 1) >> 4) + jnp.where(row >= FR, 4 * c, 0)
    parts = []
    for half in range(PAIR):
        own = jnp.zeros((8, LANES), f32)
        for i in range(NXY):
            distance = (block - i) & (NXY - 1)
            wanted = jnp.where((distance >= 1) & (distance < 8), distance, -1)
            own = jnp.where(group == wanted, tails[PAIR * i + half][8:], own)
        parts += [jnp.where(row < FR, own, 0.0), jnp.where(row < FR, 0.0, own)]
    return dot(jnp.concatenate(parts, axis=1).astype(bf16), mirror[...])


def solve_kernel(core, chip, got, packed, basis_in_t, basis_out, rows_in, mirror, own, their, scaled):
    tails = [got[i, pl.ds(GATHER_LAM, ROWS), :].astype(f32) for i in range(WIDE)]
    lam = tails[0][:8]
    for tail in tails[1:]:
        lam = lam + tail[:8]
    column = jnp.broadcast_to(lam_row(lam, 0), (8, D)).T[:, 0:1]
    column = jnp.broadcast_to(column, (D, LANES))
    curve = jnp.zeros((8, LANES), f32)
    for pair in range(0, GT, 2):
        tiles = (pair, pair + 1)
        rot = jnp.concatenate([got[:, pl.ds(j * ROWS, ROWS), :].reshape(D, LANES) for j in tiles], axis=1)
        both = dot(basis_in_t[...], rot)
        for j in tiles:
            rotated = both[:, (j - pair) * LANES : (j - pair + 1) * LANES]
            low = (rotated / (column * lam[2 * j + 1 : 2 * j + 2] + damping)).astype(bf16)
            scaled[:, pl.ds(j * LANES, LANES)] = low
            curve = curve + jnp.sum((low.astype(f32) * rotated).reshape(D // 8, 8, LANES), axis=0)
    curve = jnp.sum(jnp.sum(curve, axis=1, keepdims=True), axis=0, keepdims=True)
    back = dot(rows_in[...], scaled[...]).astype(bf16)
    prec = lax.dot_general(back, basis_out[...], (((1,), (1,)), ((), ())), preferred_element_type=f32)
    prec = prec.astype(bf16).astype(f32)
    curve = jnp.broadcast_to(curve, (2, D))
    rows, factors = direct_rows((chip[0] & (NZ - 1)) >> 1, core[0], chip[0] >> 3, packed)
    factors = factors + mirrored_rows(core[0], chip[0] >> 3, tails, mirror)
    low = jnp.concatenate([rows[0:2], factors[0:2], factors[4:6]], axis=0)
    high = jnp.concatenate([rows[2:4], factors[2:4], factors[6:8]], axis=0)
    first = core[0] == 0
    pad = jnp.zeros((6, D), f32)
    own[...] = jnp.concatenate([prec[0:2], curve, jnp.where(first, low, high), pad], axis=0)
    their[...] = jnp.concatenate([prec[2:4], curve, jnp.where(first, high, low), pad], axis=0)


def finish_kernel(scale, core, own, got, old, new_factors, gradients, updates):
    first = core[0] == 0
    curve = own[2:3, :] + got[2:3, :]
    factor = jnp.sqrt(kl_clip / (learn_rate * learn_rate * curve))
    side0 = jnp.where(first, own[...], got[...])
    side1 = jnp.where(first, got[...], own[...])
    updates[0] = (side0[0:2] * factor).astype(bf16)
    updates[1] = (side1[0:2] * factor).astype(bf16)
    gradients[:, 0, :] = side0[4:6]
    gradients[:, 1, :] = side1[4:6]
    batch = (side0[8:10] + side1[8:10], side0[6:8], side1[6:8])
    for f in range(3):
        new_factors[f] = decay * old[f] + scale * batch[f]


def exchange(value, groups):
    return lax.all_to_all(value, "dp", 0, 0, axis_index_groups=groups, tiled=True)


def body(activations, grad_key, grad_value, time_start, time_width, bases, old_factors):
    index = lax.axis_index("dp").astype(jnp.int32)
    core = index & (NC - 1)
    first = core == 0
    here = (core[None], (index >> 1)[None])
    tokens_here = activations.shape[0]
    share = (1.0 - decay) / (tokens_here * lax.axis_size("dp"))

    def in_hbm(value):
        return pltpu.with_memory_space_constraint(value, pltpu.HBM)

    masks = (in_hbm(time_start.T), in_hbm(time_width.T))
    frames, keys, vals = in_hbm(activations), in_hbm(grad_key), in_hbm(grad_value)
    mask_buf = pltpu.SMEM(time_start.shape[::-1], jnp.int32)
    buf = pltpu.VMEM((tokens_here, D), bf16)
    sems = pltpu.SemaphoreType.DMA((CHUNKS,))
    pair = pltpu.SemaphoreType.DMA((2,))
    side_rows = NXY // SIDES
    partial = shape((side_rows, PAIR, WROWS, LANES), bf16)
    spare_shape = shape((side_rows, PAIR, ROWS + ROWS // 2, LANES), bf16)
    mine_shape = shape((side_rows, PAIR, F0 + ROWS // 2, LANES), bf16)
    work = 6 * D * D * tokens_here
    with jax.named_scope("grams_theirs"):
        *sent, spare0, spare1, kept, keep, ahead = call(
            theirs_kernel,
            (
                partial,
                partial,
                spare_shape,
                spare_shape,
                shape((tokens_here, D), bf16),
                shape((tokens_here, LANES), bf16),
                shape((tokens_here, D), bf16),
            ),
            [SMEM] + [HBM] * 5,
            [buf, buf, mask_buf, mask_buf, sems, sems, pair, sems],
            flops=work,
            moved=4 * MB,
        )(core[None], *masks, frames, keys, vals)
    received = [lax.ppermute(part, "dp", SWAP) for part in sent]
    with jax.named_scope("grams_mine"):
        mine = call(
            mine_kernel,
            (mine_shape, mine_shape),
            [VMEM] * 3,
            flops=work,
            moved=4 * MB,
        )(keep, kept, ahead)
    with jax.named_scope("chip_sum0"):
        half = call(add_first_kernel, partial, [VMEM] * 3, moved=MB)(mine[0], spare0, received[0])
    with jax.named_scope("chip_sum1"):
        chip = call(
            add_second_kernel,
            pltpu.HBM((NXY, PAIR, WROWS, LANES), bf16),
            [VMEM] * 4,
            [pltpu.VMEM(partial.shape, bf16), pltpu.SemaphoreType.DMA((PIECES + 1,))],
            moved=MB,
        )(half, mine[1], spare1, received[1])
        chip = chip.reshape(WIDE, WROWS, LANES)
    with jax.named_scope("wide_sum"):
        parts = exchange(chip, WIDE_GROUPS)

    lam_shape, square = shape((2, D), f32), shape((D, D), bf16)
    with jax.named_scope("lam"):
        keep_lam, send_lam, basis_in_t, mirror, basis_out, rows_in = call(
            functools.partial(lam_kernel, share),
            (lam_shape, lam_shape, square, square, square, shape((16, D), bf16)),
            [SMEM, SMEM, HBM, VMEM, HBM, HBM, HBM, VMEM],
            [buf] * 3 + [sems] * 3,
            flops=work,
            moved=4 * MB,
        )(*here, in_hbm(chip), keep, frames, keys, vals, bases)
    old_lam = []
    my_rows = lax.dynamic_slice_in_dim(bases, 2 * index, 2, 1).astype(f32)
    for f in range(3):
        old_image = jnp.dot(old_factors[:, f, :], bases[f].astype(f32), precision=lax.Precision.HIGHEST)
        old_lam.append(decay * jnp.sum(my_rows[f] * old_image, axis=0))
    keep_lam = keep_lam + jnp.stack([old_lam[0], jnp.where(first, old_lam[1], old_lam[2])])
    send_lam = send_lam + jnp.stack([old_lam[0], jnp.where(first, old_lam[2], old_lam[1])])
    sent_lam = lax.ppermute(send_lam, "dp", SWAP)

    with jax.named_scope("pack"):
        packed = call(pack_kernel, shape((DEEP, DEEP_ROWS, LANES), bf16), [VMEM] * 3)(parts, keep_lam, sent_lam)
    with jax.named_scope("deep_sum"):
        got = exchange(packed, DEEP_GROUPS)
    lines = shape((16, D), f32)
    with jax.named_scope("rotate"):
        spread = call(rotate_kernel, shape((WIDE, GATHER_ROWS, LANES), bf16), [VMEM] * 2)(got, basis_out)
    with jax.named_scope("gather"):
        gathered = exchange(spread, WIDE_GROUPS)
    with jax.named_scope("solve"):
        own, their = call(solve_kernel, (lines, lines), [SMEM] * 2 + [VMEM] * 6, [pltpu.VMEM((D, D), bf16)])(
            *here, gathered, got, basis_in_t, basis_out, rows_in, mirror
        )
    theirs = lax.ppermute(their, "dp", SWAP)
    with jax.named_scope("finish"):
        new_factors, gradients, updates = call(
            functools.partial(finish_kernel, share),
            (shape((3, 2, D), f32), shape((2, 2, D), f32), shape((2, 2, D), bf16)),
            [SMEM] + [VMEM] * 3,
        )(core[None], own, theirs, jnp.transpose(old_factors, (1, 0, 2)))
    return (jnp.transpose(new_factors, (1, 0, 2)), gradients, updates)


def solution(mesh):
    in_specs = (
        P("dp", None),
        P("dp", None),
        P("dp", None),
        P("dp", None),
        P("dp", None),
        P(),
        P("dp", None, None),
    )
    out_specs = (P("dp", None, None), P("dp", None, None), P(None, "dp", None))
    return jax.shard_map(body, mesh=mesh, in_specs=in_specs, out_specs=out_specs, check_vma=False)
```

```python
import functools

import jax
import jax.numpy as jnp
from jax import lax
from jax.experimental import pallas as pl
from jax.experimental.pallas import tpu as pltpu
from jax.sharding import PartitionSpec as P

LEN = 128
NX, NY, NZ, NC = 4, 4, 8, 2
NXY = NX * NY
D = 512
HALF = D // 2
PAIR = 2
WIDE = NXY * PAIR
DEEP = NZ // PAIR
ROWS = D // WIDE
LANES = 128
FR = ROWS // DEEP
GT = D // LANES
BLK = D // NXY
FA, F0, FL = GT * ROWS, (GT + 2) * ROWS, (GT + 3) * ROWS
WROWS = FL + ROWS // 2
MB = 1 << 20

decay = 0.8
damping = 0.001
kl_clip = 0.001
learn_rate = 7e-05

f32, bf16 = jnp.float32, jnp.bfloat16


def device(xy, z, c):
    return (xy * NZ + z) * NC + c


SWAP = [(d, d ^ 1) for d in range(NXY * NZ * NC)]
WIDE_GROUPS = [
    [device(i, k * PAIR + l, c) for i in range(NXY) for l in range(PAIR)]
    for k in range(DEEP)
    for c in range(NC)
]
DEEP_GROUPS = [
    [device(i, k * PAIR + l, c) for k in range(DEEP)] for i in range(NXY) for l in range(PAIR) for c in range(NC)
]
VMEM = pl.BlockSpec(memory_space=pltpu.VMEM)
SMEM = pl.BlockSpec(memory_space=pltpu.SMEM)
HBM = pl.BlockSpec(memory_space=pltpu.HBM)
CHUNKS = 2


def call(kernel, outs, in_specs, scratch=(), limit=16, flops=0, moved=0):
    return pl.pallas_call(
        kernel,
        out_shape=outs,
        in_specs=in_specs,
        out_specs=jax.tree.map(lambda out: HBM if isinstance(out, pl.MemoryRef) else VMEM, outs),
        scratch_shapes=list(scratch),
        compiler_params=pltpu.CompilerParams(vmem_limit_bytes=limit * MB),
        cost_estimate=pl.CostEstimate(flops=flops, bytes_accessed=moved, transcendentals=0),
    )


def shape(dims, dtype):
    return jax.ShapeDtypeStruct(dims, dtype)


def dot(a, b):
    return jnp.dot(a, b, preferred_element_type=f32)


def arrange(value):
    size = value.shape[1]
    pairs = value.reshape(value.shape[0] // 16, 2, 8, size)
    even, odd = pairs[:, 0], pairs[:, 1]
    upper = lax.broadcasted_iota(jnp.int32, even.shape, 1) < FR
    low = jnp.where(upper, even, pltpu.roll(odd, FR, 1))
    high = jnp.where(upper, pltpu.roll(even, FR, 1), odd)
    blocks = (value.shape[0] // (PAIR * ROWS), ROWS, size)
    return low.reshape(blocks), high.reshape(blocks)


def build_keep(start, width, keep):
    position = lax.broadcasted_iota(jnp.int32, (LEN, LANES), 0)
    for u in range(start.shape[1]):
        outside = None
        for m in range(start.shape[0]):
            first = start[m, u]
            here = (position < first) | (position >= first + width[m, u])
            outside = here if outside is None else outside & here
        keep[pl.ds(u * LEN, LEN), :] = jnp.where(outside, 1.0, 0.0).astype(bf16)


def apply_mask(source, target, keep, q):
    rows = pl.ds(q * (source.shape[0] // CHUNKS), source.shape[0] // CHUNKS)
    for j in range(GT):
        view = (rows, pl.ds(j * LANES, LANES))
        target[view] = source[view] * keep[rows, :]


def fetch(source, target, sems):
    rows = source.shape[0] // CHUNKS
    return [
        pltpu.make_async_copy(source.at[pl.ds(q * rows, rows)], target.at[pl.ds(q * rows, rows)], sems.at[q])
        for q in range(CHUNKS)
    ]


def fetch_picked(pick, xk, xv, target, sems):
    @pl.when(pick == 0)
    def _():
        for copy in fetch(xk, target, sems):
            copy.start()

    @pl.when(pick != 0)
    def _():
        for copy in fetch(xv, target, sems):
            copy.start()

    return fetch(xk, target, sems)


BLOCK = 256


def put(out, r, value, begin):
    for half, rows in enumerate(arrange(value)):
        for j in range(value.shape[1] // LANES):
            out[r][:, half, pl.ds(begin + j * ROWS, ROWS), :] = rows[:, :, j * LANES : (j + 1) * LANES].astype(bf16)


def put_folded(out, r, value, begin):
    for half, rows in enumerate(arrange(value)):
        upper, lower = rows[:, : ROWS // 2], pltpu.roll(rows[:, ROWS // 2 :], LANES // 2, 2)
        lane = lax.broadcasted_iota(jnp.int32, upper.shape, 2)
        out[r][:, half, pl.ds(begin, ROWS // 2), :] = jnp.where(lane < LANES // 2, upper, lower).astype(bf16)


def end_lanes(value):
    lane = lax.broadcasted_iota(jnp.int32, value.shape, 1)
    return jnp.where(lane < BLK, value, 0.0)


def circulate(value, r):
    rows = []
    for b in range(BLOCK // BLK):
        shift = (D - BLK * (r * (BLOCK // BLK) + b)) % D
        piece = value[b * BLK : (b + 1) * BLK]
        rows.append(pltpu.roll(piece, shift, 1) if shift else piece)
    return [jnp.concatenate([p[:, t * LANES : (t + 1) * LANES] for p in rows], axis=0) for t in range(3)]


def zero_grams(pick, x0, out, spare):
    lefts, rests = [], []
    for r in range(D // BLOCK):
        lefts.append(x0[:, pl.ds(r * BLOCK, BLOCK)].T)
        tiles = circulate(dot(lefts[r], x0[...]), r)
        put(out, r, jnp.where(pick == 0, tiles[0], tiles[1]), F0)
        put(spare, r, jnp.where(pick == 0, tiles[1], tiles[0]), 0)
        last = pltpu.roll(end_lanes(tiles[2]), BLK, 1)
        rests.append(jnp.where(pick == 0, 0.0, last))
        put_folded(spare, r, jnp.where(pick == 0, last, 0.0), ROWS)
    return lefts, rests


def picked_grams(lefts, x1, keep, rests, out, end):
    for r in range(D // BLOCK):
        put(out, r, dot(lefts[r], x1[...]), 0)
    wide = jnp.concatenate([keep[...]] * (BLOCK // LANES), axis=1)
    for r in range(D // BLOCK):
        left = (x1[:, pl.ds(r * BLOCK, BLOCK)] * wide).T
        tiles = circulate(dot(left, x1[...]), r)
        put(out, r, jnp.concatenate(tiles[:2], axis=1), FA)
        last = end_lanes(tiles[2])
        put_folded(out, r, last if rests is None else last + rests[r], end)


def theirs_kernel(
    core, start, width, x0, xk, xv, out0, out1, spare0, spare1, kept, keep, ahead, buf0, buf1, starts, widths, sem0, sem1, sem2, sem3
):
    pick = 1 - core[0]
    small = [pltpu.make_async_copy(v, w, sem2.at[i]) for i, (v, w) in enumerate(((start, starts), (width, widths)))]
    copies0 = fetch(x0, buf0, sem0)
    for copy in small + copies0:
        copy.start()
    for copy in small:
        copy.wait()
    build_keep(starts, widths, keep)
    for q in range(CHUNKS):
        copies0[q].wait()
        if q == 0:
            copies1 = fetch_picked(pick, xk, xv, buf1, sem1)
        apply_mask(buf0, kept, keep, q)
    out, spare = (out0, out1), (spare0, spare1)
    lefts, rests = zero_grams(pick, kept, out, spare)
    for copy in copies1:
        copy.wait()
    copies2 = fetch_picked(core[0], xk, xv, ahead, sem3)
    picked_grams(lefts, buf1, keep, rests, out, FL)
    for copy in copies2:
        copy.wait()


def mine_kernel(keep, x0, x1, out0, out1):
    lefts = [x0[:, pl.ds(r * BLOCK, BLOCK)].T for r in range(D // BLOCK)]
    picked_grams(lefts, x1, keep, None, (out0, out1), F0)


SIDES = D // BLOCK
PIECES = 4


def add_rows(mine, spare, received, out, blocks):
    main, zero, last = slice(0, F0), slice(F0, FL), slice(FL, WROWS)
    for i in blocks:
        for j in range(PAIR):
            out[i, j, main] = mine[i, j, main] + received[i, j, main]
            out[i, j, zero] = spare[i, j, :ROWS] + received[i, j, zero]
            ends = mine[i, j, F0:] + spare[i, j, ROWS:]
            out[i, j, last] = ends + received[i, j, last]


def add_first_kernel(mine, spare, received, out):
    add_rows(mine, spare, received, out, range(NXY // SIDES))


def add_second_kernel(first, mine, spare, received, out, buf, sems):
    count = NXY // SIDES
    size = count // PIECES
    copies = []
    for q in range(2):
        part = pl.ds(q * (count // 2), count // 2)
        copies.append(pltpu.make_async_copy(first.at[part], out.at[part], sems.at[PIECES + q]))
        copies[-1].start()
    for q in range(PIECES):
        add_rows(mine, spare, received, buf, range(q * size, (q + 1) * size))
        target = out.at[pl.ds(count + q * size, size)]
        copies.append(pltpu.make_async_copy(buf.at[pl.ds(q * size, size)], target, sems.at[q]))
        copies[-1].start()
    for copy in copies:
        copy.wait()


def lam_kernel(
    share, core, chip, _, keep, x0, xk, xv, bases, keep_lam, send_lam, basis_in_t, mirror, basis_out, rows_in, b0, b1, b2, sem0, sem1, sem2
):
    c = core[0]
    bufs = (b0, b1, b2)
    copies = [fetch(x, buf, sem) for x, buf, sem in zip((x0, xk, xv), bufs, (sem0, sem1, sem2))]
    for group in copies:
        for copy in group:
            copy.start()
    low, high = arrange(bases[0].astype(f32))
    basis_in_t[...] = jnp.concatenate([low, high], axis=1).reshape(D, D).T.astype(bf16)
    lane = lax.broadcasted_iota(jnp.int32, (LANES, D), 0)
    column = lax.broadcasted_iota(jnp.int32, (LANES, D), 1)
    for half in range(PAIR):
        home = 8 * ((lane >> 2) & 3) + FR * half + (lane & 3) + 2 * D
        for kind in range(2):
            distance = (lane >> 4) + (4 * c if kind else 0)
            there = (home + BLK * ((chip[0] >> 3) - distance)) & (D - 1)
            one = jnp.where(column == there, 1.0, 0.0).astype(bf16)
            mirror[pl.ds((2 * half + kind) * LANES, LANES), :] = one
    basis_out[...] = bases[1 + c]
    row = lax.broadcasted_iota(jnp.int32, (16, D), 0)
    column = lax.broadcasted_iota(jnp.int32, (16, D), 1)
    wanted = (row < FR) & (column == FR * chip[0] + ((row + 2 * c) & (FR - 1)))
    rows_in[...] = dot(jnp.where(wanted, 1.0, 0.0).astype(bf16), bases[0]).astype(bf16)
    lam = []
    for f in range(3):
        total = jnp.zeros((8, D), f32)
        for q in range(CHUNKS):
            copies[f][q].wait()
            apply_mask(bufs[f], bufs[f], keep, q)
        for q in range(bufs[f].shape[0] // BLOCK):
            product = dot(bufs[f][pl.ds(q * BLOCK, BLOCK), :], bases[f])
            total = total + jnp.sum((product * product).reshape(BLOCK // 8, 8, D), axis=0)
        lam.append(jnp.sum(total, axis=0, keepdims=True) * share)
    keep_lam[0:1, :] = lam[0]
    send_lam[0:1, :] = lam[0]
    keep_lam[1:2, :] = jnp.where(c == 0, lam[1], lam[2])
    send_lam[1:2, :] = jnp.where(c == 0, lam[2], lam[1])


def split(value):
    high = value.astype(bf16)
    return high.astype(f32), value - high.astype(f32)


def lam_rows(lam):
    return jnp.concatenate(split(jnp.concatenate([lam[:, j * LANES : (j + 1) * LANES] for j in range(GT)], axis=0)), axis=0)


def add_lam(rows):
    return rows[: 2 * GT] + rows[2 * GT :]


def lam_row(total, index):
    return jnp.concatenate([total[2 * j + index : 2 * j + index + 1] for j in range(GT)], axis=1)


LAMR = 4 * GT
DIRECT = GT * ROWS
TURNED = DIRECT + 4 * FR
DEEP_LAM = TURNED + 16
DEEP_ROWS = DEEP_LAM + LAMR
GATHER_LAM = GT * ROWS
GATHER_TURNED = GATHER_LAM + 2 * GT
GATHER_ROWS = GATHER_TURNED + 8


def pack_kernel(parts, keep_lam, send_lam, out):
    total = parts[0].astype(f32)
    for i in range(1, WIDE):
        total = total + parts[i].astype(f32)
    lam = lam_rows(keep_lam[...] + send_lam[...]).astype(bf16)
    for j in range(GT):
        tile = total[j * ROWS : (j + 1) * ROWS].astype(bf16)
        for k in range(DEEP):
            out[k, pl.ds(j * ROWS, ROWS), :] = tile
    near, mid, zero = total[FA : FA + ROWS], total[FA + ROWS : F0], total[F0:FL]
    last = total[FL:]
    last = jnp.concatenate([last, pltpu.roll(last, LANES // 2, 1)], axis=0)
    empty = jnp.zeros((LANES - ROWS, LANES), f32)
    turned = [jnp.concatenate([v, empty], axis=0).T for v in (near, mid, zero)]
    for k in range(DEEP):
        rows = slice(k * FR, (k + 1) * FR)
        direct = jnp.concatenate([v[rows] for v in (near, mid, zero, last)], axis=0)
        out[k, pl.ds(DIRECT, 4 * FR), :] = direct.astype(bf16)

        def pieces(sources):
            result = None
            for n in range(4 * len(sources)):
                piece = sources[n // 4][(n % 4) * BLK + 8 * k : (n % 4) * BLK + 8 * k + 8]
                piece = pltpu.roll(piece, ROWS * n, 1) if n else piece
                result = piece if result is None else result + piece
            return result

        mirrored = jnp.concatenate([pieces(turned[:2]), pieces(turned[2:])], axis=0)
        out[k, pl.ds(TURNED, 16), :] = mirrored.astype(bf16)
        out[k, pl.ds(DEEP_LAM, LAMR), :] = lam


def deep_total(got):
    total = got[0].astype(f32)
    for i in range(1, DEEP):
        total = total + got[i].astype(f32)
    return total, jnp.concatenate([total[j * ROWS : (j + 1) * ROWS] for j in range(GT)], axis=1)


def rotate_kernel(got, basis, out):
    total, grad = deep_total(got)
    rot = dot(grad.astype(bf16), basis[...]).astype(bf16)
    lam = add_lam(total[DEEP_LAM:])
    picked, zero = total[TURNED : TURNED + 8], total[TURNED + 8 : TURNED + 16]
    for half in range(PAIR):
        rows = slice(half * FR, (half + 1) * FR)
        tail = jnp.concatenate([lam, picked[rows], zero[rows]], axis=0).astype(bf16)
        for i in range(half, WIDE, PAIR):
            out[i, pl.ds(GATHER_LAM, ROWS), :] = tail
    for j in range(GT):
        tile = rot[:, j * LANES : (j + 1) * LANES]
        for i in range(WIDE):
            out[i, pl.ds(j * ROWS, ROWS), :] = tile


def direct_rows(k, c, block, got):
    total, grad = deep_total(got)
    rows = grad[0:FR]
    for other in range(1, DEEP):
        rows = jnp.where(k == other, grad[other * FR : (other + 1) * FR], rows)
    near, mid, zero, last = [total[DIRECT + t * FR : DIRECT + (t + 1) * FR] for t in range(4)]
    lane = lax.broadcasted_iota(jnp.int32, last.shape, 1)
    none = jnp.zeros_like(last)
    end = jnp.where(lane < BLK, last, none)
    end0 = jnp.where(lane < BLK, pltpu.roll(last, LANES - BLK, 1), none)
    picked = jnp.concatenate([near, mid, end, none], axis=1)
    zero = jnp.where(
        c == 0,
        jnp.concatenate([zero, none, none, none], axis=1),
        jnp.concatenate([none, zero, end0, none], axis=1),
    )
    return rows, pltpu.roll(jnp.concatenate([picked, zero], axis=0), BLK * block, 1)


def mirrored_rows(c, block, tails, mirror):
    row = lax.broadcasted_iota(jnp.int32, (8, LANES), 0)
    group = (lax.broadcasted_iota(jnp.int32, (8, LANES), 1) >> 4) + jnp.where(row >= FR, 4 * c, 0)
    parts = []
    for half in range(PAIR):
        own = jnp.zeros((8, LANES), f32)
        for i in range(NXY):
            distance = (block - i) & (NXY - 1)
            wanted = jnp.where((distance >= 1) & (distance < 8), distance, -1)
            own = jnp.where(group == wanted, tails[PAIR * i + half][8:], own)
        parts += [jnp.where(row < FR, own, 0.0), jnp.where(row < FR, 0.0, own)]
    return dot(jnp.concatenate(parts, axis=1).astype(bf16), mirror[...])


def solve_kernel(core, chip, got, packed, basis_in_t, basis_out, rows_in, mirror, own, their, scaled):
    tails = [got[i, pl.ds(GATHER_LAM, ROWS), :].astype(f32) for i in range(WIDE)]
    lam = tails[0][:8]
    for tail in tails[1:]:
        lam = lam + tail[:8]
    column = jnp.broadcast_to(lam_row(lam, 0), (8, D)).T[:, 0:1]
    column = jnp.broadcast_to(column, (D, LANES))
    curve = jnp.zeros((8, LANES), f32)
    for pair in range(0, GT, 2):
        tiles = (pair, pair + 1)
        rot = jnp.concatenate([got[:, pl.ds(j * ROWS, ROWS), :].reshape(D, LANES) for j in tiles], axis=1)
        both = dot(basis_in_t[...], rot)
        for j in tiles:
            rotated = both[:, (j - pair) * LANES : (j - pair + 1) * LANES]
            low = (rotated / (column * lam[2 * j + 1 : 2 * j + 2] + damping)).astype(bf16)
            scaled[:, pl.ds(j * LANES, LANES)] = low
            curve = curve + jnp.sum((low.astype(f32) * rotated).reshape(D // 8, 8, LANES), axis=0)
    curve = jnp.sum(jnp.sum(curve, axis=1, keepdims=True), axis=0, keepdims=True)
    back = dot(rows_in[...], scaled[...]).astype(bf16)
    prec = lax.dot_general(back, basis_out[...], (((1,), (1,)), ((), ())), preferred_element_type=f32)
    prec = prec.astype(bf16).astype(f32)
    curve = jnp.broadcast_to(curve, (2, D))
    rows, factors = direct_rows((chip[0] & (NZ - 1)) >> 1, core[0], chip[0] >> 3, packed)
    factors = factors + mirrored_rows(core[0], chip[0] >> 3, tails, mirror)
    low = jnp.concatenate([rows[0:2], factors[0:2], factors[4:6]], axis=0)
    high = jnp.concatenate([rows[2:4], factors[2:4], factors[6:8]], axis=0)
    first = core[0] == 0
    pad = jnp.zeros((6, D), f32)
    own[...] = jnp.concatenate([prec[0:2], curve, jnp.where(first, low, high), pad], axis=0)
    their[...] = jnp.concatenate([prec[2:4], curve, jnp.where(first, high, low), pad], axis=0)


def finish_kernel(scale, core, own, got, old, new_factors, gradients, updates):
    first = core[0] == 0
    curve = own[2:3, :] + got[2:3, :]
    factor = jnp.sqrt(kl_clip / (learn_rate * learn_rate * curve))
    side0 = jnp.where(first, own[...], got[...])
    side1 = jnp.where(first, got[...], own[...])
    updates[0] = (side0[0:2] * factor).astype(bf16)
    updates[1] = (side1[0:2] * factor).astype(bf16)
    gradients[:, 0, :] = side0[4:6]
    gradients[:, 1, :] = side1[4:6]
    batch = (side0[8:10] + side1[8:10], side0[6:8], side1[6:8])
    for f in range(3):
        new_factors[f] = decay * old[f] + scale * batch[f]


def exchange(value, groups):
    return lax.all_to_all(value, "dp", 0, 0, axis_index_groups=groups, tiled=True)


def body(activations, grad_key, grad_value, time_start, time_width, bases, old_factors):
    index = lax.axis_index("dp").astype(jnp.int32)
    core = index & (NC - 1)
    first = core == 0
    here = (core[None], (index >> 1)[None])
    tokens_here = activations.shape[0]
    share = (1.0 - decay) / (tokens_here * lax.axis_size("dp"))

    def in_hbm(value):
        return pltpu.with_memory_space_constraint(value, pltpu.HBM)

    masks = (in_hbm(time_start.T), in_hbm(time_width.T))
    frames, keys, vals = in_hbm(activations), in_hbm(grad_key), in_hbm(grad_value)
    mask_buf = pltpu.SMEM(time_start.shape[::-1], jnp.int32)
    buf = pltpu.VMEM((tokens_here, D), bf16)
    sems = pltpu.SemaphoreType.DMA((CHUNKS,))
    pair = pltpu.SemaphoreType.DMA((2,))
    side_rows = NXY // SIDES
    partial = shape((side_rows, PAIR, WROWS, LANES), bf16)
    spare_shape = shape((side_rows, PAIR, ROWS + ROWS // 2, LANES), bf16)
    mine_shape = shape((side_rows, PAIR, F0 + ROWS // 2, LANES), bf16)
    work = 6 * D * D * tokens_here
    with jax.named_scope("grams_theirs"):
        *sent, spare0, spare1, kept, keep, ahead = call(
            theirs_kernel,
            (
                partial,
                partial,
                spare_shape,
                spare_shape,
                shape((tokens_here, D), bf16),
                shape((tokens_here, LANES), bf16),
                shape((tokens_here, D), bf16),
            ),
            [SMEM] + [HBM] * 5,
            [buf, buf, mask_buf, mask_buf, sems, sems, pair, sems],
            flops=work,
            moved=4 * MB,
        )(core[None], *masks, frames, keys, vals)
    received = [lax.ppermute(part, "dp", SWAP) for part in sent]
    with jax.named_scope("grams_mine"):
        mine = call(
            mine_kernel,
            (mine_shape, mine_shape),
            [VMEM] * 3,
            flops=work,
            moved=4 * MB,
        )(keep, kept, ahead)
    with jax.named_scope("chip_sum0"):
        half = call(add_first_kernel, partial, [VMEM] * 3, moved=MB)(mine[0], spare0, received[0])
    with jax.named_scope("chip_sum1"):
        chip = call(
            add_second_kernel,
            pltpu.HBM((NXY, PAIR, WROWS, LANES), bf16),
            [VMEM] * 4,
            [pltpu.VMEM(partial.shape, bf16), pltpu.SemaphoreType.DMA((PIECES + 2,))],
            moved=MB,
        )(half, mine[1], spare1, received[1])
        chip = chip.reshape(WIDE, WROWS, LANES)
    with jax.named_scope("wide_sum"):
        parts = exchange(chip, WIDE_GROUPS)

    lam_shape, square = shape((2, D), f32), shape((D, D), bf16)
    with jax.named_scope("lam"):
        keep_lam, send_lam, basis_in_t, mirror, basis_out, rows_in = call(
            functools.partial(lam_kernel, share),
            (lam_shape, lam_shape, square, square, square, shape((16, D), bf16)),
            [SMEM, SMEM, HBM, VMEM, HBM, HBM, HBM, VMEM],
            [buf] * 3 + [sems] * 3,
            flops=work,
            moved=4 * MB,
        )(*here, in_hbm(chip), keep, frames, keys, vals, bases)
    old_lam = []
    my_rows = lax.dynamic_slice_in_dim(bases, 2 * index, 2, 1).astype(f32)
    for f in range(3):
        old_image = jnp.dot(old_factors[:, f, :], bases[f].astype(f32), precision=lax.Precision.HIGHEST)
        old_lam.append(decay * jnp.sum(my_rows[f] * old_image, axis=0))
    keep_lam = keep_lam + jnp.stack([old_lam[0], jnp.where(first, old_lam[1], old_lam[2])])
    send_lam = send_lam + jnp.stack([old_lam[0], jnp.where(first, old_lam[2], old_lam[1])])
    sent_lam = lax.ppermute(send_lam, "dp", SWAP)

    with jax.named_scope("pack"):
        packed = call(pack_kernel, shape((DEEP, DEEP_ROWS, LANES), bf16), [VMEM] * 3)(parts, keep_lam, sent_lam)
    with jax.named_scope("deep_sum"):
        got = exchange(packed, DEEP_GROUPS)
    lines = shape((16, D), f32)
    with jax.named_scope("rotate"):
        spread = call(rotate_kernel, shape((WIDE, GATHER_ROWS, LANES), bf16), [VMEM] * 2)(got, basis_out)
    with jax.named_scope("gather"):
        gathered = exchange(spread, WIDE_GROUPS)
    with jax.named_scope("solve"):
        own, their = call(solve_kernel, (lines, lines), [SMEM] * 2 + [VMEM] * 6, [pltpu.VMEM((D, D), bf16)])(
            *here, gathered, got, basis_in_t, basis_out, rows_in, mirror
        )
    theirs = lax.ppermute(their, "dp", SWAP)
    with jax.named_scope("finish"):
        new_factors, gradients, updates = call(
            functools.partial(finish_kernel, share),
            (shape((3, 2, D), f32), shape((2, 2, D), f32), shape((2, 2, D), bf16)),
            [SMEM] + [VMEM] * 3,
        )(core[None], own, theirs, jnp.transpose(old_factors, (1, 0, 2)))
    return (jnp.transpose(new_factors, (1, 0, 2)), gradients, updates)


def solution(mesh):
    in_specs = (
        P("dp", None),
        P("dp", None),
        P("dp", None),
        P("dp", None),
        P("dp", None),
        P(),
        P("dp", None, None),
    )
    out_specs = (P("dp", None, None), P("dp", None, None), P(None, "dp", None))
    return jax.shard_map(body, mesh=mesh, in_specs=in_specs, out_specs=out_specs, check_vma=False)
```
